256 devices in a mesh: seq: 32 (over y, z), head: 8 (over x, core).
Axes of the slice: x: 4, y: 4, z: 8, core: 2. Of those that a mesh axis runs over, the one named last changes fastest.
Arguments:
- queries: bfloat16 [32768, 3072], P('seq', 'head'), may hold values from -120 to 120
- keys: bfloat16 [32768, 1024], P('seq', 'head'), may hold values from -5 to 5
- values: bfloat16 [32768, 1024], P('seq', 'head'), may hold values from -24 to 24
- out_weight: bfloat16 [3072, 3072], P('head'), may hold values from -0.15625 to 0.15625
- doc_lengths: int32 [64], replicated, may hold values from 1 to 4096, 32768 in all
Outputs:
- layer_out: bfloat16 [32768, 3072], P('seq', 'head')
The draws below stay inside these ranges and needn't reach their ends.
Inputs may be any that keep to these rules, and one draw needn't show every extreme that they name: `doc_lengths`: the documents fill the row end to end, summing to 32768 tokens; the longest has exactly 4096 tokens.
All inputs are finite; a program needn't handle non-finite values.
Results may differ from the reference program's by a relative error of at most 0.018.
Values may be sent and summed in bfloat16 or wider, within the bound.
No kernel may reach another device: no remote copies, remote signals or barrier semaphores. Data moves between devices by JAX's collectives and lax.ppermute only.
A program may use at most 192 MiB of HBM per device.

```python
import math
import jax
import jax.numpy as jnp
import numpy as np
from jax import lax

D = 3072
HD = 128
TOK_DEV = 1024
KVH = 8
QH = 24
TOKENS = 32768
MOST = 4096
NDOCS = 64
N_HEAD = 8


def shared_keys(key):
    base_keys = jnp.clip(jax.random.normal(key, (TOKENS, KVH * HD), jnp.float32), -5.0, 5.0)
    row_ids = jnp.arange(TOKENS)
    marked = row_ids % 257 == 128
    before = jnp.roll(marked, -1)
    return jnp.where(before[:, None], 0.988 * jnp.roll(base_keys, -1, axis=0), base_keys)


def draw_keys(key, part):
    return shared_keys(key).astype(jnp.bfloat16)


def draw_queries(key, part):
    key = jax.random.fold_in(key, 1)
    main_key = jax.random.fold_in(key, 0)
    queries_out = jnp.clip(jax.random.normal(main_key, (TOKENS, QH * HD), jnp.float32), -5.0, 5.0)
    return queries_out.astype(jnp.bfloat16)


def spiked(entries, stream_key, source, target, blocks, factor):
    owner, partner = [(jnp.arange(entries.shape[position]) // (entries.shape[position] // blocks)).reshape([-1 if axis == position else 1 for axis in range(entries.ndim)]) for position in (source, target)]
    chosen = jax.random.permutation(stream_key, blocks)[partner]
    strong = (owner == chosen) | (owner == (partner + blocks // 2) % blocks)
    return jnp.where(strong, factor * entries, entries)


def levels(rng, shape, pieces, least, high):
    factor_of = 1.0
    for dim, shards_of in pieces:
        draws = jax.random.uniform(jax.random.fold_in(jax.random.fold_in(rng, 6), dim), (shards_of,), jnp.float32, least / len(pieces), high / len(pieces))
        factor_of = factor_of * jnp.repeat(jnp.exp(draws), shape[dim] // shards_of).reshape((-1,) + (1,) * (len(shape) - 1 - dim))
    return factor_of


def split_up(number_of, total, bound, lean):
    weights = [(1 << 20) // math.isqrt(grade ** lean) + 1 for grade in range(2, number_of + 1)]
    rest, holding = total - bound - (number_of - 1), [1] * (number_of - 1)
    while rest > 0:
        free = [i for i in range(number_of - 1) if holding[i] < bound]
        whole, budget = sum([weights[i] for i in free]), rest
        for i in free:
            addition = min(bound - holding[i], max(1, budget * weights[i] // whole), rest)
            holding[i] = holding[i] + addition
            rest = rest - addition
    return np.array([bound] + holding)


def uneven(key, count, total, limit, lean):
    if count == 2:
        one = jax.random.randint(key, (), max(1, total - limit), min(limit, total - 1) + 1)
        return jnp.stack([one, total - one])
    sizes = jnp.asarray(split_up(count, total, limit, lean), jnp.int32)
    twos = (count - 1) // 2
    giver, sink = sizes[1:1 + 2 * twos:2], sizes[2:2 + 2 * twos:2]
    room = jnp.minimum(giver - 1, limit - sink)
    shifted = jax.random.randint(jax.random.fold_in(key, 1), (twos,), 0, 1 << 20) % (room + 1)
    sizes = sizes.at[1:1 + 2 * twos:2].set(giver - shifted).at[2:2 + 2 * twos:2].set(sink + shifted)
    return sizes[jax.random.permutation(jax.random.fold_in(key, 2), count)]


def centred(rng, shape, width, reach, cuts=(), kind=jnp.bfloat16):
    loudness = levels(rng, shape, cuts, -0.22, 0.18) if cuts else 1.0
    array = jax.random.normal(rng, shape, jnp.float32) * width * loudness
    return jnp.minimum(jnp.maximum(array, -reach), reach).astype(kind)


def gaussian_with(key, dims, deviation, limit, pieces, heavy, kind=jnp.bfloat16):
    entries = deviation * jax.random.normal(key, dims, jnp.float32)
    if pieces:
        entries = entries * levels(key, dims, pieces, -0.22, 0.18)
    return jnp.clip(spiked(entries, jax.random.fold_in(key, 3), *heavy), -limit, limit).astype(kind)


def setup_inputs(seed: int = 0) -> dict:
    arg_keys = jax.random.split(jax.random.key(seed), 6)
    return {
        "queries": draw_queries(jax.random.fold_in(arg_keys[5], 71), 0),
        "keys": draw_keys(jax.random.fold_in(arg_keys[5], 71), 0),
        "values": centred(arg_keys[2], (TOKENS, KVH * HD), 4.0, 24.0, ((0, 32), (1, 8))),
        "out_weight": gaussian_with(arg_keys[3], (QH * HD, D), (QH * HD) ** -0.5, 0.15625, ((0, 8),), (0, 1, 8, 2.0)),
        "doc_lengths": uneven(arg_keys[4], NDOCS, TOKENS, MOST, 2).astype(jnp.int32),
    }


def doc_index(positions, starts):
    hits = (starts[None, :] <= positions[:, None]).astype(jnp.int32)
    return jnp.sum(hits, axis=1, dtype=jnp.int32) - 1


def reference(queries, keys, values, out_weight, doc_lengths):
    starts = jnp.cumsum(doc_lengths, dtype=jnp.int32) - doc_lengths
    kv_heads = keys.shape[1] // HD
    group_size = queries.shape[1] // keys.shape[1]
    padding = jnp.zeros((MOST, keys.shape[1]), keys.dtype)
    keys_padded = jnp.concatenate([padding, keys], axis=0)
    values_padded = jnp.concatenate([padding, values], axis=0)
    score_scale = 1.0 / (HD ** 0.5)
    span = MOST + TOK_DEV

    def one_block(block_id):
        first_row = (block_id * TOK_DEV).astype(jnp.int32)
        query_block = lax.dynamic_slice_in_dim(queries, first_row, TOK_DEV, 0).astype(jnp.float32)
        query_block = query_block.reshape(TOK_DEV, kv_heads, group_size, HD)
        key_block = lax.dynamic_slice_in_dim(keys_padded, first_row, span, 0).astype(jnp.float32)
        key_block = key_block.reshape(span, kv_heads, HD)
        value_block = lax.dynamic_slice_in_dim(values_padded, first_row, span, 0).astype(jnp.float32)
        value_block = value_block.reshape(span, kv_heads, HD)
        query_pos = first_row + jnp.arange(TOK_DEV, dtype=jnp.int32)
        key_pos = first_row - MOST + jnp.arange(span, dtype=jnp.int32)
        visible = (doc_index(query_pos, starts)[:, None] == doc_index(key_pos, starts)[None, :])
        visible = visible & (key_pos[None, :] <= query_pos[:, None])
        scores = jnp.einsum("tkgd,nkd->kgtn", query_block, key_block) * score_scale
        live = visible[None, None]
        row_max = jnp.max(jnp.where(live, scores, -1e30), axis=-1)
        probs_live = jnp.where(live, jnp.exp(scores - row_max[..., None]), 0.0)
        totals = jnp.sum(probs_live, axis=-1)
        rounded = lax.optimization_barrier(probs_live.astype(jnp.bfloat16)).astype(jnp.float32)
        weighted = jnp.einsum("kgtn,nkd->tkgd", rounded, value_block)
        result = weighted / jnp.transpose(totals, (2, 0, 1))[..., None]
        return result.astype(jnp.bfloat16).reshape(TOK_DEV, kv_heads * group_size * HD)

    blocks = TOKENS // TOK_DEV
    attended = lax.map(one_block, jnp.arange(blocks, dtype=jnp.int32))
    attended = attended.reshape(TOKENS, queries.shape[1])
    col_count = queries.shape[1] // N_HEAD

    def add_group(running_sum, group_id):
        first_col = (group_id * col_count).astype(jnp.int32)
        columns = lax.dynamic_slice_in_dim(attended, first_col, col_count, 1)
        rows_used = lax.dynamic_slice_in_dim(out_weight, first_col, col_count, 0)
        partial_value = jnp.dot(columns, rows_used, preferred_element_type=jnp.float32).astype(jnp.bfloat16)
        partial_value = lax.optimization_barrier(partial_value).astype(jnp.float32)
        return running_sum + partial_value, None

    initial = jnp.zeros((TOKENS, out_weight.shape[1]), jnp.float32)
    summed, unused = lax.scan(add_group, initial, jnp.arange(N_HEAD, dtype=jnp.int32))
    return summed.astype(jnp.bfloat16)
```

```python
import functools

import jax
import jax.numpy as jnp
from jax import lax
from jax.experimental import pallas as pl
from jax.experimental.pallas import tpu as pltpu
from jax.sharding import PartitionSpec as P

HD = 128
WINDOW = 4
TQ = 256
TK = 512
LOG2E = 1.4426950408889634
MASKED = -1e30
LOWEST = -1e29


def attend_kernel(distance, last, rows, group, bounds_ref, start_ref, q_ref, k_ref, v_ref, *refs):
    if distance:
        acc_in, stat_in = refs[:2]
        refs = refs[2:]
    if last:
        out_ref, acc_ref, stat_ref, vt_ref = refs
    else:
        acc_ref, stat_ref, vt_ref = refs
    scale = LOG2E / HD**0.5
    tiles = rows // TQ
    if distance:
        acc_ref[...] = acc_in[...]
        stat_ref[...] = stat_in[...]
    else:
        acc_ref[...] = jnp.zeros_like(acc_ref)
        stat_ref[0:4, :] = jnp.full((4, rows), LOWEST, jnp.float32)
        stat_ref[4:8, :] = jnp.zeros((4, rows), jnp.float32)
    first_key = bounds_ref[0] - distance * rows

    def work():
        vt_ref[...] = v_ref[...].T

        def q_tile(t, carry):
            q0 = pl.multiple_of(t * TQ, TQ)
            low = bounds_ref[1 + 2 * t] - first_key
            high = bounds_ref[2 + 2 * t] - first_key
            begin = lax.div(jnp.clip(low, 0, rows), TK)
            end = rows // TK if distance else lax.div(q0 + TQ + TK - 1, TK)
            start_row = start_ref[0:1, pl.ds(q0, TQ)] - first_key

            def k_tile(j, carry):
                k0 = pl.multiple_of(j * TK, TK)
                key_tile = k_ref[pl.ds(k0, TK), :]
                value_tile = vt_ref[:, pl.ds(k0, TK)]

                def step(masked):
                    if masked:
                        key_pos = k0 + lax.broadcasted_iota(jnp.int32, (TK, TQ), 0)
                        visible = key_pos >= start_row
                        if not distance:
                            query_pos = q0 + lax.broadcasted_iota(jnp.int32, (TK, TQ), 1)
                            visible = visible & (key_pos <= query_pos)
                    for h in range(group):
                        scores = lax.dot_general(
                            key_tile,
                            q_ref[pl.ds(q0, TQ), h * HD : (h + 1) * HD],
                            (((1,), (1,)), ((), ())),
                            preferred_element_type=jnp.float32,
                        )
                        if masked:
                            scores = jnp.where(visible, scores, MASKED)
                        old_max = stat_ref[h : h + 1, pl.ds(q0, TQ)]
                        new_max = jnp.maximum(old_max, jnp.max(scores, axis=0, keepdims=True))
                        probs = jnp.exp2((scores - new_max) * scale)
                        rescale = jnp.exp2((old_max - new_max) * scale)
                        stat_ref[h : h + 1, pl.ds(q0, TQ)] = new_max
                        stat_ref[4 + h : 5 + h, pl.ds(q0, TQ)] = stat_ref[
                            4 + h : 5 + h, pl.ds(q0, TQ)
                        ] * rescale + jnp.sum(probs, axis=0, keepdims=True)
                        weighted = jnp.dot(
                            value_tile, probs.astype(jnp.bfloat16), preferred_element_type=jnp.float32
                        )
                        part = (slice(h * HD, (h + 1) * HD), pl.ds(q0, TQ))
                        acc_ref[part] = acc_ref[part] * rescale + weighted

                clear = k0 >= high
                if not distance:
                    clear = clear & (k0 + TK <= q0 + 1)
                pl.when(clear)(lambda: step(False))
                pl.when(jnp.logical_not(clear))(lambda: step(True))
                return carry

            lax.fori_loop(begin, end, k_tile, 0)
            return carry

        lax.fori_loop(0, tiles, q_tile, 0)

    if distance:
        pl.when((bounds_ref[1] < first_key + rows) & (first_key >= 0))(work)
    else:
        work()

    if last:
        def finish(t, carry):
            q0 = pl.multiple_of(t * TQ, TQ)
            for h in range(group):
                total = stat_ref[4 + h : 5 + h, pl.ds(q0, TQ)]
                scaled = acc_ref[h * HD : (h + 1) * HD, pl.ds(q0, TQ)] / total
                out_ref[pl.ds(q0, TQ), h * HD : (h + 1) * HD] = scaled.T.astype(jnp.bfloat16)
            return carry

        lax.fori_loop(0, tiles, finish, 0)


def attend(distance, last, bounds, start_rows, queries, keys, values, state):
    rows, columns = queries.shape
    group = columns // keys.shape[1]
    vmem = pl.BlockSpec(memory_space=pltpu.VMEM)
    shapes = [
        jax.ShapeDtypeStruct((columns, rows), jnp.float32),
        jax.ShapeDtypeStruct((8, rows), jnp.float32),
    ]
    scratch = [pltpu.VMEM((HD, rows), jnp.bfloat16)]
    if last:
        scratch = [pltpu.VMEM(s.shape, s.dtype) for s in shapes] + scratch
        shapes = [jax.ShapeDtypeStruct((rows, columns), jnp.bfloat16)]
    operands = [bounds, start_rows, queries, keys, values, *state]
    aliases = {}
    if state and not last:
        aliases = {5: 0, 6: 1}
    return pl.pallas_call(
        functools.partial(attend_kernel, distance, last, rows, group),
        out_shape=shapes,
        in_specs=[pl.BlockSpec(memory_space=pltpu.SMEM)] + [vmem] * (len(operands) - 1),
        out_specs=[vmem] * len(shapes),
        scratch_shapes=scratch,
        input_output_aliases=aliases,
        compiler_params=pltpu.CompilerParams(vmem_limit_bytes=40 * 2**20),
        cost_estimate=pl.CostEstimate(
            flops=4 * rows * rows * columns, bytes_accessed=6 * rows * columns, transcendentals=rows * rows * group
        ),
        name=f"attend_{distance}",
    )(*operands)


def body(queries, keys, values, out_weight, doc_lengths):
    rows, columns = queries.shape
    seq_size = lax.axis_size("seq")
    head_size = lax.axis_size("head")
    chips = head_size // 2
    starts = jnp.cumsum(doc_lengths, dtype=jnp.int32) - doc_lengths
    first_row = lax.axis_index("seq") * rows
    positions = first_row + jnp.arange(rows, dtype=jnp.int32)
    start_rows = jnp.max(jnp.where(starts[:, None] <= positions[None, :], starts[:, None], 0), axis=0)
    tile_starts = jnp.stack([start_rows[::TQ], start_rows[TQ - 1 :: TQ]], axis=1).reshape(-1)
    bounds = jnp.concatenate([first_row[None], tile_starts])
    start_rows = jnp.broadcast_to(start_rows[None, :], (8, rows))

    def next_block(block):
        return lax.ppermute(block, "seq", [(i, (i + 1) % seq_size) for i in range(seq_size)])

    def chip_shift(block, distance):
        route = [(i, (i + 2 * distance) % head_size) for i in range(head_size)]
        return lax.ppermute(block, "head", route)

    chip = lax.axis_index("head") // 2
    core = lax.axis_index("head") % 2
    wide = out_weight.shape[1] // chips

    def weight_columns(target):
        return lax.dynamic_slice_in_dim(out_weight, target * wide, wide, 1)

    state = ()
    for distance in range(WINDOW + 1):
        last = distance == WINDOW
        if not last:
            next_keys, next_values = next_block(keys), next_block(values)
        if distance == 1:
            weights = [weight_columns(chip)] + [
                chip_shift(weight_columns((chip + d) % chips), d) for d in range(1, chips)
            ]
        state = attend(distance, last, bounds, start_rows, queries, keys, values, state)
        keys, values = next_keys, next_values
    attended = state[0]

    half = rows // 2
    before, after = chip_shift(attended, 1), chip_shift(attended, -1)
    far = jnp.concatenate([chip_shift(before[:half], 1), chip_shift(after[half:], -1)], axis=0)

    def project(block, weight):
        return jnp.dot(block, weight, preferred_element_type=jnp.float32)

    summed = project(attended, weights[0]) + project(before, weights[1]) + project(after, weights[3])
    summed = summed + project(far, weights[2])
    mine = lax.dynamic_slice_in_dim(summed, core * columns, columns, 1)
    other = lax.dynamic_slice_in_dim(summed, (1 - core) * columns, columns, 1).astype(jnp.bfloat16)
    other = lax.ppermute(other, "head", [(i, i ^ 1) for i in range(head_size)])
    return (mine + other.astype(jnp.float32)).astype(jnp.bfloat16)


def solution(mesh):
    return jax.shard_map(
        body,
        mesh=mesh,
        in_specs=(P("seq", "head"), P("seq", "head"), P("seq", "head"), P("head", None), P()),
        out_specs=P("seq", "head"),
        check_vma=False,
    )
```

```python
import functools

import jax
import jax.numpy as jnp
from jax import lax
from jax.experimental import pallas as pl
from jax.experimental.pallas import tpu as pltpu
from jax.sharding import PartitionSpec as P

HD = 128
WINDOW = 4
TQ = 256
TK = 256
LOG2E = 1.4426950408889634
MASKED = -1e30
LOWEST = -1e29


def attend_kernel(distance, last, rows, group, bounds_ref, start_ref, q_ref, k_ref, v_ref, *refs):
    if distance:
        acc_in, stat_in = refs[:2]
        refs = refs[2:]
    if last:
        out_ref, acc_ref, stat_ref, vt_ref = refs
    else:
        acc_ref, stat_ref, vt_ref = refs
    scale = LOG2E / HD**0.5
    if distance:
        acc_ref[...] = acc_in[...]
        stat_ref[...] = stat_in[...]
    else:
        acc_ref[...] = jnp.zeros_like(acc_ref)
        stat_ref[0:4, :] = jnp.full((4, rows), LOWEST, jnp.float32)
        stat_ref[4:8, :] = jnp.zeros((4, rows), jnp.float32)
    first_key = bounds_ref[0] - distance * rows

    def tile(q0, q_count, key_from, key_to, masked):
        columns = slice(q0, q0 + q_count)
        pieces = [(k, min(TK, key_to - k)) for k in range(key_from, key_to, TK)]
        start_row = start_ref[0:1, columns] - first_key
        for h in range(group):
            query = q_ref[columns, h * HD : (h + 1) * HD]
            old_max = stat_ref[h : h + 1, columns]
            new_max = old_max
            scores = []
            for k0, count in pieces:
                piece = lax.dot_general(
                    k_ref[k0 : k0 + count, :], query, (((1,), (1,)), ((), ())), preferred_element_type=jnp.float32
                )
                if masked:
                    key_pos = k0 + lax.broadcasted_iota(jnp.int32, (count, q_count), 0)
                    visible = key_pos >= start_row
                    if not distance and k0 + count > q0 + 1:
                        query_pos = q0 + lax.broadcasted_iota(jnp.int32, (count, q_count), 1)
                        visible = visible & (key_pos <= query_pos)
                    piece = jnp.where(visible, piece, MASKED)
                new_max = jnp.maximum(new_max, jnp.max(piece, axis=0, keepdims=True))
                scores.append(piece)
            rescale = jnp.exp2((old_max - new_max) * scale)
            total = stat_ref[4 + h : 5 + h, columns] * rescale
            weighted = None
            for (k0, count), piece in zip(pieces, scores):
                probs = jnp.exp2((piece - new_max) * scale)
                total = total + jnp.sum(probs, axis=0, keepdims=True)
                term = jnp.dot(
                    vt_ref[:, k0 : k0 + count], probs.astype(jnp.bfloat16), preferred_element_type=jnp.float32
                )
                weighted = term if weighted is None else weighted + term
            stat_ref[h : h + 1, columns] = new_max
            stat_ref[4 + h : 5 + h, columns] = total
            part = (slice(h * HD, (h + 1) * HD), columns)
            acc_ref[part] = acc_ref[part] * rescale + weighted

    if distance == 0:
        vt_ref[...] = v_ref[...].T
        for q0 in range(0, rows, TQ):
            tile(q0, TQ, 0, q0 + TQ, True)
    else:
        low = bounds_ref[1] - first_key
        high = bounds_ref[2] - first_key
        needed = (low < rows) & (first_key >= 0)

        @pl.when(needed)
        def _():
            vt_ref[...] = v_ref[...].T

        if last:
            for t, q0 in enumerate(range(0, rows, TQ)):
                seen = bounds_ref[3 + t] - first_key
                pl.when((seen < rows) & (first_key >= 0))(lambda q0=q0: tile(q0, TQ, q0, rows, True))
        else:
            pl.when(needed & (high <= 0))(lambda: tile(0, rows, 0, rows, False))
            pl.when(needed & (high > 0))(lambda: tile(0, rows, 0, rows, True))

    if last:
        for h in range(group):
            scaled = acc_ref[h * HD : (h + 1) * HD, :] / stat_ref[4 + h : 5 + h, :]
            out_ref[:, h * HD : (h + 1) * HD] = scaled.T.astype(jnp.bfloat16)


def attend(distance, last, bounds, start_rows, queries, keys, values, state):
    rows, columns = queries.shape
    group = columns // keys.shape[1]
    vmem = pl.BlockSpec(memory_space=pltpu.VMEM)
    shapes = [
        jax.ShapeDtypeStruct((columns, rows), jnp.float32),
        jax.ShapeDtypeStruct((8, rows), jnp.float32),
    ]
    scratch = [pltpu.VMEM((HD, rows), jnp.bfloat16)]
    if last:
        scratch = [pltpu.VMEM(s.shape, s.dtype) for s in shapes] + scratch
        shapes = [jax.ShapeDtypeStruct((rows, columns), jnp.bfloat16)]
    operands = [bounds, start_rows, queries, keys, values, *state]
    aliases = {}
    if state and not last:
        aliases = {5: 0, 6: 1}
    return pl.pallas_call(
        functools.partial(attend_kernel, distance, last, rows, group),
        out_shape=shapes,
        in_specs=[pl.BlockSpec(memory_space=pltpu.SMEM)] + [vmem] * (len(operands) - 1),
        out_specs=[vmem] * len(shapes),
        scratch_shapes=scratch,
        input_output_aliases=aliases,
        compiler_params=pltpu.CompilerParams(vmem_limit_bytes=40 * 2**20),
        cost_estimate=pl.CostEstimate(
            flops=4 * rows * rows * columns, bytes_accessed=6 * rows * columns, transcendentals=rows * rows * group
        ),
        name=f"attend_{distance}",
    )(*operands)


def body(queries, keys, values, out_weight, doc_lengths):
    rows, columns = queries.shape
    seq_size = lax.axis_size("seq")
    head_size = lax.axis_size("head")
    chips = head_size // 2
    starts = jnp.cumsum(doc_lengths, dtype=jnp.int32) - doc_lengths
    first_row = lax.axis_index("seq") * rows
    positions = first_row + jnp.arange(rows, dtype=jnp.int32)
    start_rows = jnp.max(jnp.where(starts[:, None] <= positions[None, :], starts[:, None], 0), axis=0)
    bounds = jnp.concatenate([first_row[None], start_rows[:1], start_rows[-1:], start_rows[::TQ]])
    start_rows = jnp.broadcast_to(start_rows[None, :], (8, rows))

    def next_block(block):
        return lax.ppermute(block, "seq", [(i, (i + 1) % seq_size) for i in range(seq_size)])

    def chip_shift(block, distance):
        route = [(i, (i + 2 * distance) % head_size) for i in range(head_size)]
        return lax.ppermute(block, "head", route)

    chip = lax.axis_index("head") // 2
    core = lax.axis_index("head") % 2
    wide = out_weight.shape[1] // chips

    def weight_columns(target):
        return lax.dynamic_slice_in_dim(out_weight, target * wide, wide, 1)

    state = ()
    attended = None
    for distance in range(WINDOW + 1):
        last = distance == WINDOW
        if not last:
            if distance:
                keys, _ = lax.optimization_barrier((keys, state[1]))
                values, _ = lax.optimization_barrier((values, state[1]))
            next_keys, next_values = next_block(keys), next_block(values)
        if distance == 0:
            weights = [weight_columns(chip)] + [
                chip_shift(weight_columns((chip + d) % chips), d) for d in range(1, chips)
            ]
        if not last:
            state = attend(distance, last, bounds, start_rows, queries, keys, values, state)
        else:
            (state, weights) = lax.optimization_barrier((state, weights))
            attended = attend(distance, last, bounds, start_rows, queries, keys, values, state)[0]
        keys, values = next_keys, next_values

    half = rows // 2
    before, after = chip_shift(attended, 1), chip_shift(attended, -1)
    far = jnp.concatenate([chip_shift(before[:half], 1), chip_shift(after[half:], -1)], axis=0)

    def project(block, weight):
        return jnp.dot(block, weight, preferred_element_type=jnp.float32)

    summed = project(attended, weights[0]) + project(before, weights[1]) + project(after, weights[3])
    summed = summed + project(far, weights[2])
    mine = lax.dynamic_slice_in_dim(summed, core * columns, columns, 1)
    other = lax.dynamic_slice_in_dim(summed, (1 - core) * columns, columns, 1).astype(jnp.bfloat16)
    other = lax.ppermute(other, "head", [(i, i ^ 1) for i in range(head_size)])
    return (mine + other.astype(jnp.float32)).astype(jnp.bfloat16)


def solution(mesh):
    return jax.shard_map(
        body,
        mesh=mesh,
        in_specs=(P("seq", "head"), P("seq", "head"), P("seq", "head"), P("head", None), P()),
        out_specs=P("seq", "head"),
        check_vma=False,
    )
```

```python
import functools

import jax
import jax.numpy as jnp
from jax import lax
from jax.experimental import pallas as pl
from jax.experimental.pallas import tpu as pltpu
from jax.sharding import PartitionSpec as P

HD = 128
ROW = 8
TQ = 256
TK = 256
LOG2E = 1.4426950408889634
SCALE = LOG2E / HD**0.5
MASKED = -1e30
LOWEST = -1e29
VMEM = pl.BlockSpec(memory_space=pltpu.VMEM)
SMEM = pl.BlockSpec(memory_space=pltpu.SMEM)
ANY = pl.BlockSpec(memory_space=pl.ANY)
NT = (((1,), (1,)), ((), ()))


def attend_tile(q_ref, group, q0, q_count, parts, stats, start_row, causal):
    out = []
    for h in range(group):
        query = q_ref[q0 : q0 + q_count, h * HD : (h + 1) * HD]
        old_max, old_sum = stats[h]
        new_max = old_max
        scores = []
        for first, count, keys, _, masked in parts:
            piece = lax.dot_general(keys(), query, NT, preferred_element_type=jnp.float32)
            if masked:
                key_pos = first + lax.broadcasted_iota(jnp.int32, (count, q_count), 0)
                visible = key_pos >= start_row
                if causal and first + count > q0 + 1:
                    query_pos = q0 + lax.broadcasted_iota(jnp.int32, (count, q_count), 1)
                    visible = visible & (key_pos <= query_pos)
                piece = jnp.where(visible, piece, MASKED)
            new_max = jnp.maximum(new_max, jnp.max(piece, axis=0, keepdims=True))
            scores.append(piece)
        rescale = jnp.exp2((old_max - new_max) * SCALE)
        total = old_sum * rescale
        weighted = None
        for (_, _, _, values, _), piece in zip(parts, scores):
            probs = jnp.exp2((piece - new_max) * SCALE)
            total = total + jnp.sum(probs, axis=0, keepdims=True)
            term = jnp.dot(values(), probs.astype(jnp.bfloat16), preferred_element_type=jnp.float32)
            weighted = term if weighted is None else weighted + term
        out.append((new_max, total, rescale, weighted))
    return out


def update(acc_ref, stat_ref, group, q0, q_count, results):
    columns = slice(q0, q0 + q_count)
    for h, (new_max, total, rescale, weighted) in enumerate(results):
        stat_ref[h : h + 1, columns] = new_max
        stat_ref[4 + h : 5 + h, columns] = total
        part = (slice(h * HD, (h + 1) * HD), columns)
        acc_ref[part] = acc_ref[part] * rescale + weighted


def read_stats(stat_ref, group, q0, q_count):
    columns = slice(q0, q0 + q_count)
    return [(stat_ref[h : h + 1, columns], stat_ref[4 + h : 5 + h, columns]) for h in range(group)]


def first_kernel(rows, group, docs, length_ref, q_hbm, k_hbm, v_hbm, acc_ref, stat_ref, start_ref, bound_ref, q_ref, k_ref, v_ref, vt_ref, sem):
    copies = [
        pltpu.make_async_copy(source, target, sem.at[i])
        for i, (source, target) in enumerate(((q_hbm, q_ref), (k_hbm, k_ref), (v_hbm, v_ref)))
    ]
    for copy in copies:
        copy.start()
    first_row = lax.axis_index("seq") * rows
    tiles = range(0, rows, TQ)
    marks = [first_row, first_row + rows - 1] + [first_row + q0 for q0 in tiles]
    positions = first_row + lax.broadcasted_iota(jnp.int32, (1, rows), 1)

    def document(d, carried):
        begin, row_starts, found = carried
        row_starts = jnp.where(positions >= begin, begin, row_starts)
        found = [jnp.where(mark >= begin, begin, old) for mark, old in zip(marks, found)]
        return begin + length_ref[d], row_starts, found

    zero = jnp.int32(0)
    _, row_starts, found = lax.fori_loop(
        0, docs, document, (zero, jnp.zeros((1, rows), jnp.int32), [zero for _ in marks])
    )
    start_ref[0:1, :] = row_starts
    start_ref[1:8, :] = jnp.zeros((7, rows), jnp.int32)
    bound_ref[0] = first_row
    for i, value in enumerate(found):
        bound_ref[1 + i] = value
    bound_ref[7] = zero
    for copy in copies:
        copy.wait()
    vt_ref[...] = v_ref[...].T
    stat_ref[...] = jnp.zeros_like(stat_ref)
    start = row_starts - first_row
    for q0 in tiles:
        columns = slice(q0, q0 + TQ)
        stats = [(jnp.full((1, TQ), LOWEST, jnp.float32), jnp.zeros((1, TQ), jnp.float32)) for _ in range(group)]
        parts = [
            (k0, TK, lambda k0=k0: k_ref[k0 : k0 + TK, :], lambda k0=k0: vt_ref[:, k0 : k0 + TK], True)
            for k0 in range(0, q0 + TQ, TK)
        ]
        results = attend_tile(q_ref, group, q0, TQ, parts, stats, start[:, columns], True)
        for h, (new_max, total, _, weighted) in enumerate(results):
            stat_ref[h : h + 1, columns] = new_max
            stat_ref[4 + h : 5 + h, columns] = total
            acc_ref[h * HD : (h + 1) * HD, columns] = weighted


def middle_kernel(distance, rows, group, bound_ref, start_ref, q_ref, k_ref, v_ref, acc_in, stat_in, acc_ref, stat_ref, vt_ref):
    acc_ref[...] = acc_in[...]
    stat_ref[...] = stat_in[...]
    first_key = bound_ref[0] - distance * rows
    needed = (bound_ref[1] < first_key + rows) & (first_key >= 0)
    inside = bound_ref[2] > first_key

    def work(masked):
        vt_ref[...] = v_ref[...].T
        start = start_ref[0:1, :] - first_key
        parts = [
            (k0, TK, lambda k0=k0: k_ref[k0 : k0 + TK, :], lambda k0=k0: vt_ref[:, k0 : k0 + TK], masked)
            for k0 in range(0, rows, TK)
        ]
        stats = read_stats(stat_ref, group, 0, rows)
        update(acc_ref, stat_ref, group, 0, rows, attend_tile(q_ref, group, 0, rows, parts, stats, start, False))

    pl.when(needed & jnp.logical_not(inside))(lambda: work(False))
    pl.when(needed & inside)(lambda: work(True))


def last_kernel(half, rows, group, bound_ref, start_ref, q_ref, k_ref, v_ref, *refs):
    far_refs = refs[: 2 - half]
    acc_in, stat_in, *out_refs, acc_ref, stat_ref, vt_ref = refs[2 - half :]
    size = rows // 2
    base = half * size
    acc_ref[...] = acc_in[:, base : base + size]
    stat_ref[...] = stat_in[:, base : base + size]
    first_key = bound_ref[0] - 3 * rows
    needed = (bound_ref[3 + base // TQ] < first_key + rows) & (first_key >= 0)
    inside = bound_ref[2] > first_key

    def near(masked):
        vt_ref[...] = v_ref[...].T
        start = start_ref[0:1, base : base + size] - first_key
        parts = [
            (k0, TK, lambda k0=k0: k_ref[k0 : k0 + TK, :], lambda k0=k0: vt_ref[:, k0 : k0 + TK], masked)
            for k0 in range(0, rows, TK)
        ]
        results = attend_tile(q_ref, group, base, size, parts, read_stats(stat_ref, group, 0, size), start, False)
        update(acc_ref, stat_ref, group, 0, size, results)

    pl.when(needed & jnp.logical_not(inside))(lambda: near(False))
    pl.when(needed & inside)(lambda: near(True))

    far_key = first_key - rows

    def far(ref, key_from, key_to, q0):
        vt_ref[:, 0 : key_to - key_from] = ref[key_from % size : key_from % size + key_to - key_from, HD:].T
        start = start_ref[0:1, base + q0 : base + q0 + TQ] - far_key
        parts = [
            (
                k0,
                TK,
                lambda k0=k0: ref[k0 % size : k0 % size + TK, :HD],
                lambda k0=k0: vt_ref[:, k0 - key_from : k0 - key_from + TK],
                True,
            )
            for k0 in range(key_from, key_to, TK)
        ]
        results = attend_tile(q_ref, group, base + q0, TQ, parts, read_stats(stat_ref, group, q0, TQ), start, False)
        update(acc_ref, stat_ref, group, q0, TQ, results)

    for q0 in range(0, size, TQ):
        seen = bound_ref[3 + (base + q0) // TQ] - far_key
        pl.when((seen < rows) & (far_key >= 0))(
            lambda q0=q0: far(far_refs[0], max(size, base + q0), rows, q0)
        )
        if not half:
            pl.when((seen < size) & (far_key >= 0))(lambda q0=q0: far(far_refs[1], q0, size, q0))

    for h in range(group):
        for out_ref, columns in zip(out_refs, (slice(0, size // 2), slice(size // 2, size))):
            scaled = acc_ref[h * HD : (h + 1) * HD, columns] / stat_ref[4 + h : 5 + h, columns]
            out_ref[:, h * HD : (h + 1) * HD] = scaled.T.astype(jnp.bfloat16)


def cost(rows, keys, columns):
    return pl.CostEstimate(flops=4 * rows * keys * columns, bytes_accessed=6 * rows * columns, transcendentals=rows * keys * 3)


def attend_first(doc_lengths, queries, keys, values):
    rows, columns = queries.shape
    group = columns // HD
    return pl.pallas_call(
        functools.partial(first_kernel, rows, group, doc_lengths.shape[0]),
        out_shape=[
            jax.ShapeDtypeStruct((columns, rows), jnp.float32),
            jax.ShapeDtypeStruct((8, rows), jnp.float32),
            jax.ShapeDtypeStruct((8, rows), jnp.int32),
            jax.ShapeDtypeStruct((8,), jnp.int32),
        ],
        in_specs=[SMEM, ANY, ANY, ANY],
        out_specs=[VMEM, VMEM, VMEM, SMEM],
        scratch_shapes=[
            pltpu.VMEM(queries.shape, jnp.bfloat16),
            pltpu.VMEM(keys.shape, jnp.bfloat16),
            pltpu.VMEM(values.shape, jnp.bfloat16),
            pltpu.VMEM((HD, rows), jnp.bfloat16),
            pltpu.SemaphoreType.DMA((3,)),
        ],
        compiler_params=pltpu.CompilerParams(vmem_limit_bytes=32 * 2**20),
        cost_estimate=cost(rows, rows, columns),
        name="attend_first",
    )(doc_lengths, queries, keys, values)


def attend_middle(distance, bounds, start_rows, queries, keys, values, state):
    rows, columns = queries.shape
    return pl.pallas_call(
        functools.partial(middle_kernel, distance, rows, columns // HD),
        out_shape=[jax.ShapeDtypeStruct(s.shape, s.dtype) for s in state],
        in_specs=[SMEM] + [VMEM] * 6,
        out_specs=[VMEM, VMEM],
        scratch_shapes=[pltpu.VMEM((HD, rows), jnp.bfloat16)],
        input_output_aliases={5: 0, 6: 1},
        compiler_params=pltpu.CompilerParams(vmem_limit_bytes=32 * 2**20),
        cost_estimate=cost(rows, rows, columns),
        name=f"attend_{distance}",
    )(bounds, start_rows, queries, keys, values, *state)


def attend_last(half, bounds, start_rows, queries, keys, values, far, state):
    rows, columns = queries.shape
    size = rows // 2
    return pl.pallas_call(
        functools.partial(last_kernel, half, rows, columns // HD),
        out_shape=[jax.ShapeDtypeStruct((size // 2, columns), jnp.bfloat16)] * 2,
        in_specs=[SMEM] + [VMEM] * (6 + len(far)),
        out_specs=[VMEM, VMEM],
        scratch_shapes=[
            pltpu.VMEM((columns, size), jnp.float32),
            pltpu.VMEM((8, size), jnp.float32),
            pltpu.VMEM((HD, rows), jnp.bfloat16),
        ],
        compiler_params=pltpu.CompilerParams(vmem_limit_bytes=32 * 2**20),
        cost_estimate=cost(size, rows, columns),
        name=f"attend_last_{half}",
    )(bounds, start_rows, queries, keys, values, *far, *state)


def near_kernel(pieces, *refs):
    blocks, weight_refs, out_ref = refs[: 3 * pieces], refs[3 * pieces : -1], refs[-1]
    size = blocks[0].shape[0]
    weight = jnp.concatenate([w[...] for w in weight_refs], axis=0)
    for i in range(pieces):
        block = jnp.concatenate([b[...] for b in blocks[i::pieces]], axis=1)
        out_ref[i * size : (i + 1) * size, :] = jnp.dot(block, weight, preferred_element_type=jnp.float32)


def project_near(blocks, weights):
    pieces = len(blocks) // 3
    size, columns = blocks[0].shape
    wide = weights[0].shape[1]
    return pl.pallas_call(
        functools.partial(near_kernel, pieces),
        out_shape=jax.ShapeDtypeStruct((pieces * size, wide), jnp.float32),
        in_specs=[VMEM] * (len(blocks) + 3),
        out_specs=VMEM,
        compiler_params=pltpu.CompilerParams(vmem_limit_bytes=32 * 2**20),
        cost_estimate=pl.CostEstimate(
            flops=6 * pieces * size * columns * wide, bytes_accessed=8 * pieces * size * wide, transcendentals=0
        ),
        name="project_near",
    )(*blocks, *weights)


def far_kernel(pieces, *refs):
    blocks, (weight_ref, near_ref, kept_ref, given_ref) = refs[:pieces], refs[pieces:]
    size = blocks[0].shape[0]
    columns = kept_ref.shape[1]
    for i in range(pieces):
        part = slice(i * size, (i + 1) * size)
        total = near_ref[part, :] + jnp.dot(blocks[i][...], weight_ref[...], preferred_element_type=jnp.float32)
        kept_ref[part, :] = total[:, :columns]
        given_ref[part, :] = total[:, columns:].astype(jnp.bfloat16)


def project_far(blocks, weight, near):
    rows, wide = near.shape
    columns = wide // 2
    return pl.pallas_call(
        functools.partial(far_kernel, len(blocks)),
        out_shape=[jax.ShapeDtypeStruct((rows, columns), t) for t in (jnp.float32, jnp.bfloat16)],
        in_specs=[VMEM] * (len(blocks) + 2),
        out_specs=[VMEM, VMEM],
        compiler_params=pltpu.CompilerParams(vmem_limit_bytes=32 * 2**20),
        cost_estimate=pl.CostEstimate(
            flops=2 * rows * wide * blocks[0].shape[1], bytes_accessed=8 * rows * wide, transcendentals=0
        ),
        name="project_far",
    )(*blocks, weight, near)


def join_kernel(*refs):
    out_ref = refs[-1]
    size = refs[0].shape[0]
    for i in range(len(refs) // 2):
        kept, taken = refs[2 * i], refs[2 * i + 1]
        out_ref[i * size : (i + 1) * size, :] = (kept[...] + taken[...].astype(jnp.float32)).astype(jnp.bfloat16)


def join(*halves):
    size, columns = halves[0].shape
    return pl.pallas_call(
        join_kernel,
        out_shape=jax.ShapeDtypeStruct((size * len(halves) // 2, columns), jnp.bfloat16),
        in_specs=[VMEM] * len(halves),
        out_specs=VMEM,
        compiler_params=pltpu.CompilerParams(vmem_limit_bytes=32 * 2**20),
        name="join",
    )(*halves)


def after(value, *others):
    return lax.optimization_barrier((value, others))[0]


def body(queries, keys, values, out_weight, doc_lengths):
    rows, columns = queries.shape
    seq_size = lax.axis_size("seq")
    head_size = lax.axis_size("head")
    chips = head_size // 2
    half = rows // 2
    chip = lax.axis_index("head") // 2
    core = lax.axis_index("head") % 2

    def next_block(block):
        return lax.ppermute(block, "seq", [(i, (i + 1) % seq_size) for i in range(seq_size)])

    def back(block, distance):
        return lax.ppermute(block, "seq", [(i, i - i % ROW + (i - distance) % ROW) for i in range(seq_size)])

    def four_on(block):
        owners = [i - i % ROW + (i + 3) % ROW for i in range(seq_size)]
        return lax.ppermute(block, "seq", [(i, (owner + 4) % seq_size) for i, owner in enumerate(owners)])

    def chip_shift(block, distance):
        route = [(i, (i + 2 * distance) % head_size) for i in range(head_size)]
        return lax.ppermute(block, "head", route)

    def swap(block):
        return lax.ppermute(block, "head", [(i, i ^ 1) for i in range(head_size)])

    def weight_columns(target):
        return jnp.concatenate(
            [lax.dynamic_slice_in_dim(out_weight, (2 * target + c) * columns, columns, 1) for c in (core, 1 - core)], axis=1
        )

    k1, v1 = next_block(keys), next_block(values)
    far = back(jnp.concatenate([keys, values], axis=1), 1)
    *state, start_rows, bounds = attend_first(doc_lengths, queries, keys, values)
    k2, v2 = next_block(after(k1, state[1])), next_block(after(v1, state[1]))
    far = back(after(far, state[1]), 2)
    blocks = [after(weight_columns((chip + d) % chips), state[1], k1, v1) for d in range(chips)]
    weights = {0: blocks[0], 1: chip_shift(blocks[1], 1), 3: chip_shift(blocks[3], 3)}
    state = attend_middle(1, bounds, start_rows, queries, k1, v1, state)
    k3, v3 = next_block(after(k2, state[1])), next_block(after(v2, state[1]))
    bounds = after(bounds, weights[1], weights[3])
    weights[2] = chip_shift(after(blocks[2], weights[1], weights[3]), 2)
    state = attend_middle(2, bounds, start_rows, queries, k2, v2, state)
    far = after(far, state[1])
    far_late, far_early = four_on(far[half:]), four_on(far[:half])
    bounds = after(bounds, weights[2])
    late = attend_last(1, bounds, start_rows, queries, k3, v3, (far_late,), state)

    def sides(pieces):
        return [chip_shift(p, d) for d in (1, -1) for p in reversed(pieces)]

    def ordered(received):
        return received[1], received[0], received[3], received[2]

    late_before0, late_before1, late_after0, late_after1 = ordered(sides(late))
    bounds = after(bounds, late_before1)
    early = attend_last(0, bounds, start_rows, queries, k3, v3, (far_late, far_early), state)
    early_before0, early_before1, early_after0, early_after1 = ordered(sides(early))
    near_weights = (weights[0], weights[1], weights[3])
    late_far = chip_shift(late_before0, 1), chip_shift(late_after1, -1)
    late_near = project_near((*late, late_before0, late_before1, late_after0, late_after1), near_weights)
    early_far = chip_shift(early_before0, 1), chip_shift(early_after1, -1)
    early_near = project_near((*early, early_before0, early_before1, early_after0, early_after1), near_weights)
    late_kept, late_given = project_far(late_far, weights[2], late_near)
    late_taken = swap(late_given)
    early_kept, early_given = project_far(early_far, weights[2], early_near)
    early_taken = swap(early_given)
    return join(early_kept, early_taken, late_kept, late_taken)


def solution(mesh):
    return jax.shard_map(
        body,
        mesh=mesh,
        in_specs=(P("seq", "head"), P("seq", "head"), P("seq", "head"), P("head", None), P()),
        out_specs=P("seq", "head"),
        check_vma=False,
    )
```

```python
import functools

import jax
import jax.numpy as jnp
from jax import lax
from jax.experimental import pallas as pl
from jax.experimental.pallas import tpu as pltpu
from jax.sharding import PartitionSpec as P

HD = 128
ROW = 8
TFIRST = 256
TQ = 512
TK = 512
LOG2E = 1.4426950408889634
SCALE = LOG2E / HD**0.5
MASKED = -1e30
LOWEST = -1e29
VMEM = pl.BlockSpec(memory_space=pltpu.VMEM)
SMEM = pl.BlockSpec(memory_space=pltpu.SMEM)
ANY = pl.BlockSpec(memory_space=pl.ANY)
NT = (((1,), (1,)), ((), ()))


def put_scores(score_ref, row, query, key_ref, k0, count):
    for j in range(0, count, TK):
        n = min(TK, count - j)
        score_ref[row + j : row + j + n, :] = lax.dot_general(
            key_ref[k0 + j : k0 + j + n, :], query, NT, preferred_element_type=jnp.float32
        )


def add_keys(score_ref, row, count, turned_ref, v0, old_max, old_sum, old_acc, start_row=None, q0=None):
    size = score_ref.shape[1]

    def piece(j, n):
        scores = score_ref[row + j : row + j + n, :]
        if start_row is None:
            return scores
        key_pos = j + lax.broadcasted_iota(jnp.int32, (n, size), 0)
        visible = key_pos >= start_row
        if q0 is not None and j + n > q0 + 1:
            visible = visible & (key_pos <= q0 + lax.broadcasted_iota(jnp.int32, (n, size), 1))
        return jnp.where(visible, scores, MASKED)

    pieces = [(j, min(TK, count - j)) for j in range(0, count, TK)]
    new_max = old_max
    for j, n in pieces:
        new_max = jnp.maximum(new_max, jnp.max(piece(j, n), axis=0, keepdims=True))
    rescale = jnp.exp2((old_max - new_max) * SCALE)
    total = old_sum * rescale
    acc = old_acc * rescale
    for j, n in pieces:
        probs = jnp.exp2((piece(j, n) - new_max) * SCALE)
        total = total + jnp.sum(probs, axis=0, keepdims=True)
        acc = acc + jnp.dot(
            turned_ref[:, v0 + j : v0 + j + n], probs.astype(jnp.bfloat16), preferred_element_type=jnp.float32
        )
    return new_max, total, acc


def sweep(steps, first, key_ref, k0, count, turned_ref, v0, state, q_ref, score_refs, start_row):
    acc_ref, stat_ref = state

    def make(i):
        q_at, _ = first(i)
        put_scores(score_refs[i % 2], 0, q_ref[pl.ds(q_at, TQ), :], key_ref, k0, count)

    def use(i):
        columns = pl.ds(first(i)[1], TQ)
        start = None if start_row is None else start_row(i)
        stat_ref[0:1, columns], stat_ref[1:2, columns], acc_ref[:, columns] = add_keys(
            score_refs[i % 2], 0, count, turned_ref, v0, stat_ref[0:1, columns], stat_ref[1:2, columns],
            acc_ref[:, columns], start,
        )

    make(0)
    for i in range(steps):
        if i + 1 < steps:
            make(i + 1)
        use(i)


def first_kernel(
    rows, group, docs, length_ref, q_hbm, k_hbm, v_hbm,
    acc_ref, stat_ref, stack_ref, start_ref, bound_ref,
    q_ref, k_ref, v_ref, vt_ref, score_ref, sem,
):
    copies = [
        pltpu.make_async_copy(source, target, sem.at[i])
        for i, (source, target) in enumerate(((q_hbm, q_ref), (k_hbm, k_ref), (v_hbm, v_ref)))
    ]
    for copy in copies:
        copy.start()
    first_row = lax.axis_index("seq") * rows
    tiles = range(0, rows, TFIRST)
    marks = [first_row, first_row + rows // 2, first_row + rows - 1]
    positions = first_row + lax.broadcasted_iota(jnp.int32, (1, rows), 1)

    def document(d, carried):
        begin, row_starts, found = carried
        row_starts = jnp.where(positions >= begin, begin, row_starts)
        found = [jnp.where(mark >= begin, begin, old) for mark, old in zip(marks, found)]
        return begin + length_ref[d], row_starts, found

    zero = jnp.int32(0)
    _, row_starts, found = lax.fori_loop(
        0, docs, document, (zero, jnp.zeros((1, rows), jnp.int32), [zero for _ in marks])
    )
    start_ref[0:1, :] = row_starts
    start_ref[1:8, :] = jnp.zeros((7, rows), jnp.int32)
    bound_ref[0] = first_row
    for i, value in enumerate(found):
        bound_ref[1 + i] = value
    for i in range(len(found) + 1, 8):
        bound_ref[i] = zero
    for copy in copies:
        copy.wait()
    vt_ref[...] = v_ref[...].T
    for h in range(group):
        stack_ref[h * rows : (h + 1) * rows, :] = q_ref[:, h * HD : (h + 1) * HD]
    stat_ref[...] = jnp.zeros_like(stat_ref)
    offsets = {}
    used = 0
    for q0 in tiles:
        offsets[q0] = used
        used += q0 + TFIRST

    def head(h, carried):
        base = pl.multiple_of(h * rows, rows)

        def make(q0):
            put_scores(score_ref, offsets[q0], stack_ref[pl.ds(base + q0, TFIRST), :], k_ref, 0, q0 + TFIRST)

        def use(q0):
            columns = pl.ds(base + q0, TFIRST)
            start = start_ref[0:1, q0 : q0 + TFIRST] - first_row
            lowest = jnp.full((1, TFIRST), LOWEST, jnp.float32)
            none = jnp.zeros((1, TFIRST), jnp.float32)
            stat_ref[0:1, columns], stat_ref[1:2, columns], acc_ref[:, columns] = add_keys(
                score_ref, offsets[q0], q0 + TFIRST, vt_ref, 0, lowest, none, jnp.zeros((HD, TFIRST), jnp.float32), start, q0
            )

        order = list(reversed(tiles))
        make(order[0])
        for i, q0 in enumerate(order):
            if i + 1 < len(order):
                make(order[i + 1])
            use(q0)
        return carried

    lax.fori_loop(0, group, head, 0)


def middle_kernel(
    distance, rows, group, bound_ref, start_ref, q_ref, k_ref, v_ref, acc_in, stat_in, acc_ref, stat_ref, vt_ref, *score_refs
):
    acc_ref[...] = acc_in[...]
    stat_ref[...] = stat_in[...]
    first_key = bound_ref[0] - distance * rows
    needed = (bound_ref[1] < first_key + rows) & (first_key >= 0)
    inside = bound_ref[3] > first_key
    tiles = rows // TQ

    def work(masked):
        vt_ref[...] = v_ref[...].T

        def head(h, carried):
            def first(i):
                return (pl.multiple_of(h * rows + i * TQ, TQ),) * 2

            def start_row(i):
                return start_ref[0:1, i * TQ : (i + 1) * TQ] - first_key

            sweep(
                tiles, first, k_ref, 0, rows, vt_ref, 0, (acc_ref, stat_ref), q_ref, score_refs, start_row if masked else None
            )
            return carried

        lax.fori_loop(0, group, head, 0)

    pl.when(needed & jnp.logical_not(inside))(lambda: work(False))
    pl.when(needed & inside)(lambda: work(True))


def last_kernel(half, rows, group, bound_ref, start_ref, q_ref, k_ref, v_ref, *refs):
    far_count = 1 if half else 3
    far_refs = refs[:far_count]
    acc_in, stat_in, out0_ref, out1_ref, acc_ref, stat_ref, vt_ref, *score_refs = refs[far_count:]
    size = rows // 2
    base = half * size
    for h in range(group):
        acc_ref[:, h * size : (h + 1) * size] = acc_in[:, h * rows + base : h * rows + base + size]
        stat_ref[:, h * size : (h + 1) * size] = stat_in[:, h * rows + base : h * rows + base + size]

    def block(key_ref, v_block, key_from, key_count, first_key, masked):
        vt_ref[:, :key_count] = v_block().T

        def first(i):
            return i * rows + base, i * size

        def start_row(i):
            return start_ref[0:1, base : base + size] - first_key

        sweep(
            group, first, key_ref, key_from, key_count, vt_ref, 0, (acc_ref, stat_ref), q_ref, score_refs,
            start_row if masked else None,
        )

    near_key = bound_ref[0] - 3 * rows
    lowest = bound_ref[1 + half]
    needed = (lowest < near_key + rows) & (near_key >= 0)
    inside = bound_ref[3] > near_key
    pl.when(needed & jnp.logical_not(inside))(lambda: block(k_ref, lambda: v_ref[...], 0, rows, near_key, False))
    pl.when(needed & inside)(lambda: block(k_ref, lambda: v_ref[...], 0, rows, near_key, True))

    far_key = near_key - rows
    late_ref = far_refs[0]
    pl.when((lowest < far_key + rows) & (far_key >= 0))(
        lambda: block(late_ref.at[:, :HD], lambda: late_ref[:, HD:], 0, size, far_key + size, True)
    )
    if not half:
        pl.when((lowest < far_key + size) & (far_key >= 0))(
            lambda: block(far_refs[1], lambda: far_refs[2][...], 0, size, far_key, True)
        )

    piece = size // 2
    for h in range(group):
        for i, out_ref in enumerate((out0_ref, out1_ref)):
            columns = slice(h * size + i * piece, h * size + (i + 1) * piece)
            scaled = acc_ref[:, columns] / stat_ref[1:2, columns]
            out_ref[:, h * HD : (h + 1) * HD] = scaled.T.astype(jnp.bfloat16)


def cost(rows, keys, columns):
    return pl.CostEstimate(flops=4 * rows * keys * columns, bytes_accessed=6 * rows * columns, transcendentals=rows * keys * 3)


def params():
    return pltpu.CompilerParams(vmem_limit_bytes=32 * 2**20)


def attend_first(doc_lengths, queries, keys, values):
    rows, columns = queries.shape
    group = columns // HD
    tiles = rows // TFIRST
    return pl.pallas_call(
        functools.partial(first_kernel, rows, group, doc_lengths.shape[0]),
        out_shape=[
            jax.ShapeDtypeStruct((HD, group * rows), jnp.float32),
            jax.ShapeDtypeStruct((8, group * rows), jnp.float32),
            jax.ShapeDtypeStruct((group * rows, HD), jnp.bfloat16),
            jax.ShapeDtypeStruct((8, rows), jnp.int32),
            jax.ShapeDtypeStruct((8,), jnp.int32),
        ],
        in_specs=[SMEM, ANY, ANY, ANY],
        out_specs=[VMEM, VMEM, VMEM, VMEM, SMEM],
        scratch_shapes=[
            pltpu.VMEM(queries.shape, jnp.bfloat16),
            pltpu.VMEM(keys.shape, jnp.bfloat16),
            pltpu.VMEM(values.shape, jnp.bfloat16),
            pltpu.VMEM((HD, rows), jnp.bfloat16),
            pltpu.VMEM((TFIRST * tiles * (tiles + 1) // 2, TFIRST), jnp.float32),
            pltpu.SemaphoreType.DMA((3,)),
        ],
        compiler_params=params(),
        cost_estimate=cost(rows, rows, columns),
        name="attend_first",
    )(doc_lengths, queries, keys, values)


def attend_middle(distance, bounds, start_rows, stack, keys, values, state):
    rows = keys.shape[0]
    group = stack.shape[0] // rows
    return pl.pallas_call(
        functools.partial(middle_kernel, distance, rows, group),
        out_shape=[jax.ShapeDtypeStruct(s.shape, s.dtype) for s in state],
        in_specs=[SMEM] + [VMEM] * 6,
        out_specs=[VMEM, VMEM],
        scratch_shapes=[pltpu.VMEM((HD, rows), jnp.bfloat16)] + [pltpu.VMEM((rows, TQ), jnp.float32)] * 2,
        input_output_aliases={5: 0, 6: 1},
        compiler_params=params(),
        cost_estimate=cost(rows, rows, group * HD),
        name=f"attend_{distance}",
    )(bounds, start_rows, stack, keys, values, *state)


def attend_last(half, bounds, start_rows, stack, keys, values, far, state):
    rows = keys.shape[0]
    size = rows // 2
    group = stack.shape[0] // rows
    return pl.pallas_call(
        functools.partial(last_kernel, half, rows, group),
        out_shape=[jax.ShapeDtypeStruct((size // 2, group * HD), jnp.bfloat16)] * 2,
        in_specs=[SMEM] + [VMEM] * (6 + len(far)),
        out_specs=[VMEM, VMEM],
        scratch_shapes=[
            pltpu.VMEM((HD, group * size), jnp.float32),
            pltpu.VMEM((8, group * size), jnp.float32),
            pltpu.VMEM((HD, rows), jnp.bfloat16),
        ]
        + [pltpu.VMEM((rows, size), jnp.float32)] * 2,
        compiler_params=params(),
        cost_estimate=cost(size, rows, group * HD),
        name=f"attend_last_{half}",
    )(bounds, start_rows, stack, keys, values, *far, *state)


def near_kernel(pieces, *refs):
    blocks, weight_refs, out_ref = refs[: 3 * pieces], refs[3 * pieces : -1], refs[-1]
    size = blocks[0].shape[0]
    weight = jnp.concatenate([w[...] for w in weight_refs], axis=0)
    for i in range(pieces):
        block = jnp.concatenate([b[...] for b in blocks[i::pieces]], axis=1)
        out_ref[i * size : (i + 1) * size, :] = jnp.dot(block, weight, preferred_element_type=jnp.float32)


def project_near(blocks, weights):
    pieces = len(blocks) // 3
    size, columns = blocks[0].shape
    wide = weights[0].shape[1]
    return pl.pallas_call(
        functools.partial(near_kernel, pieces),
        out_shape=jax.ShapeDtypeStruct((pieces * size, wide), jnp.float32),
        in_specs=[VMEM] * (len(blocks) + 3),
        out_specs=VMEM,
        compiler_params=params(),
        cost_estimate=pl.CostEstimate(
            flops=6 * pieces * size * columns * wide, bytes_accessed=8 * pieces * size * wide, transcendentals=0
        ),
        name="project_near",
    )(*blocks, *weights)


def far_kernel(pieces, *refs):
    blocks, (weight_ref, near_ref, kept_ref, given_ref) = refs[:pieces], refs[pieces:]
    size = blocks[0].shape[0]
    columns = kept_ref.shape[1]
    for i in range(pieces):
        part = slice(i * size, (i + 1) * size)
        total = near_ref[part, :] + jnp.dot(blocks[i][...], weight_ref[...], preferred_element_type=jnp.float32)
        kept_ref[part, :] = total[:, :columns]
        given_ref[part, :] = total[:, columns:].astype(jnp.bfloat16)


def project_far(blocks, weight, near):
    rows, wide = near.shape
    columns = wide // 2
    return pl.pallas_call(
        functools.partial(far_kernel, len(blocks)),
        out_shape=[jax.ShapeDtypeStruct((rows, columns), t) for t in (jnp.float32, jnp.bfloat16)],
        in_specs=[VMEM] * (len(blocks) + 2),
        out_specs=[VMEM, VMEM],
        compiler_params=params(),
        cost_estimate=pl.CostEstimate(
            flops=2 * rows * wide * blocks[0].shape[1], bytes_accessed=8 * rows * wide, transcendentals=0
        ),
        name="project_far",
    )(*blocks, weight, near)


def join_kernel(*refs):
    out_ref = refs[-1]
    size = refs[0].shape[0]
    for i in range(len(refs) // 2):
        kept, taken = refs[2 * i], refs[2 * i + 1]
        out_ref[i * size : (i + 1) * size, :] = (kept[...] + taken[...].astype(jnp.float32)).astype(jnp.bfloat16)


def join(*halves):
    size, columns = halves[0].shape
    return pl.pallas_call(
        join_kernel,
        out_shape=jax.ShapeDtypeStruct((size * len(halves) // 2, columns), jnp.bfloat16),
        in_specs=[VMEM] * len(halves),
        out_specs=VMEM,
        compiler_params=params(),
        name="join",
    )(*halves)


def after(value, *others):
    return lax.optimization_barrier((value, others))[0]


def body(queries, keys, values, out_weight, doc_lengths):
    rows, columns = queries.shape
    seq_size = lax.axis_size("seq")
    head_size = lax.axis_size("head")
    chips = head_size // 2
    half = rows // 2
    chip = lax.axis_index("head") // 2
    core = lax.axis_index("head") % 2

    def next_block(block):
        return lax.ppermute(block, "seq", [(i, (i + 1) % seq_size) for i in range(seq_size)])

    def back(block, distance):
        return lax.ppermute(block, "seq", [(i, i - i % ROW + (i - distance) % ROW) for i in range(seq_size)])

    def four_on(block):
        owners = [i - i % ROW + (i + 3) % ROW for i in range(seq_size)]
        return lax.ppermute(block, "seq", [(i, (owner + 4) % seq_size) for i, owner in enumerate(owners)])

    def chip_shift(block, distance):
        route = [(i, (i + 2 * distance) % head_size) for i in range(head_size)]
        return lax.ppermute(block, "head", route)

    def swap(block):
        return lax.ppermute(block, "head", [(i, i ^ 1) for i in range(head_size)])

    def weight_columns(source, target):
        return jnp.concatenate(
            [lax.dynamic_slice_in_dim(source, (2 * target + c) * columns, columns, 1) for c in (core, 1 - core)], axis=1
        )

    k1, v1 = next_block(keys), next_block(values)
    far = back(jnp.concatenate([keys[half:], values[half:]], axis=1), 1)
    *state, stack, start_rows, bounds = attend_first(doc_lengths, queries, keys, values)
    k2, v2 = next_block(after(k1, state[1])), next_block(after(v1, state[1]))
    far = after(far, state[1])
    source = after(out_weight, state[1], k1, v1, far)
    far = back(far, 2)
    weights = {0: weight_columns(source, chip)}
    for d in (1, 3):
        weights[d] = chip_shift(weight_columns(source, (chip + d) % chips), d)
    state = attend_middle(1, bounds, start_rows, stack, k1, v1, state)
    k3, v3 = next_block(after(k2, state[1])), next_block(after(v2, state[1]))
    far = four_on(after(far, state[1]))
    state = attend_middle(2, bounds, start_rows, stack, k2, v2, state)
    k4, v4 = next_block(after(k3, state[1])[:half]), next_block(after(v3, state[1])[:half])
    weights[2] = chip_shift(weight_columns(after(out_weight, state[1]), (chip + 2) % chips), 2)
    bounds = after(bounds, weights[1], weights[3])
    late = attend_last(1, bounds, start_rows, stack, k3, v3, (far,), state)

    def sides(pieces):
        return [chip_shift(p, d) for d in (1, -1) for p in reversed(pieces)]

    def ordered(received):
        return received[1], received[0], received[3], received[2]

    late_before0, late_before1, late_after0, late_after1 = ordered(sides(late))
    bounds = after(bounds, late_before1)
    early = attend_last(0, bounds, start_rows, stack, k3, v3, (far, k4, v4), state)
    early_before0, early_before1, early_after0, early_after1 = ordered(sides(early))
    near_weights = (weights[0], weights[1], weights[3])
    late_far = chip_shift(late_before0, 1), chip_shift(late_after1, -1)
    late_near = project_near((*late, late_before0, late_before1, late_after0, late_after1), near_weights)
    early_far = chip_shift(early_before0, 1), chip_shift(early_after1, -1)
    early_near = project_near((*early, early_before0, early_before1, early_after0, early_after1), near_weights)
    late_kept, late_given = project_far(late_far, weights[2], late_near)
    late_taken = swap(late_given)
    early_kept, early_given = project_far(early_far, weights[2], early_near)
    early_taken = swap(early_given)
    return join(early_kept, early_taken, late_kept, late_taken)


def solution(mesh):
    return jax.shard_map(
        body,
        mesh=mesh,
        in_specs=(P("seq", "head"), P("seq", "head"), P("seq", "head"), P("head", None), P()),
        out_specs=P("seq", "head"),
        check_vma=False,
    )
```

```python
import functools

import jax
import jax.numpy as jnp
from jax import lax
from jax.experimental import pallas as pl
from jax.experimental.pallas import tpu as pltpu
from jax.sharding import PartitionSpec as P

HD = 128
ROW = 8
TFIRST = 256
TQ = 512
TK = 512
LOG2E = 1.4426950408889634
SCALE = LOG2E / HD**0.5
MASKED = -1e30
LOWEST = -1e29
VMEM = pl.BlockSpec(memory_space=pltpu.VMEM)
SMEM = pl.BlockSpec(memory_space=pltpu.SMEM)
ANY = pl.BlockSpec(memory_space=pl.ANY)
NT = (((1,), (1,)), ((), ()))


def put_scores(score_ref, row, query, key_ref, k0, count):
    for j in range(0, count, TK):
        n = min(TK, count - j)
        score_ref[row + j : row + j + n, :] = lax.dot_general(
            key_ref[k0 + j : k0 + j + n, :], query, NT, preferred_element_type=jnp.float32
        )


def add_keys(score_ref, row, count, turned_ref, v0, old_max, old_sum, old_acc, start_row=None, q0=None):
    size = score_ref.shape[1]

    def piece(j, n):
        scores = score_ref[row + j : row + j + n, :]
        if start_row is None:
            return scores
        key_pos = j + lax.broadcasted_iota(jnp.int32, (n, size), 0)
        visible = key_pos >= start_row
        if q0 is not None and j + n > q0 + 1:
            visible = visible & (key_pos <= q0 + lax.broadcasted_iota(jnp.int32, (n, size), 1))
        return jnp.where(visible, scores, MASKED)

    pieces = [(j, min(TK, count - j)) for j in range(0, count, TK)]
    new_max = old_max
    for j, n in pieces:
        new_max = jnp.maximum(new_max, jnp.max(piece(j, n), axis=0, keepdims=True))
    rescale = jnp.exp2((old_max - new_max) * SCALE)
    total = old_sum * rescale
    acc = old_acc * rescale
    for j, n in pieces:
        probs = jnp.exp2((piece(j, n) - new_max) * SCALE)
        total = total + jnp.sum(probs, axis=0, keepdims=True)
        acc = acc + jnp.dot(
            turned_ref[:, v0 + j : v0 + j + n], probs.astype(jnp.bfloat16), preferred_element_type=jnp.float32
        )
    return new_max, total, acc


def sweep(steps, first, key_ref, k0, count, turned_ref, v0, state, q_ref, score_refs, start_row):
    acc_ref, stat_ref = state

    def make(i):
        q_at, _ = first(i)
        put_scores(score_refs[i % 2], 0, q_ref[pl.ds(q_at, TQ), :], key_ref, k0, count)

    def use(i):
        columns = pl.ds(first(i)[1], TQ)
        start = None if start_row is None else start_row(i)
        stat_ref[0:1, columns], stat_ref[1:2, columns], acc_ref[:, columns] = add_keys(
            score_refs[i % 2], 0, count, turned_ref, v0, stat_ref[0:1, columns], stat_ref[1:2, columns],
            acc_ref[:, columns], start,
        )

    make(0)
    for i in range(steps):
        if i + 1 < steps:
            make(i + 1)
        use(i)


def first_kernel(
    rows, group, docs, length_ref, q_hbm, k_hbm, v_hbm,
    acc_ref, stat_ref, stack_ref, start_ref, bound_ref,
    q_ref, k_ref, v_ref, vt_ref, score_ref, sem,
):
    copies = [
        pltpu.make_async_copy(source, target, sem.at[i])
        for i, (source, target) in enumerate(((q_hbm, q_ref), (k_hbm, k_ref), (v_hbm, v_ref)))
    ]
    for copy in copies:
        copy.start()
    first_row = lax.axis_index("seq") * rows
    tiles = range(0, rows, TFIRST)
    marks = [first_row, first_row + rows // 2, first_row + rows - 1]
    positions = first_row + lax.broadcasted_iota(jnp.int32, (1, rows), 1)

    def document(d, carried):
        begin, row_starts, found = carried
        row_starts = jnp.where(positions >= begin, begin, row_starts)
        found = [jnp.where(mark >= begin, begin, old) for mark, old in zip(marks, found)]
        return begin + length_ref[d], row_starts, found

    zero = jnp.int32(0)
    _, row_starts, found = lax.fori_loop(
        0, docs, document, (zero, jnp.zeros((1, rows), jnp.int32), [zero for _ in marks])
    )
    start_ref[0:1, :] = row_starts
    start_ref[1:8, :] = jnp.zeros((7, rows), jnp.int32)
    bound_ref[0] = first_row
    for i, value in enumerate(found):
        bound_ref[1 + i] = value
    for i in range(len(found) + 1, 8):
        bound_ref[i] = zero
    for copy in copies:
        copy.wait()
    vt_ref[...] = v_ref[...].T
    for h in range(group):
        stack_ref[h * rows : (h + 1) * rows, :] = q_ref[:, h * HD : (h + 1) * HD]
    stat_ref[...] = jnp.zeros_like(stat_ref)
    offsets = {}
    used = 0
    for q0 in tiles:
        offsets[q0] = used
        used += q0 + TFIRST

    def head(h, carried):
        base = pl.multiple_of(h * rows, rows)

        def make(q0):
            put_scores(score_ref, offsets[q0], stack_ref[pl.ds(base + q0, TFIRST), :], k_ref, 0, q0 + TFIRST)

        def use(q0):
            columns = pl.ds(base + q0, TFIRST)
            start = start_ref[0:1, q0 : q0 + TFIRST] - first_row
            lowest = jnp.full((1, TFIRST), LOWEST, jnp.float32)
            none = jnp.zeros((1, TFIRST), jnp.float32)
            stat_ref[0:1, columns], stat_ref[1:2, columns], acc_ref[:, columns] = add_keys(
                score_ref, offsets[q0], q0 + TFIRST, vt_ref, 0, lowest, none, jnp.zeros((HD, TFIRST), jnp.float32), start, q0
            )

        order = list(reversed(tiles))
        make(order[0])
        for i, q0 in enumerate(order):
            if i + 1 < len(order):
                make(order[i + 1])
            use(q0)
        return carried

    lax.fori_loop(0, group, head, 0)


def middle_kernel(
    distance, rows, group, bound_ref, start_ref, q_ref, k_ref, v_ref, acc_in, stat_in, acc_ref, stat_ref, vt_ref, *score_refs
):
    acc_ref[...] = acc_in[...]
    stat_ref[...] = stat_in[...]
    first_key = bound_ref[0] - distance * rows
    needed = (bound_ref[1] < first_key + rows) & (first_key >= 0)
    inside = bound_ref[3] > first_key
    tiles = rows // TQ

    def work(masked):
        vt_ref[...] = v_ref[...].T

        def head(h, carried):
            def first(i):
                return (pl.multiple_of(h * rows + i * TQ, TQ),) * 2

            def start_row(i):
                return start_ref[0:1, i * TQ : (i + 1) * TQ] - first_key

            sweep(
                tiles, first, k_ref, 0, rows, vt_ref, 0, (acc_ref, stat_ref), q_ref, score_refs, start_row if masked else None
            )
            return carried

        lax.fori_loop(0, group, head, 0)

    pl.when(needed & jnp.logical_not(inside))(lambda: work(False))
    pl.when(needed & inside)(lambda: work(True))


def last_kernel(half, rows, group, bound_ref, start_ref, q_ref, k_ref, v_ref, *refs):
    far_count = 1 if half else 3
    far_refs = refs[:far_count]
    acc_in, stat_in, out0_ref, out1_ref, acc_ref, stat_ref, vt_ref, *score_refs = refs[far_count:]
    size = rows // 2
    base = half * size
    for h in range(group):
        acc_ref[:, h * size : (h + 1) * size] = acc_in[:, h * rows + base : h * rows + base + size]
        stat_ref[:, h * size : (h + 1) * size] = stat_in[:, h * rows + base : h * rows + base + size]

    def block(key_ref, v_block, key_from, key_count, first_key, masked):
        vt_ref[:, :key_count] = v_block().T

        def first(i):
            return i * rows + base, i * size

        def start_row(i):
            return start_ref[0:1, base : base + size] - first_key

        sweep(
            group, first, key_ref, key_from, key_count, vt_ref, 0, (acc_ref, stat_ref), q_ref, score_refs,
            start_row if masked else None,
        )

    near_key = bound_ref[0] - 3 * rows
    lowest = bound_ref[1 + half]
    needed = (lowest < near_key + rows) & (near_key >= 0)
    inside = bound_ref[3] > near_key
    pl.when(needed & jnp.logical_not(inside))(lambda: block(k_ref, lambda: v_ref[...], 0, rows, near_key, False))
    pl.when(needed & inside)(lambda: block(k_ref, lambda: v_ref[...], 0, rows, near_key, True))

    far_key = near_key - rows
    late_ref = far_refs[0]
    pl.when((lowest < far_key + rows) & (far_key >= 0))(
        lambda: block(late_ref.at[:, :HD], lambda: late_ref[:, HD:], 0, size, far_key + size, True)
    )
    if not half:
        pl.when((lowest < far_key + size) & (far_key >= 0))(
            lambda: block(far_refs[1], lambda: far_refs[2][...], 0, size, far_key, True)
        )

    piece = size // 2
    for h in range(group):
        for i, out_ref in enumerate((out0_ref, out1_ref)):
            columns = slice(h * size + i * piece, h * size + (i + 1) * piece)
            scaled = acc_ref[:, columns] / stat_ref[1:2, columns]
            out_ref[:, h * HD : (h + 1) * HD] = scaled.T.astype(jnp.bfloat16)


def cost(rows, keys, columns):
    return pl.CostEstimate(flops=4 * rows * keys * columns, bytes_accessed=6 * rows * columns, transcendentals=rows * keys * 3)


def params():
    return pltpu.CompilerParams(vmem_limit_bytes=32 * 2**20)


def attend_first(doc_lengths, queries, keys, values):
    rows, columns = queries.shape
    group = columns // HD
    tiles = rows // TFIRST
    return pl.pallas_call(
        functools.partial(first_kernel, rows, group, doc_lengths.shape[0]),
        out_shape=[
            jax.ShapeDtypeStruct((HD, group * rows), jnp.float32),
            jax.ShapeDtypeStruct((8, group * rows), jnp.float32),
            jax.ShapeDtypeStruct((group * rows, HD), jnp.bfloat16),
            jax.ShapeDtypeStruct((8, rows), jnp.int32),
            jax.ShapeDtypeStruct((8,), jnp.int32),
        ],
        in_specs=[SMEM, ANY, ANY, ANY],
        out_specs=[VMEM, VMEM, VMEM, VMEM, SMEM],
        scratch_shapes=[
            pltpu.VMEM(queries.shape, jnp.bfloat16),
            pltpu.VMEM(keys.shape, jnp.bfloat16),
            pltpu.VMEM(values.shape, jnp.bfloat16),
            pltpu.VMEM((HD, rows), jnp.bfloat16),
            pltpu.VMEM((TFIRST * tiles * (tiles + 1) // 2, TFIRST), jnp.float32),
            pltpu.SemaphoreType.DMA((3,)),
        ],
        compiler_params=params(),
        cost_estimate=cost(rows, rows, columns),
        name="attend_first",
    )(doc_lengths, queries, keys, values)


def attend_middle(distance, bounds, start_rows, stack, keys, values, state):
    rows = keys.shape[0]
    group = stack.shape[0] // rows
    return pl.pallas_call(
        functools.partial(middle_kernel, distance, rows, group),
        out_shape=[jax.ShapeDtypeStruct(s.shape, s.dtype) for s in state],
        in_specs=[SMEM] + [VMEM] * 6,
        out_specs=[VMEM, VMEM],
        scratch_shapes=[pltpu.VMEM((HD, rows), jnp.bfloat16)] + [pltpu.VMEM((rows, TQ), jnp.float32)] * 2,
        input_output_aliases={5: 0, 6: 1},
        compiler_params=params(),
        cost_estimate=cost(rows, rows, group * HD),
        name=f"attend_{distance}",
    )(bounds, start_rows, stack, keys, values, *state)


def attend_last(half, bounds, start_rows, stack, keys, values, far, state):
    rows = keys.shape[0]
    size = rows // 2
    group = stack.shape[0] // rows
    return pl.pallas_call(
        functools.partial(last_kernel, half, rows, group),
        out_shape=[jax.ShapeDtypeStruct((size // 2, group * HD), jnp.bfloat16)] * 2,
        in_specs=[SMEM] + [VMEM] * (6 + len(far)),
        out_specs=[VMEM, VMEM],
        scratch_shapes=[
            pltpu.VMEM((HD, group * size), jnp.float32),
            pltpu.VMEM((8, group * size), jnp.float32),
            pltpu.VMEM((HD, rows), jnp.bfloat16),
        ]
        + [pltpu.VMEM((rows, size), jnp.float32)] * 2,
        compiler_params=params(),
        cost_estimate=cost(size, rows, group * HD),
        name=f"attend_last_{half}",
    )(bounds, start_rows, stack, keys, values, *far, *state)


def near_kernel(pieces, *refs):
    blocks, weight_refs, out_ref = refs[: 3 * pieces], refs[3 * pieces : -1], refs[-1]
    size = blocks[0].shape[0]
    weight = jnp.concatenate([w[...] for w in weight_refs], axis=0)
    for i in range(pieces):
        block = jnp.concatenate([b[...] for b in blocks[i::pieces]], axis=1)
        out_ref[i * size : (i + 1) * size, :] = jnp.dot(block, weight, preferred_element_type=jnp.float32)


def project_near(blocks, weights):
    pieces = len(blocks) // 3
    size, columns = blocks[0].shape
    wide = weights[0].shape[1]
    return pl.pallas_call(
        functools.partial(near_kernel, pieces),
        out_shape=jax.ShapeDtypeStruct((pieces * size, wide), jnp.float32),
        in_specs=[VMEM] * (len(blocks) + 3),
        out_specs=VMEM,
        compiler_params=params(),
        cost_estimate=pl.CostEstimate(
            flops=6 * pieces * size * columns * wide, bytes_accessed=8 * pieces * size * wide, transcendentals=0
        ),
        name="project_near",
    )(*blocks, *weights)


def far_kernel(pieces, *refs):
    blocks, (weight_ref, near_ref, kept_ref, given_ref) = refs[:pieces], refs[pieces:]
    size = blocks[0].shape[0]
    columns = kept_ref.shape[1]
    for i in range(pieces):
        part = slice(i * size, (i + 1) * size)
        total = near_ref[part, :] + jnp.dot(blocks[i][...], weight_ref[...], preferred_element_type=jnp.float32)
        kept_ref[part, :] = total[:, :columns]
        given_ref[part, :] = total[:, columns:].astype(jnp.bfloat16)


def project_far(blocks, weight, near):
    rows, wide = near.shape
    columns = wide // 2
    return pl.pallas_call(
        functools.partial(far_kernel, len(blocks)),
        out_shape=[jax.ShapeDtypeStruct((rows, columns), t) for t in (jnp.float32, jnp.bfloat16)],
        in_specs=[VMEM] * (len(blocks) + 2),
        out_specs=[VMEM, VMEM],
        compiler_params=params(),
        cost_estimate=pl.CostEstimate(
            flops=2 * rows * wide * blocks[0].shape[1], bytes_accessed=8 * rows * wide, transcendentals=0
        ),
        name="project_far",
    )(*blocks, weight, near)


def join_kernel(*refs):
    out_ref = refs[-1]
    size = refs[0].shape[0]
    for i in range(len(refs) // 2):
        kept, taken = refs[2 * i], refs[2 * i + 1]
        out_ref[i * size : (i + 1) * size, :] = (kept[...] + taken[...].astype(jnp.float32)).astype(jnp.bfloat16)


def join(*halves):
    size, columns = halves[0].shape
    return pl.pallas_call(
        join_kernel,
        out_shape=jax.ShapeDtypeStruct((size * len(halves) // 2, columns), jnp.bfloat16),
        in_specs=[VMEM] * len(halves),
        out_specs=VMEM,
        compiler_params=params(),
        name="join",
    )(*halves)


def after(value, *others):
    return lax.optimization_barrier((value, others))[0]


def body(queries, keys, values, out_weight, doc_lengths):
    rows, columns = queries.shape
    seq_size = lax.axis_size("seq")
    head_size = lax.axis_size("head")
    chips = head_size // 2
    half = rows // 2
    chip = lax.axis_index("head") // 2
    core = lax.axis_index("head") % 2

    def next_block(block):
        return lax.ppermute(block, "seq", [(i, (i + 1) % seq_size) for i in range(seq_size)])

    def back(block, distance):
        return lax.ppermute(block, "seq", [(i, i - i % ROW + (i - distance) % ROW) for i in range(seq_size)])

    def four_on(block):
        owners = [i - i % ROW + (i + 3) % ROW for i in range(seq_size)]
        return lax.ppermute(block, "seq", [(i, (owner + 4) % seq_size) for i, owner in enumerate(owners)])

    def chip_shift(block, distance):
        route = [(i, (i + 2 * distance) % head_size) for i in range(head_size)]
        return lax.ppermute(block, "head", route)

    def swap(block):
        return lax.ppermute(block, "head", [(i, i ^ 1) for i in range(head_size)])

    def weight_columns(source, target):
        return jnp.concatenate(
            [lax.dynamic_slice_in_dim(source, (2 * target + c) * columns, columns, 1) for c in (core, 1 - core)], axis=1
        )

    k1, v1 = next_block(keys), next_block(values)
    far = back(jnp.concatenate([keys[half:], values[half:]], axis=1), 1)
    weights = {d: chip_shift(weight_columns(out_weight, (chip + d) % chips), d) for d in (1, 3)}
    *state, stack, start_rows, bounds = attend_first(doc_lengths, queries, keys, values)
    k2, v2 = next_block(after(k1, state[1])), next_block(after(v1, state[1]))
    far = back(after(far, state[1]), 2)
    source = after(out_weight, state[1], weights[1], weights[3])
    weights[2] = chip_shift(weight_columns(source, (chip + 2) % chips), 2)
    bounds = after(bounds, weights[1], weights[3])
    state = attend_middle(1, bounds, start_rows, stack, k1, v1, state)
    k3, v3 = next_block(after(k2, state[1])), next_block(after(v2, state[1]))
    far = four_on(after(far, state[1]))
    bounds = after(bounds, weights[2])
    state = attend_middle(2, bounds, start_rows, stack, k2, v2, state)
    k4, v4 = next_block(after(k3, state[1])[:half]), next_block(after(v3, state[1])[:half])
    weights[0] = weight_columns(after(out_weight, state[1]), chip)
    late = attend_last(1, bounds, start_rows, stack, k3, v3, (far,), state)

    def sides(pieces):
        return [chip_shift(p, d) for d in (1, -1) for p in reversed(pieces)]

    def ordered(received):
        return received[1], received[0], received[3], received[2]

    late_before0, late_before1, late_after0, late_after1 = ordered(sides(late))
    bounds = after(bounds, late_before1)
    early = attend_last(0, bounds, start_rows, stack, k3, v3, (far, k4, v4), state)
    early_before0, early_before1, early_after0, early_after1 = ordered(sides(early))
    near_weights = (weights[0], weights[1], weights[3])
    late_far = chip_shift(late_before0, 1), chip_shift(late_after1, -1)
    late_near = project_near((*late, late_before0, late_before1, late_after0, late_after1), near_weights)
    early_far = chip_shift(early_before0, 1), chip_shift(early_after1, -1)
    early_near = project_near((*early, early_before0, early_before1, early_after0, early_after1), near_weights)
    late_kept, late_given = project_far(late_far, weights[2], late_near)
    late_taken = swap(late_given)
    early_kept, early_given = project_far(early_far, weights[2], early_near)
    early_taken = swap(early_given)
    return join(early_kept, early_taken, late_kept, late_taken)


def solution(mesh):
    return jax.shard_map(
        body,
        mesh=mesh,
        in_specs=(P("seq", "head"), P("seq", "head"), P("seq", "head"), P("head", None), P()),
        out_specs=P("seq", "head"),
        check_vma=False,
    )
```

```python
import functools

import jax
import jax.numpy as jnp
from jax import lax
from jax.experimental import pallas as pl
from jax.experimental.pallas import tpu as pltpu
from jax.sharding import PartitionSpec as P

HD = 128
ROW = 8
TFIRST = 256
TQ = 512
TK = 512
LOG2E = 1.4426950408889634
SCALE = LOG2E / HD**0.5
MASKED = -1e30
LOWEST = -1e29
VMEM = pl.BlockSpec(memory_space=pltpu.VMEM)
SMEM = pl.BlockSpec(memory_space=pltpu.SMEM)
HBM = pl.BlockSpec(memory_space=pltpu.HBM)
NT = (((1,), (1,)), ((), ()))


def put_scores(score_ref, row, query, key_ref, k0, count):
    for j in range(0, count, TK):
        n = min(TK, count - j)
        score_ref[row + j : row + j + n, :] = lax.dot_general(
            key_ref[k0 + j : k0 + j + n, :], query, NT, preferred_element_type=jnp.float32
        )


def add_keys(score_ref, row, count, turned_ref, v0, old_max, old_sum, old_acc, start_row=None, q0=None):
    size = score_ref.shape[1]

    def piece(j, n):
        scores = score_ref[row + j : row + j + n, :]
        if start_row is None:
            return scores
        key_pos = j + lax.broadcasted_iota(jnp.int32, (n, size), 0)
        visible = key_pos >= start_row
        if q0 is not None and j + n > q0 + 1:
            visible = visible & (key_pos <= q0 + lax.broadcasted_iota(jnp.int32, (n, size), 1))
        return jnp.where(visible, scores, MASKED)

    pieces = [(j, min(TK, count - j)) for j in range(0, count, TK)]
    new_max = old_max
    for j, n in pieces:
        new_max = jnp.maximum(new_max, jnp.max(piece(j, n), axis=0, keepdims=True))
    rescale = jnp.exp2((old_max - new_max) * SCALE)
    total = old_sum * rescale
    acc = old_acc * rescale
    for j, n in pieces:
        probs = jnp.exp2((piece(j, n) - new_max) * SCALE)
        total = total + jnp.sum(probs, axis=0, keepdims=True)
        acc = acc + jnp.dot(
            turned_ref[:, v0 + j : v0 + j + n], probs.astype(jnp.bfloat16), preferred_element_type=jnp.float32
        )
    return new_max, total, acc


def sweep(steps, first, key_ref, k0, count, turned_ref, v0, state, q_ref, score_refs, start_row):
    acc_ref, stat_ref = state

    def make(i):
        q_at, _ = first(i)
        put_scores(score_refs[i % 2], 0, q_ref[pl.ds(q_at, TQ), :], key_ref, k0, count)

    def use(i):
        columns = pl.ds(first(i)[1], TQ)
        start = None if start_row is None else start_row(i)
        stat_ref[0:1, columns], stat_ref[1:2, columns], acc_ref[:, columns] = add_keys(
            score_refs[i % 2], 0, count, turned_ref, v0, stat_ref[0:1, columns], stat_ref[1:2, columns],
            acc_ref[:, columns], start,
        )

    make(0)
    for i in range(steps):
        if i + 1 < steps:
            make(i + 1)
        use(i)


def first_kernel(
    rows, group, docs, length_ref, q_hbm, k_hbm, v_hbm,
    acc_ref, stat_ref, stack_ref, start_ref, bound_ref,
    q_ref, k_ref, v_ref, vt_ref, score_ref, sem,
):
    copies = [
        pltpu.make_async_copy(source, target, sem.at[i])
        for i, (source, target) in enumerate(((q_hbm, q_ref), (k_hbm, k_ref), (v_hbm, v_ref)))
    ]
    for copy in copies:
        copy.start()
    first_row = lax.axis_index("seq") * rows
    tiles = range(0, rows, TFIRST)
    marks = [first_row, first_row + rows // 2, first_row + rows - 1]
    positions = first_row + lax.broadcasted_iota(jnp.int32, (1, rows), 1)

    def document(d, carried):
        begin, row_starts, found = carried
        row_starts = jnp.where(positions >= begin, begin, row_starts)
        found = [jnp.where(mark >= begin, begin, old) for mark, old in zip(marks, found)]
        return begin + length_ref[d], row_starts, found

    zero = jnp.int32(0)
    _, row_starts, found = lax.fori_loop(
        0, docs, document, (zero, jnp.zeros((1, rows), jnp.int32), [zero for _ in marks])
    )
    start_ref[0:1, :] = row_starts
    start_ref[1:8, :] = jnp.zeros((7, rows), jnp.int32)
    bound_ref[0] = first_row
    for i, value in enumerate(found):
        bound_ref[1 + i] = value
    for i in range(len(found) + 1, 8):
        bound_ref[i] = zero
    for copy in copies:
        copy.wait()
    vt_ref[...] = v_ref[...].T
    for h in range(group):
        stack_ref[h * rows : (h + 1) * rows, :] = q_ref[:, h * HD : (h + 1) * HD]
    stat_ref[...] = jnp.zeros_like(stat_ref)
    offsets = {}
    used = 0
    for q0 in tiles:
        offsets[q0] = used
        used += q0 + TFIRST

    def head(h, carried):
        base = pl.multiple_of(h * rows, rows)

        def make(q0):
            put_scores(score_ref, offsets[q0], stack_ref[pl.ds(base + q0, TFIRST), :], k_ref, 0, q0 + TFIRST)

        def use(q0):
            columns = pl.ds(base + q0, TFIRST)
            start = start_ref[0:1, q0 : q0 + TFIRST] - first_row
            lowest = jnp.full((1, TFIRST), LOWEST, jnp.float32)
            none = jnp.zeros((1, TFIRST), jnp.float32)
            stat_ref[0:1, columns], stat_ref[1:2, columns], acc_ref[:, columns] = add_keys(
                score_ref, offsets[q0], q0 + TFIRST, vt_ref, 0, lowest, none, jnp.zeros((HD, TFIRST), jnp.float32), start, q0
            )

        order = list(reversed(tiles))
        make(order[0])
        for i, q0 in enumerate(order):
            if i + 1 < len(order):
                make(order[i + 1])
            use(q0)
        return carried

    lax.fori_loop(0, group, head, 0)


def middle_kernel(
    distance, rows, group, bound_ref, start_ref, q_ref, k_ref, v_ref, acc_in, stat_in, acc_ref, stat_ref, vt_ref, *score_refs
):
    acc_ref[...] = acc_in[...]
    stat_ref[...] = stat_in[...]
    first_key = bound_ref[0] - distance * rows
    needed = (bound_ref[1] < first_key + rows) & (first_key >= 0)
    inside = bound_ref[3] > first_key
    tiles = rows // TQ

    def work(masked):
        vt_ref[...] = v_ref[...].T

        def head(h, carried):
            def first(i):
                return (pl.multiple_of(h * rows + i * TQ, TQ),) * 2

            def start_row(i):
                return start_ref[0:1, i * TQ : (i + 1) * TQ] - first_key

            sweep(
                tiles, first, k_ref, 0, rows, vt_ref, 0, (acc_ref, stat_ref), q_ref, score_refs, start_row if masked else None
            )
            return carried

        lax.fori_loop(0, group, head, 0)

    pl.when(needed & jnp.logical_not(inside))(lambda: work(False))
    pl.when(needed & inside)(lambda: work(True))


def last_kernel(half, rows, group, bound_ref, start_ref, q_ref, k_ref, v_ref, *refs):
    far_count = 1 if half else 3
    far_refs = refs[:far_count]
    acc_in, stat_in, out0_ref, out1_ref, acc_ref, stat_ref, vt_ref, *score_refs = refs[far_count:]
    size = rows // 2
    base = half * size
    for h in range(group):
        acc_ref[:, h * size : (h + 1) * size] = acc_in[:, h * rows + base : h * rows + base + size]
        stat_ref[:, h * size : (h + 1) * size] = stat_in[:, h * rows + base : h * rows + base + size]

    def block(key_ref, v_block, key_from, key_count, first_key, masked):
        vt_ref[:, :key_count] = v_block().T

        def first(i):
            return i * rows + base, i * size

        def start_row(i):
            return start_ref[0:1, base : base + size] - first_key

        sweep(
            group, first, key_ref, key_from, key_count, vt_ref, 0, (acc_ref, stat_ref), q_ref, score_refs,
            start_row if masked else None,
        )

    near_key = bound_ref[0] - 3 * rows
    lowest = bound_ref[1 + half]
    needed = (lowest < near_key + rows) & (near_key >= 0)
    inside = bound_ref[3] > near_key
    pl.when(needed & jnp.logical_not(inside))(lambda: block(k_ref, lambda: v_ref[...], 0, rows, near_key, False))
    pl.when(needed & inside)(lambda: block(k_ref, lambda: v_ref[...], 0, rows, near_key, True))

    far_key = near_key - rows
    late_ref = far_refs[0]
    pl.when((lowest < far_key + rows) & (far_key >= 0))(
        lambda: block(late_ref.at[:, :HD], lambda: late_ref[:, HD:], 0, size, far_key + size, True)
    )
    if not half:
        pl.when((lowest < far_key + size) & (far_key >= 0))(
            lambda: block(far_refs[1], lambda: far_refs[2][...], 0, size, far_key, True)
        )

    piece = size // 2
    for h in range(group):
        for i, out_ref in enumerate((out0_ref, out1_ref)):
            columns = slice(h * size + i * piece, h * size + (i + 1) * piece)
            scaled = acc_ref[:, columns] / stat_ref[1:2, columns]
            out_ref[:, h * HD : (h + 1) * HD] = scaled.T.astype(jnp.bfloat16)


def cost(rows, keys, columns):
    return pl.CostEstimate(flops=0, bytes_accessed=0, transcendentals=0)


def params():
    return pltpu.CompilerParams(vmem_limit_bytes=32 * 2**20)


def attend_first(doc_lengths, queries, keys, values):
    rows, columns = queries.shape
    group = columns // HD
    tiles = rows // TFIRST
    return pl.pallas_call(
        functools.partial(first_kernel, rows, group, doc_lengths.shape[0]),
        out_shape=[
            jax.ShapeDtypeStruct((HD, group * rows), jnp.float32),
            jax.ShapeDtypeStruct((8, group * rows), jnp.float32),
            jax.ShapeDtypeStruct((group * rows, HD), jnp.bfloat16),
            jax.ShapeDtypeStruct((8, rows), jnp.int32),
            jax.ShapeDtypeStruct((8,), jnp.int32),
        ],
        in_specs=[SMEM, HBM, HBM, HBM],
        out_specs=[VMEM, VMEM, VMEM, VMEM, SMEM],
        scratch_shapes=[
            pltpu.VMEM(queries.shape, jnp.bfloat16),
            pltpu.VMEM(keys.shape, jnp.bfloat16),
            pltpu.VMEM(values.shape, jnp.bfloat16),
            pltpu.VMEM((HD, rows), jnp.bfloat16),
            pltpu.VMEM((TFIRST * tiles * (tiles + 1) // 2, TFIRST), jnp.float32),
            pltpu.SemaphoreType.DMA((3,)),
        ],
        compiler_params=params(),
        cost_estimate=cost(rows, rows, columns),
        name="attend_first",
    )(doc_lengths, queries, keys, values)


def attend_middle(distance, bounds, start_rows, stack, keys, values, state):
    rows = keys.shape[0]
    group = stack.shape[0] // rows
    return pl.pallas_call(
        functools.partial(middle_kernel, distance, rows, group),
        out_shape=[jax.ShapeDtypeStruct(s.shape, s.dtype) for s in state],
        in_specs=[SMEM] + [VMEM] * 6,
        out_specs=[VMEM, VMEM],
        scratch_shapes=[pltpu.VMEM((HD, rows), jnp.bfloat16)] + [pltpu.VMEM((rows, TQ), jnp.float32)] * 2,
        input_output_aliases={5: 0, 6: 1},
        compiler_params=params(),
        cost_estimate=cost(rows, rows, group * HD),
        name=f"attend_{distance}",
    )(bounds, start_rows, stack, keys, values, *state)


def attend_last(half, bounds, start_rows, stack, keys, values, far, state):
    rows = keys.shape[0]
    size = rows // 2
    group = stack.shape[0] // rows
    return pl.pallas_call(
        functools.partial(last_kernel, half, rows, group),
        out_shape=[jax.ShapeDtypeStruct((size // 2, group * HD), jnp.bfloat16)] * 2,
        in_specs=[SMEM] + [VMEM] * (6 + len(far)),
        out_specs=[VMEM, VMEM],
        scratch_shapes=[
            pltpu.VMEM((HD, group * size), jnp.float32),
            pltpu.VMEM((8, group * size), jnp.float32),
            pltpu.VMEM((HD, rows), jnp.bfloat16),
        ]
        + [pltpu.VMEM((rows, size), jnp.float32)] * 2,
        compiler_params=params(),
        cost_estimate=cost(size, rows, group * HD),
        name=f"attend_last_{half}",
    )(bounds, start_rows, stack, keys, values, *far, *state)


def prelude_kernel(chips, weight_hbm, k_hbm, v_hbm, *refs):
    weight_refs, far_ref, sem = refs[:chips], refs[chips], refs[-1]
    wide = weight_refs[0].shape[1]
    half = far_ref.shape[0]
    chip = lax.axis_index("head") // 2
    copies = [
        pltpu.make_async_copy(k_hbm.at[pl.ds(half, half), :], far_ref.at[:, :HD], sem.at[chips]),
        pltpu.make_async_copy(v_hbm.at[pl.ds(half, half), :], far_ref.at[:, HD:], sem.at[chips + 1]),
    ]
    for d in (1, 3, 2, 0):
        column = pl.multiple_of(lax.rem(chip + d, chips) * wide, wide)
        copies.append(pltpu.make_async_copy(weight_hbm.at[:, pl.ds(column, wide)], weight_refs[d], sem.at[d]))
    for copy in copies:
        copy.start()
    for copy in copies:
        copy.wait()


def prelude(out_weight, keys, values, chips):
    rows, columns = out_weight.shape
    block = jax.ShapeDtypeStruct((rows, columns // chips), out_weight.dtype)
    far = jax.ShapeDtypeStruct((keys.shape[0] // 2, 2 * HD), keys.dtype)
    *weights, far = pl.pallas_call(
        functools.partial(prelude_kernel, chips),
        out_shape=[block] * chips + [far],
        in_specs=[HBM, HBM, HBM],
        out_specs=[VMEM] * (chips + 1),
        scratch_shapes=[pltpu.SemaphoreType.DMA((chips + 2,))],
        compiler_params=params(),
        name="prelude",
    )(out_weight, keys, values)
    return weights, far


def near_kernel(pieces, *refs):
    blocks, weight_refs, out_ref = refs[: 3 * pieces], refs[3 * pieces : -1], refs[-1]
    size = blocks[0].shape[0]
    weight = jnp.concatenate([w[...] for w in weight_refs], axis=0)
    for i in range(pieces):
        block = jnp.concatenate([b[...] for b in blocks[i::pieces]], axis=1)
        out_ref[i * size : (i + 1) * size, :] = jnp.dot(block, weight, preferred_element_type=jnp.float32)


def project_near(blocks, weights):
    pieces = len(blocks) // 3
    size, columns = blocks[0].shape
    wide = weights[0].shape[1]
    return pl.pallas_call(
        functools.partial(near_kernel, pieces),
        out_shape=jax.ShapeDtypeStruct((pieces * size, wide), jnp.float32),
        in_specs=[VMEM] * (len(blocks) + 3),
        out_specs=VMEM,
        compiler_params=params(),
        cost_estimate=pl.CostEstimate(
            flops=6 * pieces * size * columns * wide, bytes_accessed=8 * pieces * size * wide, transcendentals=0
        ),
        name="project_near",
    )(*blocks, *weights)


def far_kernel(pieces, *refs):
    blocks, (weight_ref, near_ref, kept_ref, given_ref) = refs[:pieces], refs[pieces:]
    size = blocks[0].shape[0]
    columns = kept_ref.shape[1]
    for i in range(pieces):
        part = slice(i * size, (i + 1) * size)
        total = near_ref[part, :] + jnp.dot(blocks[i][...], weight_ref[...], preferred_element_type=jnp.float32)

        def give(kept, given):
            kept_ref[part, :] = total[:, kept]
            given_ref[part, :] = total[:, given].astype(jnp.bfloat16)

        core = lax.axis_index("head") % 2
        low, high = slice(0, columns), slice(columns, None)
        pl.when(core == 0)(lambda: give(low, high))
        pl.when(core == 1)(lambda: give(high, low))


def project_far(blocks, weight, near):
    rows, wide = near.shape
    columns = wide // 2
    return pl.pallas_call(
        functools.partial(far_kernel, len(blocks)),
        out_shape=[jax.ShapeDtypeStruct((rows, columns), t) for t in (jnp.float32, jnp.bfloat16)],
        in_specs=[VMEM] * (len(blocks) + 2),
        out_specs=[VMEM, VMEM],
        compiler_params=params(),
        cost_estimate=pl.CostEstimate(
            flops=2 * rows * wide * blocks[0].shape[1], bytes_accessed=8 * rows * wide, transcendentals=0
        ),
        name="project_far",
    )(*blocks, weight, near)


def join_kernel(*refs):
    out_ref = refs[-1]
    size = refs[0].shape[0]
    for i in range(len(refs) // 2):
        kept, taken = refs[2 * i], refs[2 * i + 1]
        out_ref[i * size : (i + 1) * size, :] = (kept[...] + taken[...].astype(jnp.float32)).astype(jnp.bfloat16)


def join(*halves):
    size, columns = halves[0].shape
    return pl.pallas_call(
        join_kernel,
        out_shape=jax.ShapeDtypeStruct((size * len(halves) // 2, columns), jnp.bfloat16),
        in_specs=[VMEM] * len(halves),
        out_specs=VMEM,
        compiler_params=params(),
        name="join",
    )(*halves)


def after(value, *others):
    return lax.optimization_barrier((value, others))[0]


def body(queries, keys, values, out_weight, doc_lengths):
    rows, columns = queries.shape
    seq_size = lax.axis_size("seq")
    head_size = lax.axis_size("head")
    chips = head_size // 2
    half = rows // 2
    def next_block(block):
        return lax.ppermute(block, "seq", [(i, (i + 1) % seq_size) for i in range(seq_size)])

    def back(block, distance):
        return lax.ppermute(block, "seq", [(i, i - i % ROW + (i - distance) % ROW) for i in range(seq_size)])

    def four_on(block):
        owners = [i - i % ROW + (i + 3) % ROW for i in range(seq_size)]
        return lax.ppermute(block, "seq", [(i, (owner + 4) % seq_size) for i, owner in enumerate(owners)])

    def chip_shift(block, distance):
        route = [(i, (i + 2 * distance) % head_size) for i in range(head_size)]
        return lax.ppermute(block, "head", route)

    def swap(block):
        return lax.ppermute(block, "head", [(i, i ^ 1) for i in range(head_size)])

    k1, v1 = next_block(keys), next_block(values)
    blocks, far = prelude(out_weight, keys, values, chips)
    far = back(far, 1)
    weights = {0: blocks[0], 1: chip_shift(blocks[1], 1), 3: chip_shift(blocks[3], 3)}
    *state, stack, start_rows, bounds = attend_first(doc_lengths, queries, keys, values)
    k2, v2 = next_block(after(k1, state[1])), next_block(after(v1, state[1]))
    far = back(after(far, state[1]), 2)
    state = attend_middle(1, bounds, start_rows, stack, k1, v1, state)
    k3, v3 = next_block(after(k2, state[1])), next_block(after(v2, state[1]))
    far = four_on(after(far, state[1]))
    weights[2] = chip_shift(after(blocks[2], state[1], weights[1]), 2)
    bounds = after(bounds, weights[1], weights[3])
    state = attend_middle(2, bounds, start_rows, stack, k2, v2, state)
    k4, v4 = next_block(after(k3, state[1])[:half]), next_block(after(v3, state[1])[:half])
    late = attend_last(1, bounds, start_rows, stack, k3, v3, (far,), state)

    def sides(pieces):
        return [chip_shift(p, d) for d in (1, -1) for p in reversed(pieces)]

    def ordered(received):
        return received[1], received[0], received[3], received[2]

    late_before0, late_before1, late_after0, late_after1 = ordered(sides((after(late[0], k4, v4), late[1])))
    bounds = after(bounds, late_before1, weights[2])
    early = attend_last(0, bounds, start_rows, stack, k3, v3, (far, k4, v4), state)
    early_before0, early_before1, early_after0, early_after1 = ordered(sides(early))
    near_weights = (weights[0], weights[1], weights[3])
    late_far = chip_shift(late_before0, 1), chip_shift(late_after1, -1)
    late_near = project_near((*late, late_before0, late_before1, late_after0, late_after1), near_weights)
    early_far = chip_shift(early_before0, 1), chip_shift(early_after1, -1)
    early_near = project_near((*early, early_before0, early_before1, early_after0, early_after1), near_weights)
    late_kept, late_given = project_far(late_far, weights[2], late_near)
    late_taken = swap(late_given)
    early_kept, early_given = project_far(early_far, weights[2], early_near)
    early_taken = swap(early_given)
    return join(early_kept, early_taken, late_kept, late_taken)


def solution(mesh):
    return jax.shard_map(
        body,
        mesh=mesh,
        in_specs=(P("seq", "head"), P("seq", "head"), P("seq", "head"), P("head", None), P()),
        out_specs=P("seq", "head"),
        check_vma=False,
    )
```

```python
import functools

import jax
import jax.numpy as jnp
from jax import lax
from jax.experimental import pallas as pl
from jax.experimental.pallas import tpu as pltpu
from jax.sharding import PartitionSpec as P

HD = 128
ROW = 8
TFIRST = 256
TQ = 512
TK = 512
SPLIT = 384
LATE_TILES = (384, 256)
EARLY_TILES = (384,)
LOG2E = 1.4426950408889634
SCALE = LOG2E / HD**0.5
MASKED = -1e30
LOWEST = -1e29
VMEM = pl.BlockSpec(memory_space=pltpu.VMEM)
SMEM = pl.BlockSpec(memory_space=pltpu.SMEM)
HBM = pl.BlockSpec(memory_space=pltpu.HBM)
NT = (((1,), (1,)), ((), ()))


def put_scores(score_ref, row, query, key_ref, k0, count):
    for j in range(0, count, TK):
        n = min(TK, count - j)
        score_ref[row + j : row + j + n, :] = lax.dot_general(
            key_ref[k0 + j : k0 + j + n, :], query, NT, preferred_element_type=jnp.float32
        )


def add_keys(score_ref, row, count, turned_ref, v0, old_max, old_sum, old_acc, start_row=None, q0=None):
    size = score_ref.shape[1]

    def piece(j, n):
        scores = score_ref[row + j : row + j + n, :]
        if start_row is None:
            return scores
        key_pos = j + lax.broadcasted_iota(jnp.int32, (n, size), 0)
        visible = key_pos >= start_row
        if q0 is not None and j + n > q0 + 1:
            visible = visible & (key_pos <= q0 + lax.broadcasted_iota(jnp.int32, (n, size), 1))
        return jnp.where(visible, scores, MASKED)

    pieces = [(j, min(TK, count - j)) for j in range(0, count, TK)]
    new_max = old_max
    for j, n in pieces:
        new_max = jnp.maximum(new_max, jnp.max(piece(j, n), axis=0, keepdims=True))
    rescale = jnp.exp2((old_max - new_max) * SCALE)
    total = old_sum * rescale
    acc = old_acc * rescale
    for j, n in pieces:
        probs = jnp.exp2((piece(j, n) - new_max) * SCALE)
        total = total + jnp.sum(probs, axis=0, keepdims=True)
        acc = acc + jnp.dot(
            turned_ref[:, v0 + j : v0 + j + n], probs.astype(jnp.bfloat16), preferred_element_type=jnp.float32
        )
    return new_max, total, acc


def sweep(steps, first, key_ref, k0, count, turned_ref, v0, state, q_ref, score_refs, start_row):
    acc_ref, stat_ref = state

    def make(i):
        q_at, _ = first(i)
        put_scores(score_refs[i % 2], 0, q_ref[pl.ds(q_at, TQ), :], key_ref, k0, count)

    def use(i):
        columns = pl.ds(first(i)[1], TQ)
        start = None if start_row is None else start_row(i)
        stat_ref[0:1, columns], stat_ref[1:2, columns], acc_ref[:, columns] = add_keys(
            score_refs[i % 2], 0, count, turned_ref, v0, stat_ref[0:1, columns], stat_ref[1:2, columns],
            acc_ref[:, columns], start,
        )

    make(0)
    for i in range(steps):
        if i + 1 < steps:
            make(i + 1)
        use(i)


def first_kernel(
    rows, group, docs, length_ref, q_hbm, k_hbm, v_hbm,
    acc_ref, stat_ref, stack_ref, start_ref, bound_ref,
    q_ref, k_ref, v_ref, vt_ref, score_ref, sem,
):
    copies = [
        pltpu.make_async_copy(source, target, sem.at[i])
        for i, (source, target) in enumerate(((q_hbm, q_ref), (k_hbm, k_ref), (v_hbm, v_ref)))
    ]
    for copy in copies:
        copy.start()
    first_row = lax.axis_index("seq") * rows
    tiles = range(0, rows, TFIRST)
    marks = [first_row, first_row + SPLIT, first_row + rows - 1]
    positions = first_row + lax.broadcasted_iota(jnp.int32, (1, rows), 1)

    def document(d, carried):
        begin, row_starts, found = carried
        row_starts = jnp.where(positions >= begin, begin, row_starts)
        found = [jnp.where(mark >= begin, begin, old) for mark, old in zip(marks, found)]
        return begin + length_ref[d], row_starts, found

    zero = jnp.int32(0)
    _, row_starts, found = lax.fori_loop(
        0, docs, document, (zero, jnp.zeros((1, rows), jnp.int32), [zero for _ in marks])
    )
    start_ref[0:1, :] = row_starts
    start_ref[1:8, :] = jnp.zeros((7, rows), jnp.int32)
    bound_ref[0] = first_row
    for i, value in enumerate(found):
        bound_ref[1 + i] = value
    for i in range(len(found) + 1, 8):
        bound_ref[i] = zero
    for copy in copies:
        copy.wait()
    vt_ref[...] = v_ref[...].T
    for h in range(group):
        stack_ref[h * rows : (h + 1) * rows, :] = q_ref[:, h * HD : (h + 1) * HD]
    stat_ref[...] = jnp.zeros_like(stat_ref)
    offsets = {}
    used = 0
    for q0 in tiles:
        offsets[q0] = used
        used += q0 + TFIRST

    def head(h, carried):
        base = pl.multiple_of(h * rows, rows)

        def make(q0):
            put_scores(score_ref, offsets[q0], stack_ref[pl.ds(base + q0, TFIRST), :], k_ref, 0, q0 + TFIRST)

        def use(q0):
            columns = pl.ds(base + q0, TFIRST)
            start = start_ref[0:1, q0 : q0 + TFIRST] - first_row
            lowest = jnp.full((1, TFIRST), LOWEST, jnp.float32)
            none = jnp.zeros((1, TFIRST), jnp.float32)
            stat_ref[0:1, columns], stat_ref[1:2, columns], acc_ref[:, columns] = add_keys(
                score_ref, offsets[q0], q0 + TFIRST, vt_ref, 0, lowest, none, jnp.zeros((HD, TFIRST), jnp.float32), start, q0
            )

        order = list(reversed(tiles))
        make(order[0])
        for i, q0 in enumerate(order):
            if i + 1 < len(order):
                make(order[i + 1])
            use(q0)
        return carried

    lax.fori_loop(0, group, head, 0)


def middle_kernel(
    distance, rows, group, bound_ref, start_ref, q_ref, k_ref, v_ref, acc_in, stat_in, acc_ref, stat_ref, vt_ref, *score_refs
):
    acc_ref[...] = acc_in[...]
    stat_ref[...] = stat_in[...]
    first_key = bound_ref[0] - distance * rows
    needed = (bound_ref[1] < first_key + rows) & (first_key >= 0)
    inside = bound_ref[3] > first_key
    tiles = rows // TQ

    def work(masked):
        vt_ref[...] = v_ref[...].T

        def head(h, carried):
            def first(i):
                return (pl.multiple_of(h * rows + i * TQ, TQ),) * 2

            def start_row(i):
                return start_ref[0:1, i * TQ : (i + 1) * TQ] - first_key

            sweep(
                tiles, first, k_ref, 0, rows, vt_ref, 0, (acc_ref, stat_ref), q_ref, score_refs, start_row if masked else None
            )
            return carried

        lax.fori_loop(0, group, head, 0)

    pl.when(needed & jnp.logical_not(inside))(lambda: work(False))
    pl.when(needed & inside)(lambda: work(True))


def last_kernel(late, rows, group, bound_ref, start_ref, q_ref, k_ref, v_ref, *refs):
    far_count = 1 if late else 2
    far_refs = refs[:far_count]
    acc_in, stat_in, out_ref, acc_ref, stat_ref, vt_ref, *score_refs = refs[far_count:]
    base, tiles = (SPLIT, LATE_TILES) if late else (0, EARLY_TILES)
    size = sum(tiles)
    offsets = [sum(tiles[:i]) for i in range(len(tiles))]
    for h in range(group):
        acc_ref[:, h * size : (h + 1) * size] = acc_in[:, h * rows + base : h * rows + base + size]
        stat_ref[:, h * size : (h + 1) * size] = stat_in[:, h * rows + base : h * rows + base + size]

    def block(key_ref, v_block, key_count, first_key, masked, skipped):
        vt_ref[:, :key_count] = v_block().T

        def head(h, carried):
            for i, (at, width) in enumerate(zip(offsets, tiles)):
                skip = skipped(at)
                query = q_ref[pl.ds(pl.multiple_of(h * rows + base + at, 128), width), :]
                put_scores(score_refs[i], 0, query, key_ref, skip, key_count - skip)
            for i, (at, width) in enumerate(zip(offsets, tiles)):
                skip = skipped(at)
                columns = pl.ds(pl.multiple_of(h * size + at, 128), width)
                start = start_ref[0:1, base + at : base + at + width] - (first_key + skip) if masked else None
                stat_ref[0:1, columns], stat_ref[1:2, columns], acc_ref[:, columns] = add_keys(
                    score_refs[i], 0, key_count - skip, vt_ref, skip, stat_ref[0:1, columns], stat_ref[1:2, columns],
                    acc_ref[:, columns], start,
                )
            return carried

        lax.fori_loop(0, group, head, 0)

    near_key = bound_ref[0] - 3 * rows
    lowest = bound_ref[2] if late else bound_ref[1]
    needed = (lowest < near_key + rows) & (near_key >= 0)
    inside = bound_ref[3] > near_key
    pl.when(needed & jnp.logical_not(inside))(lambda: block(k_ref, lambda: v_ref[...], rows, near_key, False, lambda at: 0))
    pl.when(needed & inside)(lambda: block(k_ref, lambda: v_ref[...], rows, near_key, True, lambda at: 0))

    far_key = near_key - rows
    late_ref = far_refs[0]
    pl.when((lowest < far_key + rows) & (far_key >= 0))(
        lambda: block(
            late_ref.at[:, :HD], lambda: late_ref[:, HD:], rows - SPLIT, far_key + SPLIT, True, lambda at: at if late else 0
        )
    )
    if not late:
        early_ref = far_refs[1]
        pl.when((lowest < far_key + SPLIT) & (far_key >= 0))(
            lambda: block(early_ref.at[:, :HD], lambda: early_ref[:, HD:], SPLIT, far_key, True, lambda at: 0)
        )

    for h in range(group):
        columns = slice(h * size, (h + 1) * size)
        scaled = acc_ref[:, columns] / stat_ref[1:2, columns]
        out_ref[:, h * HD : (h + 1) * HD] = scaled.T.astype(jnp.bfloat16)


def cost(rows, keys, columns):
    return pl.CostEstimate(flops=0, bytes_accessed=0, transcendentals=0)


def params(mebibytes=32):
    return pltpu.CompilerParams(vmem_limit_bytes=mebibytes * 2**20)


def attend_first(doc_lengths, queries, keys, values):
    rows, columns = queries.shape
    group = columns // HD
    tiles = rows // TFIRST
    return pl.pallas_call(
        functools.partial(first_kernel, rows, group, doc_lengths.shape[0]),
        out_shape=[
            jax.ShapeDtypeStruct((HD, group * rows), jnp.float32),
            jax.ShapeDtypeStruct((8, group * rows), jnp.float32),
            jax.ShapeDtypeStruct((group * rows, HD), jnp.bfloat16),
            jax.ShapeDtypeStruct((8, rows), jnp.int32),
            jax.ShapeDtypeStruct((8,), jnp.int32),
        ],
        in_specs=[SMEM, HBM, HBM, HBM],
        out_specs=[VMEM, VMEM, VMEM, VMEM, SMEM],
        scratch_shapes=[
            pltpu.VMEM(queries.shape, jnp.bfloat16),
            pltpu.VMEM(keys.shape, jnp.bfloat16),
            pltpu.VMEM(values.shape, jnp.bfloat16),
            pltpu.VMEM((HD, rows), jnp.bfloat16),
            pltpu.VMEM((TFIRST * tiles * (tiles + 1) // 2, TFIRST), jnp.float32),
            pltpu.SemaphoreType.DMA((3,)),
        ],
        compiler_params=params(),
        cost_estimate=cost(rows, rows, columns),
        name="attend_first",
    )(doc_lengths, queries, keys, values)


def attend_middle(distance, bounds, start_rows, stack, keys, values, state):
    rows = keys.shape[0]
    group = stack.shape[0] // rows
    return pl.pallas_call(
        functools.partial(middle_kernel, distance, rows, group),
        out_shape=[jax.ShapeDtypeStruct(s.shape, s.dtype) for s in state],
        in_specs=[SMEM] + [VMEM] * 6,
        out_specs=[VMEM, VMEM],
        scratch_shapes=[pltpu.VMEM((HD, rows), jnp.bfloat16)] + [pltpu.VMEM((rows, TQ), jnp.float32)] * 2,
        input_output_aliases={5: 0, 6: 1},
        compiler_params=params(),
        cost_estimate=cost(rows, rows, group * HD),
        name=f"attend_{distance}",
    )(bounds, start_rows, stack, keys, values, *state)


def attend_last(late, bounds, start_rows, stack, keys, values, far, state):
    rows = keys.shape[0]
    tiles = LATE_TILES if late else EARLY_TILES
    size = sum(tiles)
    group = stack.shape[0] // rows
    return pl.pallas_call(
        functools.partial(last_kernel, late, rows, group),
        out_shape=jax.ShapeDtypeStruct((size, group * HD), jnp.bfloat16),
        in_specs=[SMEM] + [VMEM] * (6 + len(far)),
        out_specs=VMEM,
        scratch_shapes=[
            pltpu.VMEM((HD, group * size), jnp.float32),
            pltpu.VMEM((8, group * size), jnp.float32),
            pltpu.VMEM((HD, rows), jnp.bfloat16),
        ]
        + [pltpu.VMEM((rows, tile), jnp.float32) for tile in tiles],
        compiler_params=params(),
        cost_estimate=cost(size, rows, group * HD),
        name="attend_late" if late else "attend_early",
    )(bounds, start_rows, stack, keys, values, *far, *state)


def prelude_kernel(chips, weight_hbm, k_hbm, v_hbm, *refs):
    weight_refs, far_ref, sem = refs[:chips], refs[chips], refs[-1]
    wide = weight_refs[0].shape[1]
    late = far_ref.shape[0]
    chip = lax.axis_index("head") // 2
    copies = [
        pltpu.make_async_copy(k_hbm.at[pl.ds(SPLIT, late), :], far_ref.at[:, :HD], sem.at[chips]),
        pltpu.make_async_copy(v_hbm.at[pl.ds(SPLIT, late), :], far_ref.at[:, HD:], sem.at[chips + 1]),
    ]
    for d in (1, 3, 2, 0):
        column = pl.multiple_of(lax.rem(chip + d, chips) * wide, wide)
        copies.append(pltpu.make_async_copy(weight_hbm.at[:, pl.ds(column, wide)], weight_refs[d], sem.at[d]))
    for copy in copies:
        copy.start()
    for copy in copies:
        copy.wait()


def prelude(out_weight, keys, values, chips):
    rows, columns = out_weight.shape
    block = jax.ShapeDtypeStruct((rows, columns // chips), out_weight.dtype)
    far = jax.ShapeDtypeStruct((keys.shape[0] - SPLIT, 2 * HD), keys.dtype)
    *weights, far = pl.pallas_call(
        functools.partial(prelude_kernel, chips),
        out_shape=[block] * chips + [far],
        in_specs=[HBM, HBM, HBM],
        out_specs=[VMEM] * (chips + 1),
        scratch_shapes=[pltpu.SemaphoreType.DMA((chips + 2,))],
        compiler_params=params(60),
        name="prelude",
    )(out_weight, keys, values)
    return weights, far


def near_kernel(own_ref, before_ref, after_ref, w0_ref, w1_ref, w3_ref, out_ref):
    block = jnp.concatenate([own_ref[...], before_ref[...], after_ref[...]], axis=1)
    weight = jnp.concatenate([w0_ref[...], w1_ref[...], w3_ref[...]], axis=0)
    out_ref[...] = jnp.dot(block, weight, preferred_element_type=jnp.float32)


def project_near(*operands):
    size, wide = operands[0].shape[0], operands[3].shape[1]
    return pl.pallas_call(
        near_kernel,
        out_shape=jax.ShapeDtypeStruct((size, wide), jnp.float32),
        in_specs=[VMEM] * 6,
        out_specs=VMEM,
        compiler_params=params(),
        name="project_near",
    )(*operands)


def far_kernel(first_ref, second_ref, weight_ref, near_ref, kept_ref, given_ref):
    size, columns = first_ref.shape
    core = lax.axis_index("head") % 2
    low, high = slice(0, columns), slice(columns, None)
    for i, block_ref in enumerate((first_ref, second_ref)):
        part = slice(i * size, (i + 1) * size)
        total = near_ref[part, :] + jnp.dot(block_ref[...], weight_ref[...], preferred_element_type=jnp.float32)

        def give(kept, given):
            kept_ref[part, :] = total[:, kept]
            given_ref[part, :] = total[:, given].astype(jnp.bfloat16)

        pl.when(core == 0)(lambda: give(low, high))
        pl.when(core == 1)(lambda: give(high, low))


def project_far(blocks, weight, near):
    rows, wide = near.shape
    return pl.pallas_call(
        far_kernel,
        out_shape=[jax.ShapeDtypeStruct((rows, wide // 2), t) for t in (jnp.float32, jnp.bfloat16)],
        in_specs=[VMEM] * 4,
        out_specs=[VMEM, VMEM],
        compiler_params=params(),
        name="project_far",
    )(*blocks, weight, near)


def join_kernel(*refs):
    out_ref = refs[-1]
    done = 0
    for kept, taken in zip(refs[0:-1:2], refs[1:-1:2]):
        size = kept.shape[0]
        out_ref[done : done + size, :] = (kept[...] + taken[...].astype(jnp.float32)).astype(jnp.bfloat16)
        done += size


def join(*parts):
    rows, columns = sum(part.shape[0] for part in parts[::2]), parts[0].shape[1]
    return pl.pallas_call(
        join_kernel,
        out_shape=jax.ShapeDtypeStruct((rows, columns), jnp.bfloat16),
        in_specs=[VMEM] * len(parts),
        out_specs=VMEM,
        compiler_params=params(),
        name="join",
    )(*parts)


def after(value, *others):
    return lax.optimization_barrier((value, others))[0]


def body(queries, keys, values, out_weight, doc_lengths):
    seq_size = lax.axis_size("seq")
    head_size = lax.axis_size("head")
    chips = head_size // 2
    def next_block(block):
        return lax.ppermute(block, "seq", [(i, (i + 1) % seq_size) for i in range(seq_size)])

    def back(block, distance):
        return lax.ppermute(block, "seq", [(i, i - i % ROW + (i - distance) % ROW) for i in range(seq_size)])

    def four_on(block):
        owners = [i - i % ROW + (i + 3) % ROW for i in range(seq_size)]
        return lax.ppermute(block, "seq", [(i, (owner + 4) % seq_size) for i, owner in enumerate(owners)])

    def chip_shift(block, distance):
        route = [(i, (i + 2 * distance) % head_size) for i in range(head_size)]
        return lax.ppermute(block, "head", route)

    def swap(block):
        return lax.ppermute(block, "head", [(i, i ^ 1) for i in range(head_size)])

    k1, v1 = next_block(keys), next_block(values)
    blocks, far = prelude(out_weight, keys, values, chips)
    far = back(far, 1)
    weights = {0: blocks[0], 1: chip_shift(blocks[1], 1), 3: chip_shift(blocks[3], 3)}
    *state, stack, start_rows, bounds = attend_first(doc_lengths, queries, keys, values)
    k2, v2 = next_block(after(k1, state[1])), next_block(after(v1, state[1]))
    far = back(after(far, state[1]), 2)
    state = attend_middle(1, bounds, start_rows, stack, k1, v1, state)
    k3, v3 = next_block(after(k2, state[1])), next_block(after(v2, state[1]))
    far = four_on(after(far, state[1]))
    weights[2] = chip_shift(after(blocks[2], state[1], weights[1]), 2)
    bounds = after(bounds, weights[1], weights[3])
    state = attend_middle(2, bounds, start_rows, stack, k2, v2, state)
    late = attend_last(True, bounds, start_rows, stack, k3, v3, (far,), state)
    k3a, v3a = after(k3, late), after(v3, late)
    first_far = next_block(jnp.concatenate([k3a[:SPLIT], v3a[:SPLIT]], axis=1))

    def sides(block):
        return chip_shift(block, 1), chip_shift(block, -1)

    def forwarded(before, behind):
        middle = before.shape[0] // 2
        return chip_shift(before[:middle], 1), chip_shift(behind[middle:], -1)

    near_weights = (weights[0], weights[1], weights[3])
    late_sides = sides(late)
    bounds = after(bounds, weights[2], late)
    early = attend_last(False, bounds, start_rows, stack, k3, v3, (far, first_far), state)
    early_sides = sides(early)
    late_far = forwarded(*late_sides)
    late_near = project_near(late, *late_sides, *near_weights)
    early_far = forwarded(*early_sides)
    early_near = project_near(early, *early_sides, *near_weights)
    late_kept, late_given = project_far(late_far, weights[2], late_near)
    late_taken = swap(late_given)
    early_kept, early_given = project_far(early_far, weights[2], early_near)
    early_taken = swap(early_given)
    return join(early_kept, early_taken, late_kept, late_taken)


def solution(mesh):
    return jax.shard_map(
        body,
        mesh=mesh,
        in_specs=(P("seq", "head"), P("seq", "head"), P("seq", "head"), P("head", None), P()),
        out_specs=P("seq", "head"),
        check_vma=False,
    )
```

```python
import functools

import jax
import jax.numpy as jnp
from jax import lax
from jax.experimental import pallas as pl
from jax.experimental.pallas import tpu as pltpu
from jax.sharding import PartitionSpec as P

HD = 128
ROW = 8
TFIRST = 256
TQ = 512
TK = 512
SPLIT = 512
LATE_TILES = (256, 256)
EARLY_TILES = (256, 256)
LOG2E = 1.4426950408889634
SCALE = LOG2E / HD**0.5
MASKED = -1e30
LOWEST = -1e29
VMEM = pl.BlockSpec(memory_space=pltpu.VMEM)
SMEM = pl.BlockSpec(memory_space=pltpu.SMEM)
HBM = pl.BlockSpec(memory_space=pltpu.HBM)
NT = (((1,), (1,)), ((), ()))


def put_scores(score_ref, row, query, key_ref, k0, count):
    for j in range(0, count, TK):
        n = min(TK, count - j)
        score_ref[row + j : row + j + n, :] = lax.dot_general(
            key_ref[k0 + j : k0 + j + n, :], query, NT, preferred_element_type=jnp.float32
        )


def add_keys(score_ref, row, count, turned_ref, v0, old_max, old_sum, old_acc, start_row=None, q0=None):
    size = score_ref.shape[1]

    def piece(j, n):
        scores = score_ref[row + j : row + j + n, :]
        if start_row is None:
            return scores
        key_pos = j + lax.broadcasted_iota(jnp.int32, (n, size), 0)
        visible = key_pos >= start_row
        if q0 is not None and j + n > q0 + 1:
            visible = visible & (key_pos <= q0 + lax.broadcasted_iota(jnp.int32, (n, size), 1))
        return jnp.where(visible, scores, MASKED)

    pieces = [(j, min(TK, count - j)) for j in range(0, count, TK)]
    new_max = old_max
    for j, n in pieces:
        new_max = jnp.maximum(new_max, jnp.max(piece(j, n), axis=0, keepdims=True))
    rescale = jnp.exp2((old_max - new_max) * SCALE)
    total = old_sum * rescale
    acc = old_acc * rescale
    for j, n in pieces:
        probs = jnp.exp2((piece(j, n) - new_max) * SCALE)
        total = total + jnp.sum(probs, axis=0, keepdims=True)
        acc = acc + jnp.dot(
            turned_ref[:, v0 + j : v0 + j + n], probs.astype(jnp.bfloat16), preferred_element_type=jnp.float32
        )
    return new_max, total, acc


def sweep(steps, first, key_ref, k0, count, turned_ref, v0, state, q_ref, score_refs, start_row):
    acc_ref, stat_ref = state

    def make(i):
        q_at, _ = first(i)
        put_scores(score_refs[i % 2], 0, q_ref[pl.ds(q_at, TQ), :], key_ref, k0, count)

    def use(i):
        columns = pl.ds(first(i)[1], TQ)
        start = None if start_row is None else start_row(i)
        stat_ref[0:1, columns], stat_ref[1:2, columns], acc_ref[:, columns] = add_keys(
            score_refs[i % 2], 0, count, turned_ref, v0, stat_ref[0:1, columns], stat_ref[1:2, columns],
            acc_ref[:, columns], start,
        )

    make(0)
    for i in range(steps):
        if i + 1 < steps:
            make(i + 1)
        use(i)


def first_kernel(
    rows, group, docs, length_ref, q_hbm, k_hbm, v_hbm,
    acc_ref, stat_ref, stack_ref, start_ref, bound_ref,
    q_ref, k_ref, v_ref, vt_ref, score_ref, sem,
):
    copies = [
        pltpu.make_async_copy(source, target, sem.at[i])
        for i, (source, target) in enumerate(((q_hbm, q_ref), (k_hbm, k_ref), (v_hbm, v_ref)))
    ]
    for copy in copies:
        copy.start()
    first_row = lax.axis_index("seq") * rows
    tiles = range(0, rows, TFIRST)
    marks = [first_row, first_row + SPLIT, first_row + rows - 1]
    positions = first_row + lax.broadcasted_iota(jnp.int32, (1, rows), 1)

    def document(d, carried):
        begin, row_starts, found = carried
        row_starts = jnp.where(positions >= begin, begin, row_starts)
        found = [jnp.where(mark >= begin, begin, old) for mark, old in zip(marks, found)]
        return begin + length_ref[d], row_starts, found

    zero = jnp.int32(0)
    _, row_starts, found = lax.fori_loop(
        0, docs, document, (zero, jnp.zeros((1, rows), jnp.int32), [zero for _ in marks])
    )
    start_ref[0:1, :] = row_starts
    start_ref[1:8, :] = jnp.zeros((7, rows), jnp.int32)
    bound_ref[0] = first_row
    for i, value in enumerate(found):
        bound_ref[1 + i] = value
    for i in range(len(found) + 1, 8):
        bound_ref[i] = zero
    for copy in copies:
        copy.wait()
    vt_ref[...] = v_ref[...].T
    for h in range(group):
        stack_ref[h * rows : (h + 1) * rows, :] = q_ref[:, h * HD : (h + 1) * HD]
    stat_ref[...] = jnp.zeros_like(stat_ref)
    offsets = {}
    used = 0
    for q0 in tiles:
        offsets[q0] = used
        used += q0 + TFIRST

    def head(h, carried):
        base = pl.multiple_of(h * rows, rows)

        def make(q0):
            put_scores(score_ref, offsets[q0], stack_ref[pl.ds(base + q0, TFIRST), :], k_ref, 0, q0 + TFIRST)

        def use(q0):
            columns = pl.ds(base + q0, TFIRST)
            start = start_ref[0:1, q0 : q0 + TFIRST] - first_row
            lowest = jnp.full((1, TFIRST), LOWEST, jnp.float32)
            none = jnp.zeros((1, TFIRST), jnp.float32)
            stat_ref[0:1, columns], stat_ref[1:2, columns], acc_ref[:, columns] = add_keys(
                score_ref, offsets[q0], q0 + TFIRST, vt_ref, 0, lowest, none, jnp.zeros((HD, TFIRST), jnp.float32), start, q0
            )

        order = list(reversed(tiles))
        make(order[0])
        for i, q0 in enumerate(order):
            if i + 1 < len(order):
                make(order[i + 1])
            use(q0)
        return carried

    lax.fori_loop(0, group, head, 0)


def middle_kernel(
    distance, rows, group, bound_ref, start_ref, q_ref, k_ref, v_ref, acc_in, stat_in, acc_ref, stat_ref, vt_ref, *score_refs
):
    acc_ref[...] = acc_in[...]
    stat_ref[...] = stat_in[...]
    first_key = bound_ref[0] - distance * rows
    needed = (bound_ref[1] < first_key + rows) & (first_key >= 0)
    inside = bound_ref[3] > first_key
    tiles = rows // TQ

    def work(masked):
        vt_ref[...] = v_ref[...].T

        def head(h, carried):
            def first(i):
                return (pl.multiple_of(h * rows + i * TQ, TQ),) * 2

            def start_row(i):
                return start_ref[0:1, i * TQ : (i + 1) * TQ] - first_key

            sweep(
                tiles, first, k_ref, 0, rows, vt_ref, 0, (acc_ref, stat_ref), q_ref, score_refs, start_row if masked else None
            )
            return carried

        lax.fori_loop(0, group, head, 0)

    pl.when(needed & jnp.logical_not(inside))(lambda: work(False))
    pl.when(needed & inside)(lambda: work(True))


def last_kernel(late, rows, group, bound_ref, start_ref, q_ref, k_ref, v_ref, *refs):
    far_count = 1 if late else 2
    far_refs = refs[:far_count]
    acc_in, stat_in, out_ref, acc_ref, stat_ref, vt_ref, *score_refs = refs[far_count:]
    base, tiles = (SPLIT, LATE_TILES) if late else (0, EARLY_TILES)
    size = sum(tiles)
    offsets = [sum(tiles[:i]) for i in range(len(tiles))]
    for h in range(group):
        acc_ref[:, h * size : (h + 1) * size] = acc_in[:, h * rows + base : h * rows + base + size]
        stat_ref[:, h * size : (h + 1) * size] = stat_in[:, h * rows + base : h * rows + base + size]

    def block(key_ref, v_block, key_count, first_key, masked, skipped):
        vt_ref[:, :key_count] = v_block().T

        def head(h, carried):
            for i, (at, width) in enumerate(zip(offsets, tiles)):
                skip = skipped(at)
                query = q_ref[pl.ds(pl.multiple_of(h * rows + base + at, 128), width), :]
                put_scores(score_refs[i], 0, query, key_ref, skip, key_count - skip)
            for i, (at, width) in enumerate(zip(offsets, tiles)):
                skip = skipped(at)
                columns = pl.ds(pl.multiple_of(h * size + at, 128), width)
                start = start_ref[0:1, base + at : base + at + width] - (first_key + skip) if masked else None
                stat_ref[0:1, columns], stat_ref[1:2, columns], acc_ref[:, columns] = add_keys(
                    score_refs[i], 0, key_count - skip, vt_ref, skip, stat_ref[0:1, columns], stat_ref[1:2, columns],
                    acc_ref[:, columns], start,
                )
            return carried

        lax.fori_loop(0, group, head, 0)

    near_key = bound_ref[0] - 3 * rows
    lowest = bound_ref[2] if late else bound_ref[1]
    needed = (lowest < near_key + rows) & (near_key >= 0)
    inside = bound_ref[3] > near_key
    pl.when(needed & jnp.logical_not(inside))(lambda: block(k_ref, lambda: v_ref[...], rows, near_key, False, lambda at: 0))
    pl.when(needed & inside)(lambda: block(k_ref, lambda: v_ref[...], rows, near_key, True, lambda at: 0))

    far_key = near_key - rows
    late_ref = far_refs[0]
    pl.when((lowest < far_key + rows) & (far_key >= 0))(
        lambda: block(
            late_ref.at[:, :HD], lambda: late_ref[:, HD:], rows - SPLIT, far_key + SPLIT, True, lambda at: at if late else 0
        )
    )
    if not late:
        early_ref = far_refs[1]
        pl.when((lowest < far_key + SPLIT) & (far_key >= 0))(
            lambda: block(early_ref.at[:, :HD], lambda: early_ref[:, HD:], SPLIT, far_key, True, lambda at: 0)
        )

    for h in range(group):
        columns = slice(h * size, (h + 1) * size)
        scaled = acc_ref[:, columns] / stat_ref[1:2, columns]
        out_ref[:, h * HD : (h + 1) * HD] = scaled.T.astype(jnp.bfloat16)


def cost(rows, keys, columns, weight=0):
    return pl.CostEstimate(flops=4 * weight * rows * keys * columns, bytes_accessed=6 * weight * rows * columns, transcendentals=weight * rows * keys * 3)


def params(mebibytes=32):
    return pltpu.CompilerParams(vmem_limit_bytes=mebibytes * 2**20)


def attend_first(doc_lengths, queries, keys, values):
    rows, columns = queries.shape
    group = columns // HD
    tiles = rows // TFIRST
    return pl.pallas_call(
        functools.partial(first_kernel, rows, group, doc_lengths.shape[0]),
        out_shape=[
            jax.ShapeDtypeStruct((HD, group * rows), jnp.float32),
            jax.ShapeDtypeStruct((8, group * rows), jnp.float32),
            jax.ShapeDtypeStruct((group * rows, HD), jnp.bfloat16),
            jax.ShapeDtypeStruct((8, rows), jnp.int32),
            jax.ShapeDtypeStruct((8,), jnp.int32),
        ],
        in_specs=[SMEM, HBM, HBM, HBM],
        out_specs=[VMEM, VMEM, VMEM, VMEM, SMEM],
        scratch_shapes=[
            pltpu.VMEM(queries.shape, jnp.bfloat16),
            pltpu.VMEM(keys.shape, jnp.bfloat16),
            pltpu.VMEM(values.shape, jnp.bfloat16),
            pltpu.VMEM((HD, rows), jnp.bfloat16),
            pltpu.VMEM((TFIRST * tiles * (tiles + 1) // 2, TFIRST), jnp.float32),
            pltpu.SemaphoreType.DMA((3,)),
        ],
        compiler_params=params(60),
        cost_estimate=cost(rows, rows, columns, 1),
        name="attend_first",
    )(doc_lengths, queries, keys, values)


def attend_middle(distance, bounds, start_rows, stack, keys, values, state):
    rows = keys.shape[0]
    group = stack.shape[0] // rows
    return pl.pallas_call(
        functools.partial(middle_kernel, distance, rows, group),
        out_shape=[jax.ShapeDtypeStruct(s.shape, s.dtype) for s in state],
        in_specs=[SMEM] + [VMEM] * 6,
        out_specs=[VMEM, VMEM],
        scratch_shapes=[pltpu.VMEM((HD, rows), jnp.bfloat16)] + [pltpu.VMEM((rows, TQ), jnp.float32)] * 2,
        input_output_aliases={5: 0, 6: 1},
        compiler_params=params(),
        cost_estimate=cost(rows, rows, group * HD),
        name=f"attend_{distance}",
    )(bounds, start_rows, stack, keys, values, *state)


def attend_last(late, bounds, start_rows, stack, keys, values, far, state):
    rows = keys.shape[0]
    tiles = LATE_TILES if late else EARLY_TILES
    size = sum(tiles)
    group = stack.shape[0] // rows
    return pl.pallas_call(
        functools.partial(last_kernel, late, rows, group),
        out_shape=jax.ShapeDtypeStruct((size, group * HD), jnp.bfloat16),
        in_specs=[SMEM] + [VMEM] * (6 + len(far)),
        out_specs=VMEM,
        scratch_shapes=[
            pltpu.VMEM((HD, group * size), jnp.float32),
            pltpu.VMEM((8, group * size), jnp.float32),
            pltpu.VMEM((HD, rows), jnp.bfloat16),
        ]
        + [pltpu.VMEM((rows, tile), jnp.float32) for tile in tiles],
        compiler_params=params(),
        cost_estimate=cost(size, rows, group * HD),
        name="attend_late" if late else "attend_early",
    )(bounds, start_rows, stack, keys, values, *far, *state)


def prelude_kernel(chips, weight_hbm, k_hbm, v_hbm, *refs):
    weight_refs, far_ref, sem = refs[:chips], refs[chips], refs[-1]
    wide = weight_refs[0].shape[1]
    late = far_ref.shape[0]
    chip = lax.axis_index("head") // 2
    copies = [
        pltpu.make_async_copy(k_hbm.at[pl.ds(SPLIT, late), :], far_ref.at[:, :HD], sem.at[chips]),
        pltpu.make_async_copy(v_hbm.at[pl.ds(SPLIT, late), :], far_ref.at[:, HD:], sem.at[chips + 1]),
    ]
    for d in (1, 3, 2, 0):
        column = pl.multiple_of(lax.rem(chip + d, chips) * wide, wide)
        copies.append(pltpu.make_async_copy(weight_hbm.at[:, pl.ds(column, wide)], weight_refs[d], sem.at[d]))
    for copy in copies:
        copy.start()
    for copy in copies:
        copy.wait()


def prelude(out_weight, keys, values, chips):
    rows, columns = out_weight.shape
    block = jax.ShapeDtypeStruct((rows, columns // chips), out_weight.dtype)
    far = jax.ShapeDtypeStruct((keys.shape[0] - SPLIT, 2 * HD), keys.dtype)
    *weights, far = pl.pallas_call(
        functools.partial(prelude_kernel, chips),
        out_shape=[block] * chips + [far],
        in_specs=[HBM, HBM, HBM],
        out_specs=[VMEM] * (chips + 1),
        scratch_shapes=[pltpu.SemaphoreType.DMA((chips + 2,))],
        compiler_params=params(58),
        name="prelude",
    )(out_weight, keys, values)
    return weights, far


def near_kernel(own_ref, before_ref, after_ref, w0_ref, w1_ref, w3_ref, out_ref):
    block = jnp.concatenate([own_ref[...], before_ref[...], after_ref[...]], axis=1)
    weight = jnp.concatenate([w0_ref[...], w1_ref[...], w3_ref[...]], axis=0)
    out_ref[...] = jnp.dot(block, weight, preferred_element_type=jnp.float32)


def project_near(*operands):
    size, wide = operands[0].shape[0], operands[3].shape[1]
    return pl.pallas_call(
        near_kernel,
        out_shape=jax.ShapeDtypeStruct((size, wide), jnp.float32),
        in_specs=[VMEM] * 6,
        out_specs=VMEM,
        compiler_params=params(),
        name="project_near",
    )(*operands)


def far_kernel(first_ref, second_ref, weight_ref, near_ref, kept_ref, given_ref):
    size, columns = first_ref.shape
    core = lax.axis_index("head") % 2
    low, high = slice(0, columns), slice(columns, None)
    for i, block_ref in enumerate((first_ref, second_ref)):
        part = slice(i * size, (i + 1) * size)
        total = near_ref[part, :] + jnp.dot(block_ref[...], weight_ref[...], preferred_element_type=jnp.float32)

        def give(kept, given):
            kept_ref[part, :] = total[:, kept]
            given_ref[part, :] = total[:, given].astype(jnp.bfloat16)

        pl.when(core == 0)(lambda: give(low, high))
        pl.when(core == 1)(lambda: give(high, low))


def project_far(blocks, weight, near):
    rows, wide = near.shape
    return pl.pallas_call(
        far_kernel,
        out_shape=[jax.ShapeDtypeStruct((rows, wide // 2), t) for t in (jnp.float32, jnp.bfloat16)],
        in_specs=[VMEM] * 4,
        out_specs=[VMEM, VMEM],
        compiler_params=params(),
        name="project_far",
    )(*blocks, weight, near)


def join_kernel(*refs):
    out_ref = refs[-1]
    done = 0
    for kept, taken in zip(refs[0:-1:2], refs[1:-1:2]):
        size = kept.shape[0]
        out_ref[done : done + size, :] = (kept[...] + taken[...].astype(jnp.float32)).astype(jnp.bfloat16)
        done += size


def join(*parts):
    rows, columns = sum(part.shape[0] for part in parts[::2]), parts[0].shape[1]
    return pl.pallas_call(
        join_kernel,
        out_shape=jax.ShapeDtypeStruct((rows, columns), jnp.bfloat16),
        in_specs=[VMEM] * len(parts),
        out_specs=VMEM,
        compiler_params=params(),
        name="join",
    )(*parts)


def after(value, *others):
    return lax.optimization_barrier((value, others))[0]


def body(queries, keys, values, out_weight, doc_lengths):
    seq_size = lax.axis_size("seq")
    head_size = lax.axis_size("head")
    chips = head_size // 2
    def next_block(block):
        return lax.ppermute(block, "seq", [(i, (i + 1) % seq_size) for i in range(seq_size)])

    def three_back(block):
        return lax.ppermute(block, "seq", [(i, i - i % ROW + (i - 3) % ROW) for i in range(seq_size)])

    def four_on(block):
        owners = [i - i % ROW + (i + 3) % ROW for i in range(seq_size)]
        return lax.ppermute(block, "seq", [(i, (owner + 4) % seq_size) for i, owner in enumerate(owners)])

    def chip_shift(block, distance):
        route = [(i, (i + 2 * distance) % head_size) for i in range(head_size)]
        return lax.ppermute(block, "head", route)

    def swap(block):
        return lax.ppermute(block, "head", [(i, i ^ 1) for i in range(head_size)])

    k1, v1 = next_block(keys), next_block(values)
    *state, stack, start_rows, bounds = attend_first(doc_lengths, queries, keys, values)
    k2, v2 = next_block(after(k1, state[1], v1)), next_block(after(v1, state[1]))
    blocks, far = prelude(after(out_weight, k1, state[1]), keys, values, chips)
    far = three_back(far)
    weights = {0: blocks[0], 1: chip_shift(after(blocks[1], v1), 1), 3: chip_shift(after(blocks[3], v1), 3)}
    state = attend_middle(1, bounds, start_rows, stack, k1, v1, state)
    k3, v3 = next_block(after(k2, state[1])), next_block(after(v2, state[1]))
    weights[2] = chip_shift(after(blocks[2], state[1], weights[1]), 2)
    bounds = after(bounds, weights[1], weights[3], far)
    far = four_on(far)
    state = attend_middle(2, bounds, start_rows, stack, k2, v2, state)
    first_far = next_block(jnp.concatenate([after(k3, state[1])[:SPLIT], after(v3, state[1])[:SPLIT]], axis=1))
    bounds = after(bounds, weights[2])
    late = attend_last(True, bounds, start_rows, stack, k3, v3, (far,), state)

    def sides(block):
        return chip_shift(block, 1), chip_shift(block, -1)

    def forwarded(before, behind):
        middle = before.shape[0] // 2
        return chip_shift(before[:middle], 1), chip_shift(behind[middle:], -1)

    near_weights = (weights[0], weights[1], weights[3])
    late_sides = sides(after(late, first_far))
    early = attend_last(False, bounds, start_rows, stack, k3, v3, (far, first_far), state)
    early_sides = sides(early)
    late_far = forwarded(*late_sides)
    late_near = project_near(late, *late_sides, *near_weights)
    early_far = forwarded(*early_sides)
    early_near = project_near(early, *early_sides, *near_weights)
    late_kept, late_given = project_far(late_far, weights[2], late_near)
    late_taken = swap(late_given)
    early_kept, early_given = project_far(early_far, weights[2], early_near)
    early_taken = swap(early_given)
    return join(early_kept, early_taken, late_kept, late_taken)


def solution(mesh):
    return jax.shard_map(
        body,
        mesh=mesh,
        in_specs=(P("seq", "head"), P("seq", "head"), P("seq", "head"), P("head", None), P()),
        out_specs=P("seq", "head"),
        check_vma=False,
    )
```

```python
import functools

import jax
import jax.numpy as jnp
from jax import lax
from jax.experimental import pallas as pl
from jax.experimental.pallas import tpu as pltpu
from jax.sharding import PartitionSpec as P

HD = 128
ROW = 8
TFIRST = 256
TQ = 512
TK = 512
SPLIT = 512
LATE_TILES = (256, 256)
EARLY_TILES = (256, 256)
LOG2E = 1.4426950408889634
SCALE = LOG2E / HD**0.5
MASKED = -1e30
LOWEST = -1e29
VMEM = pl.BlockSpec(memory_space=pltpu.VMEM)
SMEM = pl.BlockSpec(memory_space=pltpu.SMEM)
HBM = pl.BlockSpec(memory_space=pltpu.HBM)
NT = (((1,), (1,)), ((), ()))


def put_scores(score_ref, row, query, key_ref, k0, count):
    for j in range(0, count, TK):
        n = min(TK, count - j)
        score_ref[row + j : row + j + n, :] = lax.dot_general(
            key_ref[k0 + j : k0 + j + n, :], query, NT, preferred_element_type=jnp.float32
        )


def add_keys(score_ref, row, count, turned_ref, v0, old_max, old_sum, old_acc, start_row=None, q0=None):
    size = score_ref.shape[1]

    def piece(j, n):
        scores = score_ref[row + j : row + j + n, :]
        if start_row is None:
            return scores
        key_pos = j + lax.broadcasted_iota(jnp.int32, (n, size), 0)
        visible = key_pos >= start_row
        if q0 is not None and j + n > q0 + 1:
            visible = visible & (key_pos <= q0 + lax.broadcasted_iota(jnp.int32, (n, size), 1))
        return jnp.where(visible, scores, MASKED)

    pieces = [(j, min(TK, count - j)) for j in range(0, count, TK)]
    new_max = old_max
    for j, n in pieces:
        new_max = jnp.maximum(new_max, jnp.max(piece(j, n), axis=0, keepdims=True))
    rescale = jnp.exp2((old_max - new_max) * SCALE)
    total = old_sum * rescale
    acc = old_acc * rescale
    for j, n in pieces:
        probs = jnp.exp2((piece(j, n) - new_max) * SCALE)
        total = total + jnp.sum(probs, axis=0, keepdims=True)
        acc = acc + jnp.dot(
            turned_ref[:, v0 + j : v0 + j + n], probs.astype(jnp.bfloat16), preferred_element_type=jnp.float32
        )
    return new_max, total, acc


def sweep(steps, first, key_ref, k0, count, turned_ref, v0, state, q_ref, score_refs, start_row):
    acc_ref, stat_ref = state

    def make(i):
        q_at, _ = first(i)
        put_scores(score_refs[i % 2], 0, q_ref[pl.ds(q_at, TQ), :], key_ref, k0, count)

    def use(i):
        columns = pl.ds(first(i)[1], TQ)
        start = None if start_row is None else start_row(i)
        stat_ref[0:1, columns], stat_ref[1:2, columns], acc_ref[:, columns] = add_keys(
            score_refs[i % 2], 0, count, turned_ref, v0, stat_ref[0:1, columns], stat_ref[1:2, columns],
            acc_ref[:, columns], start,
        )

    make(0)
    for i in range(steps):
        if i + 1 < steps:
            make(i + 1)
        use(i)


def first_kernel(
    rows, group, docs, length_ref, q_hbm, k_hbm, v_hbm,
    acc_ref, stat_ref, stack_ref, start_ref, bound_ref,
    q_ref, k_ref, v_ref, vt_ref, score_ref, sem,
):
    copies = [
        pltpu.make_async_copy(source, target, sem.at[i])
        for i, (source, target) in enumerate(((q_hbm, q_ref), (k_hbm, k_ref), (v_hbm, v_ref)))
    ]
    for copy in copies:
        copy.start()
    first_row = lax.axis_index("seq") * rows
    tiles = range(0, rows, TFIRST)
    marks = [first_row, first_row + SPLIT, first_row + rows - 1]
    positions = first_row + lax.broadcasted_iota(jnp.int32, (1, rows), 1)

    def document(d, carried):
        begin, row_starts, found = carried
        row_starts = jnp.where(positions >= begin, begin, row_starts)
        found = [jnp.where(mark >= begin, begin, old) for mark, old in zip(marks, found)]
        return begin + length_ref[d], row_starts, found

    zero = jnp.int32(0)
    _, row_starts, found = lax.fori_loop(
        0, docs, document, (zero, jnp.zeros((1, rows), jnp.int32), [zero for _ in marks])
    )
    start_ref[0:1, :] = row_starts
    start_ref[1:8, :] = jnp.zeros((7, rows), jnp.int32)
    bound_ref[0] = first_row
    for i, value in enumerate(found):
        bound_ref[1 + i] = value
    for i in range(len(found) + 1, 8):
        bound_ref[i] = zero
    for copy in copies:
        copy.wait()
    vt_ref[...] = v_ref[...].T
    for h in range(group):
        stack_ref[h * rows : (h + 1) * rows, :] = q_ref[:, h * HD : (h + 1) * HD]
    stat_ref[...] = jnp.zeros_like(stat_ref)
    offsets = {}
    used = 0
    for q0 in tiles:
        offsets[q0] = used
        used += q0 + TFIRST

    def head(h, carried):
        base = pl.multiple_of(h * rows, rows)

        def make(q0):
            put_scores(score_ref, offsets[q0], stack_ref[pl.ds(base + q0, TFIRST), :], k_ref, 0, q0 + TFIRST)

        def use(q0):
            columns = pl.ds(base + q0, TFIRST)
            start = start_ref[0:1, q0 : q0 + TFIRST] - first_row
            lowest = jnp.full((1, TFIRST), LOWEST, jnp.float32)
            none = jnp.zeros((1, TFIRST), jnp.float32)
            stat_ref[0:1, columns], stat_ref[1:2, columns], acc_ref[:, columns] = add_keys(
                score_ref, offsets[q0], q0 + TFIRST, vt_ref, 0, lowest, none, jnp.zeros((HD, TFIRST), jnp.float32), start, q0
            )

        order = list(reversed(tiles))
        make(order[0])
        for i, q0 in enumerate(order):
            if i + 1 < len(order):
                make(order[i + 1])
            use(q0)
        return carried

    lax.fori_loop(0, group, head, 0)


def middle_kernel(
    distance, rows, group, bound_ref, start_ref, q_ref, k_ref, v_ref, acc_in, stat_in, acc_ref, stat_ref, vt_ref, *score_refs
):
    acc_ref[...] = acc_in[...]
    stat_ref[...] = stat_in[...]
    first_key = bound_ref[0] - distance * rows
    needed = (bound_ref[1] < first_key + rows) & (first_key >= 0)
    inside = bound_ref[3] > first_key
    tiles = rows // TQ

    def work(masked):
        vt_ref[...] = v_ref[...].T

        def head(h, carried):
            def first(i):
                return (pl.multiple_of(h * rows + i * TQ, TQ),) * 2

            def start_row(i):
                return start_ref[0:1, i * TQ : (i + 1) * TQ] - first_key

            sweep(
                tiles, first, k_ref, 0, rows, vt_ref, 0, (acc_ref, stat_ref), q_ref, score_refs, start_row if masked else None
            )
            return carried

        lax.fori_loop(0, group, head, 0)

    pl.when(needed & jnp.logical_not(inside))(lambda: work(False))
    pl.when(needed & inside)(lambda: work(True))


def add_block(tiles, base, rows, group, q_ref, start_ref, acc_ref, stat_ref, vt_ref, score_refs, key_ref, v_block, key_count, first_key, masked, skipped):
    size = sum(tiles)
    offsets = [sum(tiles[:i]) for i in range(len(tiles))]
    vt_ref[:, :key_count] = v_block().T

    def head(h, carried):
        for i, (at, width) in enumerate(zip(offsets, tiles)):
            skip = skipped(at)
            query = q_ref[pl.ds(pl.multiple_of(h * rows + base + at, 128), width), :]
            put_scores(score_refs[i], 0, query, key_ref, skip, key_count - skip)
        for i, (at, width) in enumerate(zip(offsets, tiles)):
            skip = skipped(at)
            columns = pl.ds(pl.multiple_of(h * size + at, 128), width)
            start = start_ref[0:1, base + at : base + at + width] - (first_key + skip) if masked else None
            stat_ref[0:1, columns], stat_ref[1:2, columns], acc_ref[:, columns] = add_keys(
                score_refs[i], 0, key_count - skip, vt_ref, skip, stat_ref[0:1, columns], stat_ref[1:2, columns],
                acc_ref[:, columns], start,
            )
        return carried

    lax.fori_loop(0, group, head, 0)


def near_part(late, rows, group, bound_ref, start_ref, q_ref, k_ref, v_ref, far_ref, acc_in, stat_in, acc_ref, stat_ref, vt_ref, score_refs):
    base, tiles = (SPLIT, LATE_TILES) if late else (0, EARLY_TILES)
    size = sum(tiles)
    for h in range(group):
        acc_ref[:, h * size : (h + 1) * size] = acc_in[:, h * rows + base : h * rows + base + size]
        stat_ref[:, h * size : (h + 1) * size] = stat_in[:, h * rows + base : h * rows + base + size]
    block = functools.partial(add_block, tiles, base, rows, group, q_ref, start_ref, acc_ref, stat_ref, vt_ref, score_refs)
    near_key = bound_ref[0] - 3 * rows
    lowest = bound_ref[2] if late else bound_ref[1]
    needed = (lowest < near_key + rows) & (near_key >= 0)
    inside = bound_ref[3] > near_key
    pl.when(needed & jnp.logical_not(inside))(lambda: block(k_ref, lambda: v_ref[...], rows, near_key, False, lambda at: 0))
    pl.when(needed & inside)(lambda: block(k_ref, lambda: v_ref[...], rows, near_key, True, lambda at: 0))
    far_key = near_key - rows
    pl.when((lowest < far_key + rows) & (far_key >= 0))(
        lambda: block(
            far_ref.at[:, :HD], lambda: far_ref[:, HD:], rows - SPLIT, far_key + SPLIT, True, lambda at: at if late else 0
        )
    )


def give_rows(group, acc_ref, stat_ref, out_ref):
    size = out_ref.shape[0]
    for h in range(group):
        columns = slice(h * size, (h + 1) * size)
        scaled = acc_ref[:, columns] / stat_ref[1:2, columns]
        out_ref[:, h * HD : (h + 1) * HD] = scaled.T.astype(jnp.bfloat16)


def late_kernel(rows, group, bound_ref, start_ref, q_ref, k_ref, v_ref, far_ref, acc_in, stat_in, out_ref, acc_ref, stat_ref, vt_ref, *score_refs):
    near_part(
        True, rows, group, bound_ref, start_ref, q_ref, k_ref, v_ref, far_ref, acc_in, stat_in, acc_ref, stat_ref, vt_ref, score_refs
    )
    give_rows(group, acc_ref, stat_ref, out_ref)


def early_kernel(rows, group, bound_ref, start_ref, q_ref, k_ref, v_ref, far_ref, acc_in, stat_in, acc_ref, stat_ref, vt_ref, *score_refs):
    near_part(
        False, rows, group, bound_ref, start_ref, q_ref, k_ref, v_ref, far_ref, acc_in, stat_in, acc_ref, stat_ref, vt_ref, score_refs
    )


def final_kernel(rows, group, bound_ref, start_ref, q_ref, far_ref, acc_in, stat_in, out_ref, acc_ref, stat_ref, vt_ref, *score_refs):
    acc_ref[...] = acc_in[...]
    stat_ref[...] = stat_in[...]
    far_key = bound_ref[0] - 4 * rows
    pl.when((bound_ref[1] < far_key + SPLIT) & (far_key >= 0))(
        lambda: add_block(
            EARLY_TILES, 0, rows, group, q_ref, start_ref, acc_ref, stat_ref, vt_ref, score_refs,
            far_ref.at[:, :HD], lambda: far_ref[:, HD:], SPLIT, far_key, True, lambda at: at,
        )
    )
    give_rows(group, acc_ref, stat_ref, out_ref)


def cost(rows, keys, columns, weight=0):
    return pl.CostEstimate(flops=4 * weight * rows * keys * columns, bytes_accessed=6 * weight * rows * columns, transcendentals=weight * rows * keys * 3)


def params(mebibytes=32):
    return pltpu.CompilerParams(vmem_limit_bytes=mebibytes * 2**20)


def attend_first(doc_lengths, queries, keys, values):
    rows, columns = queries.shape
    group = columns // HD
    tiles = rows // TFIRST
    return pl.pallas_call(
        functools.partial(first_kernel, rows, group, doc_lengths.shape[0]),
        out_shape=[
            jax.ShapeDtypeStruct((HD, group * rows), jnp.float32),
            jax.ShapeDtypeStruct((8, group * rows), jnp.float32),
            jax.ShapeDtypeStruct((group * rows, HD), jnp.bfloat16),
            jax.ShapeDtypeStruct((8, rows), jnp.int32),
            jax.ShapeDtypeStruct((8,), jnp.int32),
        ],
        in_specs=[SMEM, HBM, HBM, HBM],
        out_specs=[VMEM, VMEM, VMEM, VMEM, SMEM],
        scratch_shapes=[
            pltpu.VMEM(queries.shape, jnp.bfloat16),
            pltpu.VMEM(keys.shape, jnp.bfloat16),
            pltpu.VMEM(values.shape, jnp.bfloat16),
            pltpu.VMEM((HD, rows), jnp.bfloat16),
            pltpu.VMEM((TFIRST * tiles * (tiles + 1) // 2, TFIRST), jnp.float32),
            pltpu.SemaphoreType.DMA((3,)),
        ],
        compiler_params=params(60),
        cost_estimate=cost(rows, rows, columns, 1),
        name="attend_first",
    )(doc_lengths, queries, keys, values)


def attend_middle(distance, bounds, start_rows, stack, keys, values, state):
    rows = keys.shape[0]
    group = stack.shape[0] // rows
    return pl.pallas_call(
        functools.partial(middle_kernel, distance, rows, group),
        out_shape=[jax.ShapeDtypeStruct(s.shape, s.dtype) for s in state],
        in_specs=[SMEM] + [VMEM] * 6,
        out_specs=[VMEM, VMEM],
        scratch_shapes=[pltpu.VMEM((HD, rows), jnp.bfloat16)] + [pltpu.VMEM((rows, TQ), jnp.float32)] * 2,
        input_output_aliases={5: 0, 6: 1},
        compiler_params=params(),
        cost_estimate=cost(rows, rows, group * HD),
        name=f"attend_{distance}",
    )(bounds, start_rows, stack, keys, values, *state)


def attend_last(kind, bounds, start_rows, stack, rows, arrays, weight=0):
    kernel, tiles = {
        "late": (late_kernel, LATE_TILES),
        "early": (early_kernel, EARLY_TILES),
        "final": (final_kernel, EARLY_TILES),
    }[kind]
    size = sum(tiles)
    group = stack.shape[0] // rows
    state = [(HD, group * size), (8, group * size)]
    work = [pltpu.VMEM((HD, rows), jnp.bfloat16)] + [pltpu.VMEM((rows, tile), jnp.float32) for tile in tiles]
    if kind == "early":
        out = [jax.ShapeDtypeStruct(shape, jnp.float32) for shape in state]
    else:
        out = jax.ShapeDtypeStruct((size, group * HD), jnp.bfloat16)
        work = [pltpu.VMEM(shape, jnp.float32) for shape in state] + work
    return pl.pallas_call(
        functools.partial(kernel, rows, group),
        out_shape=out,
        in_specs=[SMEM] + [VMEM] * (2 + len(arrays)),
        out_specs=[VMEM, VMEM] if kind == "early" else VMEM,
        scratch_shapes=work,
        compiler_params=params(),
        cost_estimate=cost(size, rows, group * HD, weight),
        name="attend_" + kind,
    )(bounds, start_rows, stack, *arrays)


def pack_kernel(k_hbm, v_hbm, far_ref, sem):
    late = far_ref.shape[0]
    copies = [
        pltpu.make_async_copy(source.at[pl.ds(SPLIT, late), :], far_ref.at[:, part], sem.at[i])
        for i, (source, part) in enumerate(((k_hbm, slice(0, HD)), (v_hbm, slice(HD, 2 * HD))))
    ]
    for copy in copies:
        copy.start()
    for copy in copies:
        copy.wait()


def pack(keys, values):
    return pl.pallas_call(
        pack_kernel,
        out_shape=jax.ShapeDtypeStruct((keys.shape[0] - SPLIT, 2 * HD), keys.dtype),
        in_specs=[HBM, HBM],
        out_specs=HBM,
        scratch_shapes=[pltpu.SemaphoreType.DMA((2,))],
        compiler_params=params(58),
        name="pack",
    )(keys, values)


def cut_kernel(chips, weight_hbm, *refs):
    weight_refs, sem = refs[:chips], refs[-1]
    wide = weight_refs[0].shape[1]
    chip = lax.axis_index("head") // 2
    copies = []
    for d in (1, 3, 2, 0):
        column = pl.multiple_of(lax.rem(chip + d, chips) * wide, wide)
        copies.append(pltpu.make_async_copy(weight_hbm.at[:, pl.ds(column, wide)], weight_refs[d], sem.at[d]))
    for copy in copies:
        copy.start()
    for copy in copies:
        copy.wait()


def cut(out_weight, chips):
    rows, columns = out_weight.shape
    block = jax.ShapeDtypeStruct((rows, columns // chips), out_weight.dtype)
    return pl.pallas_call(
        functools.partial(cut_kernel, chips),
        out_shape=[block] * chips,
        in_specs=[HBM],
        out_specs=[HBM] * chips,
        scratch_shapes=[pltpu.SemaphoreType.DMA((chips,))],
        compiler_params=params(58),
        name="cut",
    )(out_weight)


def near_kernel(own_ref, before_ref, after_ref, w0_ref, w1_ref, w3_ref, out_ref):
    block = jnp.concatenate([own_ref[...], before_ref[...], after_ref[...]], axis=1)
    weight = jnp.concatenate([w0_ref[...], w1_ref[...], w3_ref[...]], axis=0)
    out_ref[...] = jnp.dot(block, weight, preferred_element_type=jnp.float32)


def project_near(*operands):
    size, wide = operands[0].shape[0], operands[3].shape[1]
    return pl.pallas_call(
        near_kernel,
        out_shape=jax.ShapeDtypeStruct((size, wide), jnp.float32),
        in_specs=[VMEM] * 6,
        out_specs=VMEM,
        compiler_params=params(),
        name="project_near",
    )(*operands)


def far_kernel(first_ref, second_ref, weight_ref, near_ref, kept_ref, given_ref):
    size, columns = first_ref.shape
    core = lax.axis_index("head") % 2
    low, high = slice(0, columns), slice(columns, None)
    for i, block_ref in enumerate((first_ref, second_ref)):
        part = slice(i * size, (i + 1) * size)
        total = near_ref[part, :] + jnp.dot(block_ref[...], weight_ref[...], preferred_element_type=jnp.float32)

        def give(kept, given):
            kept_ref[part, :] = total[:, kept]
            given_ref[part, :] = total[:, given].astype(jnp.bfloat16)

        pl.when(core == 0)(lambda: give(low, high))
        pl.when(core == 1)(lambda: give(high, low))


def project_far(blocks, weight, near):
    rows, wide = near.shape
    return pl.pallas_call(
        far_kernel,
        out_shape=[jax.ShapeDtypeStruct((rows, wide // 2), t) for t in (jnp.float32, jnp.bfloat16)],
        in_specs=[VMEM] * 4,
        out_specs=[VMEM, VMEM],
        compiler_params=params(),
        name="project_far",
    )(*blocks, weight, near)


def join_kernel(*refs):
    out_ref = refs[-1]
    done = 0
    for kept, taken in zip(refs[0:-1:2], refs[1:-1:2]):
        size = kept.shape[0]
        out_ref[done : done + size, :] = (kept[...] + taken[...].astype(jnp.float32)).astype(jnp.bfloat16)
        done += size


def join(*parts):
    rows, columns = sum(part.shape[0] for part in parts[::2]), parts[0].shape[1]
    return pl.pallas_call(
        join_kernel,
        out_shape=jax.ShapeDtypeStruct((rows, columns), jnp.bfloat16),
        in_specs=[VMEM] * len(parts),
        out_specs=VMEM,
        compiler_params=params(),
        name="join",
    )(*parts)


def after(value, *others):
    return lax.optimization_barrier((value, others))[0]


def body(queries, keys, values, out_weight, doc_lengths):
    rows = queries.shape[0]
    seq_size = lax.axis_size("seq")
    head_size = lax.axis_size("head")
    chips = head_size // 2
    def next_block(block):
        return lax.ppermute(block, "seq", [(i, (i + 1) % seq_size) for i in range(seq_size)])

    def back(block, distance):
        return lax.ppermute(block, "seq", [(i, i - i % ROW + (i - distance) % ROW) for i in range(seq_size)])

    def four_on(block):
        owners = [i - i % ROW + (i + 3) % ROW for i in range(seq_size)]
        return lax.ppermute(block, "seq", [(i, (owner + 4) % seq_size) for i, owner in enumerate(owners)])

    def chip_shift(block, distance):
        route = [(i, (i + 2 * distance) % head_size) for i in range(head_size)]
        return lax.ppermute(block, "head", route)

    def swap(block):
        return lax.ppermute(block, "head", [(i, i ^ 1) for i in range(head_size)])

    k1, v1 = next_block(keys), next_block(values)
    far = back(pack(keys, values), 1)
    *state, stack, start_rows, bounds = attend_first(doc_lengths, queries, keys, values)
    k2, v2 = next_block(after(k1, state[1], v1)), next_block(after(v1, state[1]))
    blocks = cut(after(out_weight, k1, state[1], far), chips)
    far = back(after(far, v1), 2)
    weights = {0: blocks[0], 1: chip_shift(after(blocks[1], v1), 1), 3: chip_shift(after(blocks[3], v1), 3)}
    state = attend_middle(1, bounds, start_rows, stack, k1, v1, state)
    k3, v3 = next_block(after(k2, state[1])), next_block(after(v2, state[1]))
    weights[2] = chip_shift(after(blocks[2], state[1], weights[1]), 2)
    bounds = after(bounds, weights[1], weights[3], far)
    far = four_on(far)
    state = attend_middle(2, bounds, start_rows, stack, k2, v2, state)
    late = attend_last("late", bounds, start_rows, stack, rows, (k3, v3, far, *state))
    k4, v4 = (after(block, state[1], late)[:SPLIT] for block in (k3, v3))
    first_far = next_block(jnp.concatenate([k4, v4], axis=1))
    bounds = after(bounds, late, weights[2])
    early_state = attend_last("early", bounds, start_rows, stack, rows, (k3, v3, far, *state), 0)

    def sides(block):
        return chip_shift(block, 1), chip_shift(block, -1)

    def forwarded(before, behind):
        middle = before.shape[0] // 2
        return chip_shift(before[:middle], 1), chip_shift(behind[middle:], -1)

    near_weights = (weights[0], weights[1], weights[3])
    late_sides = sides(late)
    early = attend_last("final", bounds, start_rows, stack, rows, (first_far, *early_state))
    early_sides = sides(early)
    late_far = forwarded(*late_sides)
    late_near = project_near(late, *late_sides, *near_weights)
    early_far = forwarded(*early_sides)
    early_near = project_near(early, *early_sides, *near_weights)
    late_kept, late_given = project_far(late_far, weights[2], late_near)
    late_taken = swap(late_given)
    early_kept, early_given = project_far(early_far, weights[2], early_near)
    early_taken = swap(early_given)
    return join(early_kept, early_taken, late_kept, late_taken)


def solution(mesh):
    return jax.shard_map(
        body,
        mesh=mesh,
        in_specs=(P("seq", "head"), P("seq", "head"), P("seq", "head"), P("head", None), P()),
        out_specs=P("seq", "head"),
        check_vma=False,
    )
```

```python
import functools

import jax
import jax.numpy as jnp
from jax import lax
from jax.experimental import pallas as pl
from jax.experimental.pallas import tpu as pltpu
from jax.sharding import PartitionSpec as P

HD = 128
ROW = 8
TFIRST = 256
TQ = 512
TK = 512
SPLIT = 512
LATE_TILES = (256, 256)
EARLY_TILES = (256, 256)
LOG2E = 1.4426950408889634
SCALE = LOG2E / HD**0.5
MASKED = -1e30
LOWEST = -1e29
VMEM = pl.BlockSpec(memory_space=pltpu.VMEM)
SMEM = pl.BlockSpec(memory_space=pltpu.SMEM)
HBM = pl.BlockSpec(memory_space=pltpu.HBM)
NT = (((1,), (1,)), ((), ()))


def put_scores(score_ref, row, query, key_ref, k0, count):
    for j in range(0, count, TK):
        n = min(TK, count - j)
        score_ref[row + j : row + j + n, :] = lax.dot_general(
            key_ref[k0 + j : k0 + j + n, :], query, NT, preferred_element_type=jnp.float32
        )


def add_keys(score_ref, row, count, turned_ref, v0, old_max, old_sum, old_acc, start_row=None, q0=None):
    size = score_ref.shape[1]

    def piece(j, n):
        scores = score_ref[row + j : row + j + n, :]
        if start_row is None:
            return scores
        key_pos = j + lax.broadcasted_iota(jnp.int32, (n, size), 0)
        visible = key_pos >= start_row
        if q0 is not None and j + n > q0 + 1:
            visible = visible & (key_pos <= q0 + lax.broadcasted_iota(jnp.int32, (n, size), 1))
        return jnp.where(visible, scores, MASKED)

    pieces = [(j, min(TK, count - j)) for j in range(0, count, TK)]
    new_max = old_max
    for j, n in pieces:
        new_max = jnp.maximum(new_max, jnp.max(piece(j, n), axis=0, keepdims=True))
    rescale = jnp.exp2((old_max - new_max) * SCALE)
    total = old_sum * rescale
    acc = old_acc * rescale
    for j, n in pieces:
        probs = jnp.exp2((piece(j, n) - new_max) * SCALE)
        total = total + jnp.sum(probs, axis=0, keepdims=True)
        acc = acc + jnp.dot(
            turned_ref[:, v0 + j : v0 + j + n], probs.astype(jnp.bfloat16), preferred_element_type=jnp.float32
        )
    return new_max, total, acc


def sweep(steps, first, key_ref, k0, count, turned_ref, v0, state, q_ref, score_refs, start_row):
    acc_ref, stat_ref = state

    def make(i):
        q_at, _ = first(i)
        put_scores(score_refs[i % 2], 0, q_ref[pl.ds(q_at, TQ), :], key_ref, k0, count)

    def use(i):
        columns = pl.ds(first(i)[1], TQ)
        start = None if start_row is None else start_row(i)
        stat_ref[0:1, columns], stat_ref[1:2, columns], acc_ref[:, columns] = add_keys(
            score_refs[i % 2], 0, count, turned_ref, v0, stat_ref[0:1, columns], stat_ref[1:2, columns],
            acc_ref[:, columns], start,
        )

    make(0)
    for i in range(steps):
        if i + 1 < steps:
            make(i + 1)
        use(i)


def first_kernel(
    rows, group, docs, length_ref, q_hbm, k_hbm, v_hbm,
    acc_ref, stat_ref, stack_ref, start_ref, bound_ref,
    q_ref, k_ref, v_ref, vt_ref, score_ref, sem,
):
    copies = [
        pltpu.make_async_copy(source, target, sem.at[i])
        for i, (source, target) in enumerate(((q_hbm, q_ref), (k_hbm, k_ref), (v_hbm, v_ref)))
    ]
    for copy in copies:
        copy.start()
    first_row = lax.axis_index("seq") * rows
    tiles = range(0, rows, TFIRST)
    marks = [first_row, first_row + SPLIT, first_row + rows - 1]
    positions = first_row + lax.broadcasted_iota(jnp.int32, (1, rows), 1)

    def document(d, carried):
        begin, row_starts, found = carried
        row_starts = jnp.where(positions >= begin, begin, row_starts)
        found = [jnp.where(mark >= begin, begin, old) for mark, old in zip(marks, found)]
        return begin + length_ref[d], row_starts, found

    zero = jnp.int32(0)
    _, row_starts, found = lax.fori_loop(
        0, docs, document, (zero, jnp.zeros((1, rows), jnp.int32), [zero for _ in marks])
    )
    start_ref[0:1, :] = row_starts
    start_ref[1:8, :] = jnp.zeros((7, rows), jnp.int32)
    bound_ref[0] = first_row
    for i, value in enumerate(found):
        bound_ref[1 + i] = value
    for i in range(len(found) + 1, 8):
        bound_ref[i] = zero
    for copy in copies:
        copy.wait()
    vt_ref[...] = v_ref[...].T
    for h in range(group):
        stack_ref[h * rows : (h + 1) * rows, :] = q_ref[:, h * HD : (h + 1) * HD]
    stat_ref[...] = jnp.zeros_like(stat_ref)
    offsets = {}
    used = 0
    for q0 in tiles:
        offsets[q0] = used
        used += q0 + TFIRST

    def head(h, carried):
        base = pl.multiple_of(h * rows, rows)

        def make(q0):
            put_scores(score_ref, offsets[q0], stack_ref[pl.ds(base + q0, TFIRST), :], k_ref, 0, q0 + TFIRST)

        def use(q0):
            columns = pl.ds(base + q0, TFIRST)
            start = start_ref[0:1, q0 : q0 + TFIRST] - first_row
            lowest = jnp.full((1, TFIRST), LOWEST, jnp.float32)
            none = jnp.zeros((1, TFIRST), jnp.float32)
            stat_ref[0:1, columns], stat_ref[1:2, columns], acc_ref[:, columns] = add_keys(
                score_ref, offsets[q0], q0 + TFIRST, vt_ref, 0, lowest, none, jnp.zeros((HD, TFIRST), jnp.float32), start, q0
            )

        order = list(reversed(tiles))
        make(order[0])
        for i, q0 in enumerate(order):
            if i + 1 < len(order):
                make(order[i + 1])
            use(q0)
        return carried

    lax.fori_loop(0, group, head, 0)


def middle_kernel(
    distance, rows, group, bound_ref, start_ref, q_ref, k_ref, v_ref, acc_in, stat_in, acc_ref, stat_ref, vt_ref, *score_refs
):
    acc_ref[...] = acc_in[...]
    stat_ref[...] = stat_in[...]
    first_key = bound_ref[0] - distance * rows
    needed = (bound_ref[1] < first_key + rows) & (first_key >= 0)
    inside = bound_ref[3] > first_key
    tiles = rows // TQ

    def work(masked):
        vt_ref[...] = v_ref[...].T

        def head(h, carried):
            def first(i):
                return (pl.multiple_of(h * rows + i * TQ, TQ),) * 2

            def start_row(i):
                return start_ref[0:1, i * TQ : (i + 1) * TQ] - first_key

            sweep(
                tiles, first, k_ref, 0, rows, vt_ref, 0, (acc_ref, stat_ref), q_ref, score_refs, start_row if masked else None
            )
            return carried

        lax.fori_loop(0, group, head, 0)

    pl.when(needed & jnp.logical_not(inside))(lambda: work(False))
    pl.when(needed & inside)(lambda: work(True))


def add_block(tiles, base, rows, group, q_ref, start_ref, acc_ref, stat_ref, vt_ref, score_refs, key_ref, v_block, key_count, first_key, masked, skipped):
    size = sum(tiles)
    offsets = [sum(tiles[:i]) for i in range(len(tiles))]
    vt_ref[:, :key_count] = v_block().T

    def head(h, carried):
        for i, (at, width) in enumerate(zip(offsets, tiles)):
            skip = skipped(at)
            query = q_ref[pl.ds(pl.multiple_of(h * rows + base + at, 128), width), :]
            put_scores(score_refs[i], 0, query, key_ref, skip, key_count - skip)
        for i, (at, width) in enumerate(zip(offsets, tiles)):
            skip = skipped(at)
            columns = pl.ds(pl.multiple_of(h * size + at, 128), width)
            start = start_ref[0:1, base + at : base + at + width] - (first_key + skip) if masked else None
            stat_ref[0:1, columns], stat_ref[1:2, columns], acc_ref[:, columns] = add_keys(
                score_refs[i], 0, key_count - skip, vt_ref, skip, stat_ref[0:1, columns], stat_ref[1:2, columns],
                acc_ref[:, columns], start,
            )
        return carried

    lax.fori_loop(0, group, head, 0)


def near_part(late, rows, group, bound_ref, start_ref, q_ref, k_ref, v_ref, far_ref, acc_in, stat_in, acc_ref, stat_ref, vt_ref, score_refs):
    base, tiles = (SPLIT, LATE_TILES) if late else (0, EARLY_TILES)
    size = sum(tiles)
    for h in range(group):
        acc_ref[:, h * size : (h + 1) * size] = acc_in[:, h * rows + base : h * rows + base + size]
        stat_ref[:, h * size : (h + 1) * size] = stat_in[:, h * rows + base : h * rows + base + size]
    block = functools.partial(add_block, tiles, base, rows, group, q_ref, start_ref, acc_ref, stat_ref, vt_ref, score_refs)
    near_key = bound_ref[0] - 3 * rows
    lowest = bound_ref[2] if late else bound_ref[1]
    needed = (lowest < near_key + rows) & (near_key >= 0)
    inside = bound_ref[3] > near_key
    pl.when(needed & jnp.logical_not(inside))(lambda: block(k_ref, lambda: v_ref[...], rows, near_key, False, lambda at: 0))
    pl.when(needed & inside)(lambda: block(k_ref, lambda: v_ref[...], rows, near_key, True, lambda at: 0))
    far_key = near_key - rows
    pl.when((lowest < far_key + rows) & (far_key >= 0))(
        lambda: block(
            far_ref.at[:, :HD], lambda: far_ref[:, HD:], rows - SPLIT, far_key + SPLIT, True, lambda at: at if late else 0
        )
    )


def give_rows(group, acc_ref, stat_ref, out_ref):
    size = out_ref.shape[0]
    for h in range(group):
        columns = slice(h * size, (h + 1) * size)
        scaled = acc_ref[:, columns] / stat_ref[1:2, columns]
        out_ref[:, h * HD : (h + 1) * HD] = scaled.T.astype(jnp.bfloat16)


def late_kernel(rows, group, bound_ref, start_ref, q_ref, k_ref, v_ref, far_ref, acc_in, stat_in, out_ref, acc_ref, stat_ref, vt_ref, *score_refs):
    near_part(
        True, rows, group, bound_ref, start_ref, q_ref, k_ref, v_ref, far_ref, acc_in, stat_in, acc_ref, stat_ref, vt_ref, score_refs
    )
    give_rows(group, acc_ref, stat_ref, out_ref)


def early_kernel(rows, group, bound_ref, start_ref, q_ref, k_ref, v_ref, far_ref, acc_in, stat_in, acc_ref, stat_ref, vt_ref, *score_refs):
    near_part(
        False, rows, group, bound_ref, start_ref, q_ref, k_ref, v_ref, far_ref, acc_in, stat_in, acc_ref, stat_ref, vt_ref, score_refs
    )


def final_kernel(rows, group, bound_ref, start_ref, q_ref, far_ref, acc_in, stat_in, out_ref, acc_ref, stat_ref, vt_ref, *score_refs):
    acc_ref[...] = acc_in[...]
    stat_ref[...] = stat_in[...]
    far_key = bound_ref[0] - 4 * rows
    pl.when((bound_ref[1] < far_key + SPLIT) & (far_key >= 0))(
        lambda: add_block(
            EARLY_TILES, 0, rows, group, q_ref, start_ref, acc_ref, stat_ref, vt_ref, score_refs,
            far_ref.at[:, :HD], lambda: far_ref[:, HD:], SPLIT, far_key, True, lambda at: at,
        )
    )
    give_rows(group, acc_ref, stat_ref, out_ref)


def cost(rows, keys, columns, weight=0):
    return pl.CostEstimate(flops=4 * weight * rows * keys * columns, bytes_accessed=6 * weight * rows * columns, transcendentals=weight * rows * keys * 3)


def params(mebibytes=32):
    return pltpu.CompilerParams(vmem_limit_bytes=mebibytes * 2**20)


def attend_first(doc_lengths, queries, keys, values):
    rows, columns = queries.shape
    group = columns // HD
    tiles = rows // TFIRST
    return pl.pallas_call(
        functools.partial(first_kernel, rows, group, doc_lengths.shape[0]),
        out_shape=[
            jax.ShapeDtypeStruct((HD, group * rows), jnp.float32),
            jax.ShapeDtypeStruct((8, group * rows), jnp.float32),
            jax.ShapeDtypeStruct((group * rows, HD), jnp.bfloat16),
            jax.ShapeDtypeStruct((8, rows), jnp.int32),
            jax.ShapeDtypeStruct((8,), jnp.int32),
        ],
        in_specs=[SMEM, HBM, HBM, HBM],
        out_specs=[VMEM, VMEM, VMEM, VMEM, SMEM],
        scratch_shapes=[
            pltpu.VMEM(queries.shape, jnp.bfloat16),
            pltpu.VMEM(keys.shape, jnp.bfloat16),
            pltpu.VMEM(values.shape, jnp.bfloat16),
            pltpu.VMEM((HD, rows), jnp.bfloat16),
            pltpu.VMEM((TFIRST * tiles * (tiles + 1) // 2, TFIRST), jnp.float32),
            pltpu.SemaphoreType.DMA((3,)),
        ],
        compiler_params=params(60),
        cost_estimate=cost(rows, rows, columns, 1),
        name="attend_first",
    )(doc_lengths, queries, keys, values)


def attend_middle(distance, bounds, start_rows, stack, keys, values, state):
    rows = keys.shape[0]
    group = stack.shape[0] // rows
    return pl.pallas_call(
        functools.partial(middle_kernel, distance, rows, group),
        out_shape=[jax.ShapeDtypeStruct(s.shape, s.dtype) for s in state],
        in_specs=[SMEM] + [VMEM] * 6,
        out_specs=[VMEM, VMEM],
        scratch_shapes=[pltpu.VMEM((HD, rows), jnp.bfloat16)] + [pltpu.VMEM((rows, TQ), jnp.float32)] * 2,
        input_output_aliases={5: 0, 6: 1},
        compiler_params=params(),
        cost_estimate=cost(rows, rows, group * HD),
        name=f"attend_{distance}",
    )(bounds, start_rows, stack, keys, values, *state)


def attend_last(kind, bounds, start_rows, stack, rows, arrays, weight=0):
    kernel, tiles = {
        "late": (late_kernel, LATE_TILES),
        "early": (early_kernel, EARLY_TILES),
        "final": (final_kernel, EARLY_TILES),
    }[kind]
    size = sum(tiles)
    group = stack.shape[0] // rows
    state = [(HD, group * size), (8, group * size)]
    work = [pltpu.VMEM((HD, rows), jnp.bfloat16)] + [pltpu.VMEM((rows, tile), jnp.float32) for tile in tiles]
    if kind == "early":
        out = [jax.ShapeDtypeStruct(shape, jnp.float32) for shape in state]
    else:
        out = jax.ShapeDtypeStruct((size, group * HD), jnp.bfloat16)
        work = [pltpu.VMEM(shape, jnp.float32) for shape in state] + work
    return pl.pallas_call(
        functools.partial(kernel, rows, group),
        out_shape=out,
        in_specs=[SMEM] + [VMEM] * (2 + len(arrays)),
        out_specs=[VMEM, VMEM] if kind == "early" else VMEM,
        scratch_shapes=work,
        compiler_params=params(),
        cost_estimate=cost(size, rows, group * HD, weight),
        name="attend_" + kind,
    )(bounds, start_rows, stack, *arrays)


def pack_kernel(k_hbm, v_hbm, far_ref, sem):
    late = far_ref.shape[0]
    copies = [
        pltpu.make_async_copy(source.at[pl.ds(SPLIT, late), :], far_ref.at[:, part], sem.at[i])
        for i, (source, part) in enumerate(((k_hbm, slice(0, HD)), (v_hbm, slice(HD, 2 * HD))))
    ]
    for copy in copies:
        copy.start()
    for copy in copies:
        copy.wait()


def pack(keys, values):
    return pl.pallas_call(
        pack_kernel,
        out_shape=jax.ShapeDtypeStruct((keys.shape[0] - SPLIT, 2 * HD), keys.dtype),
        in_specs=[HBM, HBM],
        out_specs=VMEM,
        scratch_shapes=[pltpu.SemaphoreType.DMA((2,))],
        compiler_params=params(),
        name="pack",
    )(keys, values)


def cut_kernel(chips, weight_hbm, *refs):
    weight_refs, sem = refs[:chips], refs[-1]
    wide = weight_refs[0].shape[1]
    chip = lax.axis_index("head") // 2
    copies = []
    for d in (1, 3, 2, 0):
        column = pl.multiple_of(lax.rem(chip + d, chips) * wide, wide)
        copies.append(pltpu.make_async_copy(weight_hbm.at[:, pl.ds(column, wide)], weight_refs[d], sem.at[d]))
    for copy in copies:
        copy.start()
    for copy in copies:
        copy.wait()


def cut(out_weight, chips):
    rows, columns = out_weight.shape
    block = jax.ShapeDtypeStruct((rows, columns // chips), out_weight.dtype)
    return pl.pallas_call(
        functools.partial(cut_kernel, chips),
        out_shape=[block] * chips,
        in_specs=[HBM],
        out_specs=[VMEM] * chips,
        scratch_shapes=[pltpu.SemaphoreType.DMA((chips,))],
        compiler_params=params(),
        name="cut",
    )(out_weight)


def near_kernel(own_ref, before_ref, after_ref, w0_ref, w1_ref, w3_ref, out_ref):
    block = jnp.concatenate([own_ref[...], before_ref[...], after_ref[...]], axis=1)
    weight = jnp.concatenate([w0_ref[...], w1_ref[...], w3_ref[...]], axis=0)
    out_ref[...] = jnp.dot(block, weight, preferred_element_type=jnp.float32)


def project_near(*operands):
    size, wide = operands[0].shape[0], operands[3].shape[1]
    return pl.pallas_call(
        near_kernel,
        out_shape=jax.ShapeDtypeStruct((size, wide), jnp.float32),
        in_specs=[VMEM] * 6,
        out_specs=VMEM,
        compiler_params=params(),
        name="project_near",
    )(*operands)


def far_kernel(first_ref, second_ref, weight_ref, near_ref, kept_ref, given_ref):
    size, columns = first_ref.shape
    core = lax.axis_index("head") % 2
    low, high = slice(0, columns), slice(columns, None)
    for i, block_ref in enumerate((first_ref, second_ref)):
        part = slice(i * size, (i + 1) * size)
        total = near_ref[part, :] + jnp.dot(block_ref[...], weight_ref[...], preferred_element_type=jnp.float32)

        def give(kept, given):
            kept_ref[part, :] = total[:, kept]
            given_ref[part, :] = total[:, given].astype(jnp.bfloat16)

        pl.when(core == 0)(lambda: give(low, high))
        pl.when(core == 1)(lambda: give(high, low))


def project_far(blocks, weight, near):
    rows, wide = near.shape
    return pl.pallas_call(
        far_kernel,
        out_shape=[jax.ShapeDtypeStruct((rows, wide // 2), t) for t in (jnp.float32, jnp.bfloat16)],
        in_specs=[VMEM] * 4,
        out_specs=[VMEM, VMEM],
        compiler_params=params(),
        name="project_far",
    )(*blocks, weight, near)


def join_kernel(*refs):
    out_ref = refs[-1]
    done = 0
    for kept, taken in zip(refs[0:-1:2], refs[1:-1:2]):
        size = kept.shape[0]
        out_ref[done : done + size, :] = (kept[...] + taken[...].astype(jnp.float32)).astype(jnp.bfloat16)
        done += size


def join(*parts):
    rows, columns = sum(part.shape[0] for part in parts[::2]), parts[0].shape[1]
    return pl.pallas_call(
        join_kernel,
        out_shape=jax.ShapeDtypeStruct((rows, columns), jnp.bfloat16),
        in_specs=[VMEM] * len(parts),
        out_specs=VMEM,
        compiler_params=params(),
        name="join",
    )(*parts)


def after(value, *others):
    return lax.optimization_barrier((value, others))[0]


def body(queries, keys, values, out_weight, doc_lengths):
    rows = queries.shape[0]
    seq_size = lax.axis_size("seq")
    head_size = lax.axis_size("head")
    chips = head_size // 2
    def next_block(block):
        return lax.ppermute(block, "seq", [(i, (i + 1) % seq_size) for i in range(seq_size)])

    def back(block, distance):
        return lax.ppermute(block, "seq", [(i, i - i % ROW + (i - distance) % ROW) for i in range(seq_size)])

    def four_on(block):
        owners = [i - i % ROW + (i + 3) % ROW for i in range(seq_size)]
        return lax.ppermute(block, "seq", [(i, (owner + 4) % seq_size) for i, owner in enumerate(owners)])

    def chip_shift(block, distance):
        route = [(i, (i + 2 * distance) % head_size) for i in range(head_size)]
        return lax.ppermute(block, "head", route)

    def swap(block):
        return lax.ppermute(block, "head", [(i, i ^ 1) for i in range(head_size)])

    k1, v1 = next_block(keys), next_block(values)
    far = back(pack(keys, values), 1)
    *state, stack, start_rows, bounds = attend_first(doc_lengths, queries, keys, values)
    k2, v2 = next_block(after(k1, state[1], v1)), next_block(after(v1, state[1]))
    blocks = cut(after(out_weight, k1, state[1], far), chips)
    far = back(after(far, v1), 2)
    weights = {0: blocks[0], 1: chip_shift(after(blocks[1], v1), 1), 3: chip_shift(after(blocks[3], v1), 3)}
    state = attend_middle(1, bounds, start_rows, stack, k1, v1, state)
    k3, v3 = next_block(after(k2, state[1])), next_block(after(v2, state[1]))
    weights[2] = chip_shift(after(blocks[2], state[1], weights[1]), 2)
    bounds = after(bounds, weights[1], weights[3], far)
    far = four_on(far)
    state = attend_middle(2, bounds, start_rows, stack, k2, v2, state)
    late = attend_last("late", bounds, start_rows, stack, rows, (k3, v3, far, *state))
    k4, v4 = (after(block, state[1], late)[:SPLIT] for block in (k3, v3))
    first_far = next_block(jnp.concatenate([k4, v4], axis=1))
    bounds = after(bounds, late, weights[2])
    early_state = attend_last("early", bounds, start_rows, stack, rows, (k3, v3, far, *state), 0)

    def sides(block):
        return chip_shift(block, 1), chip_shift(block, -1)

    def forwarded(before, behind):
        middle = before.shape[0] // 2
        return chip_shift(before[:middle], 1), chip_shift(behind[middle:], -1)

    near_weights = (weights[0], weights[1], weights[3])
    late_sides = sides(late)
    early = attend_last("final", bounds, start_rows, stack, rows, (first_far, *early_state))
    early_sides = sides(early)
    late_far = forwarded(*late_sides)
    late_near = project_near(late, *late_sides, *near_weights)
    early_far = forwarded(*early_sides)
    early_near = project_near(early, *early_sides, *near_weights)
    late_kept, late_given = project_far(late_far, weights[2], late_near)
    late_taken = swap(late_given)
    early_kept, early_given = project_far(early_far, weights[2], early_near)
    early_taken = swap(early_given)
    return join(early_kept, early_taken, late_kept, late_taken)


def solution(mesh):
    return jax.shard_map(
        body,
        mesh=mesh,
        in_specs=(P("seq", "head"), P("seq", "head"), P("seq", "head"), P("head", None), P()),
        out_specs=P("seq", "head"),
        check_vma=False,
    )
```

```python
import functools

import jax
import jax.numpy as jnp
from jax import lax
from jax.experimental import pallas as pl
from jax.experimental.pallas import tpu as pltpu
from jax.sharding import PartitionSpec as P

HD = 128
ROW = 8
TFIRST = 256
TQ = 512
TK = 512
SPLIT = 512
LATE_TILES = (256, 256)
EARLY_TILES = (256, 256)
LOG2E = 1.4426950408889634
SCALE = LOG2E / HD**0.5
MASKED = -1e30
LOWEST = -1e29
VMEM = pl.BlockSpec(memory_space=pltpu.VMEM)
SMEM = pl.BlockSpec(memory_space=pltpu.SMEM)
HBM = pl.BlockSpec(memory_space=pltpu.HBM)
NT = (((1,), (1,)), ((), ()))


def put_scores(score_ref, row, query, key_ref, k0, count):
    for j in range(0, count, TK):
        n = min(TK, count - j)
        score_ref[row + j : row + j + n, :] = lax.dot_general(
            key_ref[k0 + j : k0 + j + n, :], query, NT, preferred_element_type=jnp.float32
        )


def add_keys(score_ref, row, count, turned_ref, v0, old_max, old_sum, old_acc, start_row=None, q0=None):
    size = score_ref.shape[1]

    def piece(j, n):
        scores = score_ref[row + j : row + j + n, :]
        if start_row is None:
            return scores
        key_pos = j + lax.broadcasted_iota(jnp.int32, (n, size), 0)
        visible = key_pos >= start_row
        if q0 is not None and j + n > q0 + 1:
            visible = visible & (key_pos <= q0 + lax.broadcasted_iota(jnp.int32, (n, size), 1))
        return jnp.where(visible, scores, MASKED)

    pieces = [(j, min(TK, count - j)) for j in range(0, count, TK)]
    new_max = old_max
    for j, n in pieces:
        new_max = jnp.maximum(new_max, jnp.max(piece(j, n), axis=0, keepdims=True))
    rescale = jnp.exp2((old_max - new_max) * SCALE)
    total = old_sum * rescale
    acc = old_acc * rescale
    for j, n in pieces:
        probs = jnp.exp2((piece(j, n) - new_max) * SCALE)
        total = total + jnp.sum(probs, axis=0, keepdims=True)
        acc = acc + jnp.dot(
            turned_ref[:, v0 + j : v0 + j + n], probs.astype(jnp.bfloat16), preferred_element_type=jnp.float32
        )
    return new_max, total, acc


def sweep(steps, first, key_ref, k0, count, turned_ref, v0, state, q_ref, score_refs, start_row):
    acc_ref, stat_ref = state

    def make(i):
        q_at, _ = first(i)
        put_scores(score_refs[i % 2], 0, q_ref[pl.ds(q_at, TQ), :], key_ref, k0, count)

    def use(i):
        columns = pl.ds(first(i)[1], TQ)
        start = None if start_row is None else start_row(i)
        stat_ref[0:1, columns], stat_ref[1:2, columns], acc_ref[:, columns] = add_keys(
            score_refs[i % 2], 0, count, turned_ref, v0, stat_ref[0:1, columns], stat_ref[1:2, columns],
            acc_ref[:, columns], start,
        )

    make(0)
    for i in range(steps):
        if i + 1 < steps:
            make(i + 1)
        use(i)


def first_kernel(
    rows, group, docs, length_ref, q_hbm, k_hbm, v_hbm,
    acc_ref, stat_ref, stack_ref, start_ref, bound_ref,
    q_ref, k_ref, v_ref, vt_ref, score_ref, sem,
):
    copies = [
        pltpu.make_async_copy(source, target, sem.at[i])
        for i, (source, target) in enumerate(((q_hbm, q_ref), (k_hbm, k_ref), (v_hbm, v_ref)))
    ]
    for copy in copies:
        copy.start()
    first_row = lax.axis_index("seq") * rows
    tiles = range(0, rows, TFIRST)
    marks = [first_row, first_row + SPLIT, first_row + rows - 1]
    positions = first_row + lax.broadcasted_iota(jnp.int32, (1, rows), 1)

    def document(d, carried):
        begin, row_starts, found = carried
        row_starts = jnp.where(positions >= begin, begin, row_starts)
        found = [jnp.where(mark >= begin, begin, old) for mark, old in zip(marks, found)]
        return begin + length_ref[d], row_starts, found

    zero = jnp.int32(0)
    _, row_starts, found = lax.fori_loop(
        0, docs, document, (zero, jnp.zeros((1, rows), jnp.int32), [zero for _ in marks])
    )
    start_ref[0:1, :] = row_starts
    start_ref[1:8, :] = jnp.zeros((7, rows), jnp.int32)
    bound_ref[0] = first_row
    for i, value in enumerate(found):
        bound_ref[1 + i] = value
    for i in range(len(found) + 1, 8):
        bound_ref[i] = zero
    for copy in copies:
        copy.wait()
    vt_ref[...] = v_ref[...].T
    for h in range(group):
        stack_ref[h * rows : (h + 1) * rows, :] = q_ref[:, h * HD : (h + 1) * HD]
    stat_ref[...] = jnp.zeros_like(stat_ref)
    offsets = {}
    used = 0
    for q0 in tiles:
        offsets[q0] = used
        used += q0 + TFIRST

    def head(h, carried):
        base = pl.multiple_of(h * rows, rows)

        def make(q0):
            put_scores(score_ref, offsets[q0], stack_ref[pl.ds(base + q0, TFIRST), :], k_ref, 0, q0 + TFIRST)

        def use(q0):
            columns = pl.ds(base + q0, TFIRST)
            start = start_ref[0:1, q0 : q0 + TFIRST] - first_row
            lowest = jnp.full((1, TFIRST), LOWEST, jnp.float32)
            none = jnp.zeros((1, TFIRST), jnp.float32)
            stat_ref[0:1, columns], stat_ref[1:2, columns], acc_ref[:, columns] = add_keys(
                score_ref, offsets[q0], q0 + TFIRST, vt_ref, 0, lowest, none, jnp.zeros((HD, TFIRST), jnp.float32), start, q0
            )

        order = list(reversed(tiles))
        make(order[0])
        for i, q0 in enumerate(order):
            if i + 1 < len(order):
                make(order[i + 1])
            use(q0)
        return carried

    lax.fori_loop(0, group, head, 0)


def middle_kernel(
    distance, rows, group, bound_ref, start_ref, q_ref, k_ref, v_ref, acc_in, stat_in, acc_ref, stat_ref, vt_ref, *score_refs
):
    acc_ref[...] = acc_in[...]
    stat_ref[...] = stat_in[...]
    first_key = bound_ref[0] - distance * rows
    needed = (bound_ref[1] < first_key + rows) & (first_key >= 0)
    inside = bound_ref[3] > first_key
    tiles = rows // TQ

    def work(masked):
        vt_ref[...] = v_ref[...].T

        def head(h, carried):
            def first(i):
                return (pl.multiple_of(h * rows + i * TQ, TQ),) * 2

            def start_row(i):
                return start_ref[0:1, i * TQ : (i + 1) * TQ] - first_key

            sweep(
                tiles, first, k_ref, 0, rows, vt_ref, 0, (acc_ref, stat_ref), q_ref, score_refs, start_row if masked else None
            )
            return carried

        lax.fori_loop(0, group, head, 0)

    pl.when(needed & jnp.logical_not(inside))(lambda: work(False))
    pl.when(needed & inside)(lambda: work(True))


def add_block(tiles, base, rows, group, q_ref, start_ref, acc_ref, stat_ref, vt_ref, score_refs, key_ref, v_block, key_count, first_key, masked, skipped):
    size = sum(tiles)
    offsets = [sum(tiles[:i]) for i in range(len(tiles))]
    vt_ref[:, :key_count] = v_block().T

    def head(h, carried):
        for i, (at, width) in enumerate(zip(offsets, tiles)):
            skip = skipped(at)
            query = q_ref[pl.ds(pl.multiple_of(h * rows + base + at, 128), width), :]
            put_scores(score_refs[i], 0, query, key_ref, skip, key_count - skip)
        for i, (at, width) in enumerate(zip(offsets, tiles)):
            skip = skipped(at)
            columns = pl.ds(pl.multiple_of(h * size + at, 128), width)
            start = start_ref[0:1, base + at : base + at + width] - (first_key + skip) if masked else None
            stat_ref[0:1, columns], stat_ref[1:2, columns], acc_ref[:, columns] = add_keys(
                score_refs[i], 0, key_count - skip, vt_ref, skip, stat_ref[0:1, columns], stat_ref[1:2, columns],
                acc_ref[:, columns], start,
            )
        return carried

    lax.fori_loop(0, group, head, 0)


def near_part(late, rows, group, bound_ref, start_ref, q_ref, k_ref, v_ref, far_ref, acc_in, stat_in, acc_ref, stat_ref, vt_ref, score_refs):
    base, tiles = (SPLIT, LATE_TILES) if late else (0, EARLY_TILES)
    size = sum(tiles)
    for h in range(group):
        acc_ref[:, h * size : (h + 1) * size] = acc_in[:, h * rows + base : h * rows + base + size]
        stat_ref[:, h * size : (h + 1) * size] = stat_in[:, h * rows + base : h * rows + base + size]
    block = functools.partial(add_block, tiles, base, rows, group, q_ref, start_ref, acc_ref, stat_ref, vt_ref, score_refs)
    near_key = bound_ref[0] - 3 * rows
    lowest = bound_ref[2] if late else bound_ref[1]
    needed = (lowest < near_key + rows) & (near_key >= 0)
    inside = bound_ref[3] > near_key
    pl.when(needed & jnp.logical_not(inside))(lambda: block(k_ref, lambda: v_ref[...], rows, near_key, False, lambda at: 0))
    pl.when(needed & inside)(lambda: block(k_ref, lambda: v_ref[...], rows, near_key, True, lambda at: 0))
    far_key = near_key - rows
    pl.when((lowest < far_key + rows) & (far_key >= 0))(
        lambda: block(
            far_ref.at[:, :HD], lambda: far_ref[:, HD:], rows - SPLIT, far_key + SPLIT, True, lambda at: at if late else 0
        )
    )


def give_rows(group, acc_ref, stat_ref, out_ref):
    size = out_ref.shape[0]
    for h in range(group):
        columns = slice(h * size, (h + 1) * size)
        scaled = acc_ref[:, columns] / stat_ref[1:2, columns]
        out_ref[:, h * HD : (h + 1) * HD] = scaled.T.astype(jnp.bfloat16)


def late_kernel(rows, group, bound_ref, start_ref, q_ref, k_ref, v_ref, far_ref, acc_in, stat_in, out_ref, acc_ref, stat_ref, vt_ref, *score_refs):
    near_part(
        True, rows, group, bound_ref, start_ref, q_ref, k_ref, v_ref, far_ref, acc_in, stat_in, acc_ref, stat_ref, vt_ref, score_refs
    )
    give_rows(group, acc_ref, stat_ref, out_ref)


def early_kernel(rows, group, bound_ref, start_ref, q_ref, k_ref, v_ref, far_ref, acc_in, stat_in, acc_ref, stat_ref, vt_ref, *score_refs):
    near_part(
        False, rows, group, bound_ref, start_ref, q_ref, k_ref, v_ref, far_ref, acc_in, stat_in, acc_ref, stat_ref, vt_ref, score_refs
    )


def final_kernel(rows, group, bound_ref, start_ref, q_ref, far_ref, acc_in, stat_in, out_ref, acc_ref, stat_ref, vt_ref, *score_refs):
    acc_ref[...] = acc_in[...]
    stat_ref[...] = stat_in[...]
    far_key = bound_ref[0] - 4 * rows
    pl.when((bound_ref[1] < far_key + SPLIT) & (far_key >= 0))(
        lambda: add_block(
            EARLY_TILES, 0, rows, group, q_ref, start_ref, acc_ref, stat_ref, vt_ref, score_refs,
            far_ref.at[:, :HD], lambda: far_ref[:, HD:], SPLIT, far_key, True, lambda at: at,
        )
    )
    give_rows(group, acc_ref, stat_ref, out_ref)


def cost(rows, keys, columns, weight=0):
    return pl.CostEstimate(flops=4 * weight * rows * keys * columns, bytes_accessed=6 * weight * rows * columns, transcendentals=weight * rows * keys * 3)


def params(mebibytes=32):
    return pltpu.CompilerParams(vmem_limit_bytes=mebibytes * 2**20)


def attend_first(doc_lengths, queries, keys, values):
    rows, columns = queries.shape
    group = columns // HD
    tiles = rows // TFIRST
    return pl.pallas_call(
        functools.partial(first_kernel, rows, group, doc_lengths.shape[0]),
        out_shape=[
            jax.ShapeDtypeStruct((HD, group * rows), jnp.float32),
            jax.ShapeDtypeStruct((8, group * rows), jnp.float32),
            jax.ShapeDtypeStruct((group * rows, HD), jnp.bfloat16),
            jax.ShapeDtypeStruct((8, rows), jnp.int32),
            jax.ShapeDtypeStruct((8,), jnp.int32),
        ],
        in_specs=[SMEM, HBM, HBM, HBM],
        out_specs=[VMEM, VMEM, VMEM, VMEM, SMEM],
        scratch_shapes=[
            pltpu.VMEM(queries.shape, jnp.bfloat16),
            pltpu.VMEM(keys.shape, jnp.bfloat16),
            pltpu.VMEM(values.shape, jnp.bfloat16),
            pltpu.VMEM((HD, rows), jnp.bfloat16),
            pltpu.VMEM((TFIRST * tiles * (tiles + 1) // 2, TFIRST), jnp.float32),
            pltpu.SemaphoreType.DMA((3,)),
        ],
        compiler_params=params(32),
        cost_estimate=cost(rows, rows, columns, 1),
        name="attend_first",
    )(doc_lengths, queries, keys, values)


def attend_middle(distance, bounds, start_rows, stack, keys, values, state):
    rows = keys.shape[0]
    group = stack.shape[0] // rows
    return pl.pallas_call(
        functools.partial(middle_kernel, distance, rows, group),
        out_shape=[jax.ShapeDtypeStruct(s.shape, s.dtype) for s in state],
        in_specs=[SMEM] + [VMEM] * 6,
        out_specs=[VMEM, VMEM],
        scratch_shapes=[pltpu.VMEM((HD, rows), jnp.bfloat16)] + [pltpu.VMEM((rows, TQ), jnp.float32)] * 2,
        input_output_aliases={5: 0, 6: 1},
        compiler_params=params(),
        cost_estimate=cost(rows, rows, group * HD),
        name=f"attend_{distance}",
    )(bounds, start_rows, stack, keys, values, *state)


def attend_last(kind, bounds, start_rows, stack, rows, arrays, weight=0):
    kernel, tiles = {
        "late": (late_kernel, LATE_TILES),
        "early": (early_kernel, EARLY_TILES),
        "final": (final_kernel, EARLY_TILES),
    }[kind]
    size = sum(tiles)
    group = stack.shape[0] // rows
    state = [(HD, group * size), (8, group * size)]
    work = [pltpu.VMEM((HD, rows), jnp.bfloat16)] + [pltpu.VMEM((rows, tile), jnp.float32) for tile in tiles]
    if kind == "early":
        out = [jax.ShapeDtypeStruct(shape, jnp.float32) for shape in state]
    else:
        out = jax.ShapeDtypeStruct((size, group * HD), jnp.bfloat16)
        work = [pltpu.VMEM(shape, jnp.float32) for shape in state] + work
    return pl.pallas_call(
        functools.partial(kernel, rows, group),
        out_shape=out,
        in_specs=[SMEM] + [VMEM] * (2 + len(arrays)),
        out_specs=[VMEM, VMEM] if kind == "early" else VMEM,
        scratch_shapes=work,
        compiler_params=params(),
        cost_estimate=cost(size, rows, group * HD, weight),
        name="attend_" + kind,
    )(bounds, start_rows, stack, *arrays)


def pack_kernel(k_hbm, v_hbm, far_ref, sem):
    late = far_ref.shape[0]
    copies = [
        pltpu.make_async_copy(source.at[pl.ds(SPLIT, late), :], far_ref.at[:, part], sem.at[i])
        for i, (source, part) in enumerate(((k_hbm, slice(0, HD)), (v_hbm, slice(HD, 2 * HD))))
    ]
    for copy in copies:
        copy.start()
    for copy in copies:
        copy.wait()


def pack(keys, values):
    return pl.pallas_call(
        pack_kernel,
        out_shape=jax.ShapeDtypeStruct((keys.shape[0] - SPLIT, 2 * HD), keys.dtype),
        in_specs=[HBM, HBM],
        out_specs=VMEM,
        scratch_shapes=[pltpu.SemaphoreType.DMA((2,))],
        compiler_params=params(),
        name="pack",
    )(keys, values)


def cut_kernel(chips, weight_hbm, *refs):
    weight_refs, sem = refs[:chips], refs[-1]
    wide = weight_refs[0].shape[1]
    chip = lax.axis_index("head") // 2
    copies = []
    for d in (1, 3, 2, 0):
        column = pl.multiple_of(lax.rem(chip + d, chips) * wide, wide)
        copies.append(pltpu.make_async_copy(weight_hbm.at[:, pl.ds(column, wide)], weight_refs[d], sem.at[d]))
    for copy in copies:
        copy.start()
    for copy in copies:
        copy.wait()


def cut(out_weight, chips):
    rows, columns = out_weight.shape
    block = jax.ShapeDtypeStruct((rows, columns // chips), out_weight.dtype)
    return pl.pallas_call(
        functools.partial(cut_kernel, chips),
        out_shape=[block] * chips,
        in_specs=[HBM],
        out_specs=[VMEM] * chips,
        scratch_shapes=[pltpu.SemaphoreType.DMA((chips,))],
        compiler_params=params(),
        name="cut",
    )(out_weight)


def near_kernel(own_ref, before_ref, after_ref, w0_ref, w1_ref, w3_ref, out_ref):
    block = jnp.concatenate([own_ref[...], before_ref[...], after_ref[...]], axis=1)
    weight = jnp.concatenate([w0_ref[...], w1_ref[...], w3_ref[...]], axis=0)
    out_ref[...] = jnp.dot(block, weight, preferred_element_type=jnp.float32)


def project_near(*operands):
    size, wide = operands[0].shape[0], operands[3].shape[1]
    return pl.pallas_call(
        near_kernel,
        out_shape=jax.ShapeDtypeStruct((size, wide), jnp.float32),
        in_specs=[VMEM] * 6,
        out_specs=VMEM,
        compiler_params=params(),
        name="project_near",
    )(*operands)


def far_kernel(first_ref, second_ref, weight_ref, near_ref, kept_ref, given_ref):
    size, columns = first_ref.shape
    core = lax.axis_index("head") % 2
    low, high = slice(0, columns), slice(columns, None)
    for i, block_ref in enumerate((first_ref, second_ref)):
        part = slice(i * size, (i + 1) * size)
        total = near_ref[part, :] + jnp.dot(block_ref[...], weight_ref[...], preferred_element_type=jnp.float32)

        def give(kept, given):
            kept_ref[part, :] = total[:, kept]
            given_ref[part, :] = total[:, given].astype(jnp.bfloat16)

        pl.when(core == 0)(lambda: give(low, high))
        pl.when(core == 1)(lambda: give(high, low))


def project_far(blocks, weight, near):
    rows, wide = near.shape
    return pl.pallas_call(
        far_kernel,
        out_shape=[jax.ShapeDtypeStruct((rows, wide // 2), t) for t in (jnp.float32, jnp.bfloat16)],
        in_specs=[VMEM] * 4,
        out_specs=[VMEM, VMEM],
        compiler_params=params(),
        name="project_far",
    )(*blocks, weight, near)


def join_kernel(*refs):
    out_ref = refs[-1]
    done = 0
    for kept, taken in zip(refs[0:-1:2], refs[1:-1:2]):
        size = kept.shape[0]
        out_ref[done : done + size, :] = (kept[...] + taken[...].astype(jnp.float32)).astype(jnp.bfloat16)
        done += size


def join(*parts):
    rows, columns = sum(part.shape[0] for part in parts[::2]), parts[0].shape[1]
    return pl.pallas_call(
        join_kernel,
        out_shape=jax.ShapeDtypeStruct((rows, columns), jnp.bfloat16),
        in_specs=[VMEM] * len(parts),
        out_specs=VMEM,
        compiler_params=params(),
        name="join",
    )(*parts)


def after(value, *others):
    return lax.optimization_barrier((value, others))[0]


def body(queries, keys, values, out_weight, doc_lengths):
    rows = queries.shape[0]
    seq_size = lax.axis_size("seq")
    head_size = lax.axis_size("head")
    chips = head_size // 2
    def next_block(block):
        return lax.ppermute(block, "seq", [(i, (i + 1) % seq_size) for i in range(seq_size)])

    def back(block, distance):
        return lax.ppermute(block, "seq", [(i, i - i % ROW + (i - distance) % ROW) for i in range(seq_size)])

    def four_on(block):
        owners = [i - i % ROW + (i + 3) % ROW for i in range(seq_size)]
        return lax.ppermute(block, "seq", [(i, (owner + 4) % seq_size) for i, owner in enumerate(owners)])

    def chip_shift(block, distance):
        route = [(i, (i + 2 * distance) % head_size) for i in range(head_size)]
        return lax.ppermute(block, "head", route)

    def swap(block):
        return lax.ppermute(block, "head", [(i, i ^ 1) for i in range(head_size)])

    k1, v1 = next_block(keys), next_block(values)
    far = back(pack(keys, values), 1)
    *state, stack, start_rows, bounds = attend_first(doc_lengths, queries, keys, values)
    k2, v2 = next_block(after(k1, state[1], v1)), next_block(after(v1, state[1]))
    blocks = cut(after(out_weight, k1, state[1], far), chips)
    far = back(after(far, v1), 2)
    weights = {0: blocks[0], 1: chip_shift(after(blocks[1], v1), 1), 3: chip_shift(after(blocks[3], v1), 3)}
    state = attend_middle(1, bounds, start_rows, stack, k1, v1, state)
    k3, v3 = next_block(after(k2, state[1])), next_block(after(v2, state[1]))
    weights[2] = chip_shift(after(blocks[2], state[1], weights[1]), 2)
    bounds = after(bounds, weights[1], weights[3], far)
    far = four_on(far)
    state = attend_middle(2, bounds, start_rows, stack, k2, v2, state)
    late = attend_last("late", bounds, start_rows, stack, rows, (k3, v3, far, *state))
    k4, v4 = (after(block, state[1])[:SPLIT] for block in (k3, v3))
    first_far = next_block(jnp.concatenate([k4, v4], axis=1))
    bounds = after(bounds, late, weights[2], first_far)
    early_state = attend_last("early", bounds, start_rows, stack, rows, (k3, v3, far, *state), 0)

    def sides(block):
        return chip_shift(block, 1), chip_shift(block, -1)

    def forwarded(before, behind):
        middle = before.shape[0] // 2
        return chip_shift(before[:middle], 1), chip_shift(behind[middle:], -1)

    near_weights = (weights[0], weights[1], weights[3])
    late_sides = sides(late)
    early = attend_last("final", bounds, start_rows, stack, rows, (first_far, *early_state))
    early_sides = sides(early)
    late_far = forwarded(*late_sides)
    late_near = project_near(late, *late_sides, *near_weights)
    early_far = forwarded(*early_sides)
    early_near = project_near(early, *early_sides, *near_weights)
    late_kept, late_given = project_far(late_far, weights[2], late_near)
    late_taken = swap(late_given)
    early_kept, early_given = project_far(early_far, weights[2], early_near)
    early_taken = swap(early_given)
    return join(early_kept, early_taken, late_kept, late_taken)


def solution(mesh):
    return jax.shard_map(
        body,
        mesh=mesh,
        in_specs=(P("seq", "head"), P("seq", "head"), P("seq", "head"), P("head", None), P()),
        out_specs=P("seq", "head"),
        check_vma=False,
    )
```

```python
import functools

import jax
import jax.numpy as jnp
from jax import lax
from jax.experimental import pallas as pl
from jax.experimental.pallas import tpu as pltpu
from jax.sharding import PartitionSpec as P

HD = 128
ROW = 8
TFIRST = 256
TQ = 512
TK = 512
SPLIT = 512
LATE_TILES = (256, 256)
EARLY_TILES = (256, 256)
LOG2E = 1.4426950408889634
SCALE = LOG2E / HD**0.5
MASKED = -1e30
LOWEST = -1e29
VMEM = pl.BlockSpec(memory_space=pltpu.VMEM)
SMEM = pl.BlockSpec(memory_space=pltpu.SMEM)
HBM = pl.BlockSpec(memory_space=pltpu.HBM)
NT = (((1,), (1,)), ((), ()))


def put_scores(score_ref, row, query, key_ref, k0, count):
    for j in range(0, count, TK):
        n = min(TK, count - j)
        score_ref[row + j : row + j + n, :] = lax.dot_general(
            key_ref[k0 + j : k0 + j + n, :], query, NT, preferred_element_type=jnp.float32
        )


def add_keys(score_ref, row, count, turned_ref, v0, old_max, old_sum, old_acc, start_row=None, q0=None):
    size = score_ref.shape[1]

    def piece(j, n):
        scores = score_ref[row + j : row + j + n, :]
        if start_row is None:
            return scores
        key_pos = j + lax.broadcasted_iota(jnp.int32, (n, size), 0)
        visible = key_pos >= start_row
        if q0 is not None and j + n > q0 + 1:
            visible = visible & (key_pos <= q0 + lax.broadcasted_iota(jnp.int32, (n, size), 1))
        return jnp.where(visible, scores, MASKED)

    pieces = [(j, min(TK, count - j)) for j in range(0, count, TK)]
    new_max = old_max
    for j, n in pieces:
        new_max = jnp.maximum(new_max, jnp.max(piece(j, n), axis=0, keepdims=True))
    rescale = jnp.exp2((old_max - new_max) * SCALE)
    total = old_sum * rescale
    acc = old_acc * rescale
    for j, n in pieces:
        probs = jnp.exp2((piece(j, n) - new_max) * SCALE)
        total = total + jnp.sum(probs, axis=0, keepdims=True)
        acc = acc + jnp.dot(
            turned_ref[:, v0 + j : v0 + j + n], probs.astype(jnp.bfloat16), preferred_element_type=jnp.float32
        )
    return new_max, total, acc


def sweep(steps, first, key_ref, k0, count, turned_ref, v0, state, q_ref, score_refs, start_row):
    acc_ref, stat_ref = state

    def make(i):
        q_at, _ = first(i)
        put_scores(score_refs[i % 2], 0, q_ref[pl.ds(q_at, TQ), :], key_ref, k0, count)

    def use(i):
        columns = pl.ds(first(i)[1], TQ)
        start = None if start_row is None else start_row(i)
        stat_ref[0:1, columns], stat_ref[1:2, columns], acc_ref[:, columns] = add_keys(
            score_refs[i % 2], 0, count, turned_ref, v0, stat_ref[0:1, columns], stat_ref[1:2, columns],
            acc_ref[:, columns], start,
        )

    make(0)
    for i in range(steps):
        if i + 1 < steps:
            make(i + 1)
        use(i)


def first_kernel(
    rows, group, docs, length_ref, q_hbm, k_hbm, v_hbm,
    acc_ref, stat_ref, stack_ref, start_ref, bound_ref,
    q_ref, k_ref, v_ref, vt_ref, score_ref, sem,
):
    copies = [
        pltpu.make_async_copy(source, target, sem.at[i])
        for i, (source, target) in enumerate(((q_hbm, q_ref), (k_hbm, k_ref), (v_hbm, v_ref)))
    ]
    for copy in copies:
        copy.start()
    first_row = lax.axis_index("seq") * rows
    tiles = range(0, rows, TFIRST)
    marks = [first_row, first_row + SPLIT, first_row + rows - 1]
    positions = first_row + lax.broadcasted_iota(jnp.int32, (1, rows), 1)

    def document(d, carried):
        begin, row_starts, found = carried
        row_starts = jnp.where(positions >= begin, begin, row_starts)
        found = [jnp.where(mark >= begin, begin, old) for mark, old in zip(marks, found)]
        return begin + length_ref[d], row_starts, found

    zero = jnp.int32(0)
    _, row_starts, found = lax.fori_loop(
        0, docs, document, (zero, jnp.zeros((1, rows), jnp.int32), [zero for _ in marks])
    )
    start_ref[0:1, :] = row_starts
    start_ref[1:8, :] = jnp.zeros((7, rows), jnp.int32)
    bound_ref[0] = first_row
    for i, value in enumerate(found):
        bound_ref[1 + i] = value
    for i in range(len(found) + 1, 8):
        bound_ref[i] = zero
    for copy in copies:
        copy.wait()
    vt_ref[...] = v_ref[...].T
    for h in range(group):
        stack_ref[h * rows : (h + 1) * rows, :] = q_ref[:, h * HD : (h + 1) * HD]
    stat_ref[...] = jnp.zeros_like(stat_ref)
    offsets = {}
    used = 0
    for q0 in tiles:
        offsets[q0] = used
        used += q0 + TFIRST

    def head(h, carried):
        base = pl.multiple_of(h * rows, rows)

        def make(q0):
            put_scores(score_ref, offsets[q0], stack_ref[pl.ds(base + q0, TFIRST), :], k_ref, 0, q0 + TFIRST)

        def use(q0):
            columns = pl.ds(base + q0, TFIRST)
            start = start_ref[0:1, q0 : q0 + TFIRST] - first_row
            lowest = jnp.full((1, TFIRST), LOWEST, jnp.float32)
            none = jnp.zeros((1, TFIRST), jnp.float32)
            stat_ref[0:1, columns], stat_ref[1:2, columns], acc_ref[:, columns] = add_keys(
                score_ref, offsets[q0], q0 + TFIRST, vt_ref, 0, lowest, none, jnp.zeros((HD, TFIRST), jnp.float32), start, q0
            )

        order = list(reversed(tiles))
        make(order[0])
        for i, q0 in enumerate(order):
            if i + 1 < len(order):
                make(order[i + 1])
            use(q0)
        return carried

    lax.fori_loop(0, group, head, 0)


def middle_kernel(
    distance, rows, group, bound_ref, start_ref, q_ref, k_ref, v_ref, acc_in, stat_in, acc_ref, stat_ref, vt_ref, *score_refs
):
    acc_ref[...] = acc_in[...]
    stat_ref[...] = stat_in[...]
    first_key = bound_ref[0] - distance * rows
    needed = (bound_ref[1] < first_key + rows) & (first_key >= 0)
    inside = bound_ref[3] > first_key
    tiles = rows // TQ

    def work(masked):
        vt_ref[...] = v_ref[...].T

        def head(h, carried):
            def first(i):
                return (pl.multiple_of(h * rows + i * TQ, TQ),) * 2

            def start_row(i):
                return start_ref[0:1, i * TQ : (i + 1) * TQ] - first_key

            sweep(
                tiles, first, k_ref, 0, rows, vt_ref, 0, (acc_ref, stat_ref), q_ref, score_refs, start_row if masked else None
            )
            return carried

        lax.fori_loop(0, group, head, 0)

    pl.when(needed & jnp.logical_not(inside))(lambda: work(False))
    pl.when(needed & inside)(lambda: work(True))


def add_block(tiles, base, rows, group, q_ref, start_ref, acc_ref, stat_ref, vt_ref, score_refs, key_ref, v_block, key_count, first_key, masked, skipped):
    size = sum(tiles)
    offsets = [sum(tiles[:i]) for i in range(len(tiles))]
    vt_ref[:, :key_count] = v_block().T

    def head(h, carried):
        for i, (at, width) in enumerate(zip(offsets, tiles)):
            skip = skipped(at)
            query = q_ref[pl.ds(pl.multiple_of(h * rows + base + at, 128), width), :]
            put_scores(score_refs[i], 0, query, key_ref, skip, key_count - skip)
        for i, (at, width) in enumerate(zip(offsets, tiles)):
            skip = skipped(at)
            columns = pl.ds(pl.multiple_of(h * size + at, 128), width)
            start = start_ref[0:1, base + at : base + at + width] - (first_key + skip) if masked else None
            stat_ref[0:1, columns], stat_ref[1:2, columns], acc_ref[:, columns] = add_keys(
                score_refs[i], 0, key_count - skip, vt_ref, skip, stat_ref[0:1, columns], stat_ref[1:2, columns],
                acc_ref[:, columns], start,
            )
        return carried

    lax.fori_loop(0, group, head, 0)


def near_part(late, rows, group, bound_ref, start_ref, q_ref, k_ref, v_ref, far_ref, acc_in, stat_in, acc_ref, stat_ref, vt_ref, score_refs):
    base, tiles = (SPLIT, LATE_TILES) if late else (0, EARLY_TILES)
    size = sum(tiles)
    for h in range(group):
        acc_ref[:, h * size : (h + 1) * size] = acc_in[:, h * rows + base : h * rows + base + size]
        stat_ref[:, h * size : (h + 1) * size] = stat_in[:, h * rows + base : h * rows + base + size]
    block = functools.partial(add_block, tiles, base, rows, group, q_ref, start_ref, acc_ref, stat_ref, vt_ref, score_refs)
    near_key = bound_ref[0] - 3 * rows
    lowest = bound_ref[2] if late else bound_ref[1]
    needed = (lowest < near_key + rows) & (near_key >= 0)
    inside = bound_ref[3] > near_key
    pl.when(needed & jnp.logical_not(inside))(lambda: block(k_ref, lambda: v_ref[...], rows, near_key, False, lambda at: 0))
    pl.when(needed & inside)(lambda: block(k_ref, lambda: v_ref[...], rows, near_key, True, lambda at: 0))
    far_key = near_key - rows
    pl.when((lowest < far_key + rows) & (far_key >= 0))(
        lambda: block(
            far_ref.at[:, :HD], lambda: far_ref[:, HD:], rows - SPLIT, far_key + SPLIT, True, lambda at: at if late else 0
        )
    )


def give_rows(group, acc_ref, stat_ref, out_ref):
    size = out_ref.shape[0]
    for h in range(group):
        columns = slice(h * size, (h + 1) * size)
        scaled = acc_ref[:, columns] / stat_ref[1:2, columns]
        out_ref[:, h * HD : (h + 1) * HD] = scaled.T.astype(jnp.bfloat16)


def late_kernel(rows, group, bound_ref, start_ref, q_ref, k_ref, v_ref, far_ref, acc_in, stat_in, out_ref, acc_ref, stat_ref, vt_ref, *score_refs):
    near_part(
        True, rows, group, bound_ref, start_ref, q_ref, k_ref, v_ref, far_ref, acc_in, stat_in, acc_ref, stat_ref, vt_ref, score_refs
    )
    give_rows(group, acc_ref, stat_ref, out_ref)


def early_kernel(
    rows, group, bound_ref, start_ref, q_ref, k_ref, v_ref, far_ref, first_ref, acc_in, stat_in, out_ref, acc_ref, stat_ref, vt_ref, *score_refs
):
    near_part(
        False, rows, group, bound_ref, start_ref, q_ref, k_ref, v_ref, far_ref, acc_in, stat_in, acc_ref, stat_ref, vt_ref, score_refs
    )
    far_key = bound_ref[0] - 4 * rows
    pl.when((bound_ref[1] < far_key + SPLIT) & (far_key >= 0))(
        lambda: add_block(
            EARLY_TILES, 0, rows, group, q_ref, start_ref, acc_ref, stat_ref, vt_ref, score_refs,
            first_ref.at[:, :HD], lambda: first_ref[:, HD:], SPLIT, far_key, True, lambda at: at,
        )
    )
    give_rows(group, acc_ref, stat_ref, out_ref)


def cost(rows, keys, columns, weight=0):
    return pl.CostEstimate(flops=4 * weight * rows * keys * columns, bytes_accessed=6 * weight * rows * columns, transcendentals=weight * rows * keys * 3)


def params(mebibytes=32):
    return pltpu.CompilerParams(vmem_limit_bytes=mebibytes * 2**20)


def attend_first(doc_lengths, queries, keys, values):
    rows, columns = queries.shape
    group = columns // HD
    tiles = rows // TFIRST
    return pl.pallas_call(
        functools.partial(first_kernel, rows, group, doc_lengths.shape[0]),
        out_shape=[
            jax.ShapeDtypeStruct((HD, group * rows), jnp.float32),
            jax.ShapeDtypeStruct((8, group * rows), jnp.float32),
            jax.ShapeDtypeStruct((group * rows, HD), jnp.bfloat16),
            jax.ShapeDtypeStruct((8, rows), jnp.int32),
            jax.ShapeDtypeStruct((8,), jnp.int32),
        ],
        in_specs=[SMEM, HBM, HBM, HBM],
        out_specs=[VMEM, VMEM, VMEM, VMEM, SMEM],
        scratch_shapes=[
            pltpu.VMEM(queries.shape, jnp.bfloat16),
            pltpu.VMEM(keys.shape, jnp.bfloat16),
            pltpu.VMEM(values.shape, jnp.bfloat16),
            pltpu.VMEM((HD, rows), jnp.bfloat16),
            pltpu.VMEM((TFIRST * tiles * (tiles + 1) // 2, TFIRST), jnp.float32),
            pltpu.SemaphoreType.DMA((3,)),
        ],
        compiler_params=params(32),
        cost_estimate=cost(rows, rows, columns, 1),
        name="attend_first",
    )(doc_lengths, queries, keys, values)


def attend_middle(distance, bounds, start_rows, stack, keys, values, state):
    rows = keys.shape[0]
    group = stack.shape[0] // rows
    return pl.pallas_call(
        functools.partial(middle_kernel, distance, rows, group),
        out_shape=[jax.ShapeDtypeStruct(s.shape, s.dtype) for s in state],
        in_specs=[SMEM] + [VMEM] * 6,
        out_specs=[VMEM, VMEM],
        scratch_shapes=[pltpu.VMEM((HD, rows), jnp.bfloat16)] + [pltpu.VMEM((rows, TQ), jnp.float32)] * 2,
        input_output_aliases={5: 0, 6: 1},
        compiler_params=params(),
        cost_estimate=cost(rows, rows, group * HD),
        name=f"attend_{distance}",
    )(bounds, start_rows, stack, keys, values, *state)


def attend_last(late, bounds, start_rows, stack, rows, arrays):
    tiles = LATE_TILES if late else EARLY_TILES
    size = sum(tiles)
    group = stack.shape[0] // rows
    return pl.pallas_call(
        functools.partial(late_kernel if late else early_kernel, rows, group),
        out_shape=jax.ShapeDtypeStruct((size, group * HD), jnp.bfloat16),
        in_specs=[SMEM] + [VMEM] * (2 + len(arrays)),
        out_specs=VMEM,
        scratch_shapes=[
            pltpu.VMEM((HD, group * size), jnp.float32),
            pltpu.VMEM((8, group * size), jnp.float32),
            pltpu.VMEM((HD, rows), jnp.bfloat16),
        ]
        + [pltpu.VMEM((rows, tile), jnp.float32) for tile in tiles],
        compiler_params=params(),
        cost_estimate=cost(size, rows, group * HD),
        name="attend_late" if late else "attend_early",
    )(bounds, start_rows, stack, *arrays)


def pack_kernel(k_hbm, v_hbm, far_ref, sem):
    late = far_ref.shape[0]
    copies = [
        pltpu.make_async_copy(source.at[pl.ds(SPLIT, late), :], far_ref.at[:, part], sem.at[i])
        for i, (source, part) in enumerate(((k_hbm, slice(0, HD)), (v_hbm, slice(HD, 2 * HD))))
    ]
    for copy in copies:
        copy.start()
    for copy in copies:
        copy.wait()


def pack(keys, values):
    return pl.pallas_call(
        pack_kernel,
        out_shape=jax.ShapeDtypeStruct((keys.shape[0] - SPLIT, 2 * HD), keys.dtype),
        in_specs=[HBM, HBM],
        out_specs=VMEM,
        scratch_shapes=[pltpu.SemaphoreType.DMA((2,))],
        compiler_params=params(),
        name="pack",
    )(keys, values)


def cut_kernel(chips, weight_hbm, *refs):
    weight_refs, sem = refs[:chips], refs[-1]
    wide = weight_refs[0].shape[1]
    chip = lax.axis_index("head") // 2
    copies = []
    for d in (1, 3, 2, 0):
        column = pl.multiple_of(lax.rem(chip + d, chips) * wide, wide)
        copies.append(pltpu.make_async_copy(weight_hbm.at[:, pl.ds(column, wide)], weight_refs[d], sem.at[d]))
    for copy in copies:
        copy.start()
    for copy in copies:
        copy.wait()


def cut(out_weight, chips):
    rows, columns = out_weight.shape
    block = jax.ShapeDtypeStruct((rows, columns // chips), out_weight.dtype)
    return pl.pallas_call(
        functools.partial(cut_kernel, chips),
        out_shape=[block] * chips,
        in_specs=[HBM],
        out_specs=[VMEM] * chips,
        scratch_shapes=[pltpu.SemaphoreType.DMA((chips,))],
        compiler_params=params(),
        name="cut",
    )(out_weight)


def near_kernel(own_ref, before_ref, after_ref, w0_ref, w1_ref, w3_ref, out_ref):
    block = jnp.concatenate([own_ref[...], before_ref[...], after_ref[...]], axis=1)
    weight = jnp.concatenate([w0_ref[...], w1_ref[...], w3_ref[...]], axis=0)
    out_ref[...] = jnp.dot(block, weight, preferred_element_type=jnp.float32)


def project_near(*operands):
    size, wide = operands[0].shape[0], operands[3].shape[1]
    return pl.pallas_call(
        near_kernel,
        out_shape=jax.ShapeDtypeStruct((size, wide), jnp.float32),
        in_specs=[VMEM] * 6,
        out_specs=VMEM,
        compiler_params=params(),
        name="project_near",
    )(*operands)


def far_kernel(first_ref, second_ref, weight_ref, near_ref, kept_ref, given_ref):
    size, columns = first_ref.shape
    core = lax.axis_index("head") % 2
    low, high = slice(0, columns), slice(columns, None)
    for i, block_ref in enumerate((first_ref, second_ref)):
        part = slice(i * size, (i + 1) * size)
        total = near_ref[part, :] + jnp.dot(block_ref[...], weight_ref[...], preferred_element_type=jnp.float32)

        def give(kept, given):
            kept_ref[part, :] = total[:, kept]
            given_ref[part, :] = total[:, given].astype(jnp.bfloat16)

        pl.when(core == 0)(lambda: give(low, high))
        pl.when(core == 1)(lambda: give(high, low))


def project_far(blocks, weight, near):
    rows, wide = near.shape
    return pl.pallas_call(
        far_kernel,
        out_shape=[jax.ShapeDtypeStruct((rows, wide // 2), t) for t in (jnp.float32, jnp.bfloat16)],
        in_specs=[VMEM] * 4,
        out_specs=[VMEM, VMEM],
        compiler_params=params(),
        name="project_far",
    )(*blocks, weight, near)


def join_kernel(*refs):
    out_ref = refs[-1]
    done = 0
    for kept, taken in zip(refs[0:-1:2], refs[1:-1:2]):
        size = kept.shape[0]
        out_ref[done : done + size, :] = (kept[...] + taken[...].astype(jnp.float32)).astype(jnp.bfloat16)
        done += size


def join(*parts):
    rows, columns = sum(part.shape[0] for part in parts[::2]), parts[0].shape[1]
    return pl.pallas_call(
        join_kernel,
        out_shape=jax.ShapeDtypeStruct((rows, columns), jnp.bfloat16),
        in_specs=[VMEM] * len(parts),
        out_specs=VMEM,
        compiler_params=params(),
        name="join",
    )(*parts)


def after(value, *others):
    return lax.optimization_barrier((value, others))[0]


def body(queries, keys, values, out_weight, doc_lengths):
    rows = queries.shape[0]
    seq_size = lax.axis_size("seq")
    head_size = lax.axis_size("head")
    chips = head_size // 2
    def next_block(block):
        return lax.ppermute(block, "seq", [(i, (i + 1) % seq_size) for i in range(seq_size)])

    def back(block, distance):
        return lax.ppermute(block, "seq", [(i, i - i % ROW + (i - distance) % ROW) for i in range(seq_size)])

    def four_on(block):
        owners = [i - i % ROW + (i + 3) % ROW for i in range(seq_size)]
        return lax.ppermute(block, "seq", [(i, (owner + 4) % seq_size) for i, owner in enumerate(owners)])

    def chip_shift(block, distance):
        route = [(i, (i + 2 * distance) % head_size) for i in range(head_size)]
        return lax.ppermute(block, "head", route)

    def swap(block):
        return lax.ppermute(block, "head", [(i, i ^ 1) for i in range(head_size)])

    k1, v1 = next_block(keys), next_block(values)
    far = back(pack(keys, values), 1)
    *state, stack, start_rows, bounds = attend_first(doc_lengths, queries, keys, values)
    k2, v2 = next_block(after(k1, state[1], v1)), next_block(after(v1, state[1]))
    blocks = cut(after(out_weight, k1, state[1], far), chips)
    far = back(after(far, v1), 2)
    weights = {0: blocks[0], 1: chip_shift(after(blocks[1], v1), 1), 3: chip_shift(after(blocks[3], v1), 3)}
    state = attend_middle(1, bounds, start_rows, stack, k1, v1, state)
    k3, v3 = next_block(after(k2, state[1])), next_block(after(v2, state[1]))
    weights[2] = chip_shift(after(blocks[2], state[1], weights[1]), 2)
    bounds = after(bounds, weights[1], weights[3], far)
    far = four_on(far)
    state = attend_middle(2, bounds, start_rows, stack, k2, v2, state)
    late = attend_last(True, bounds, start_rows, stack, rows, (k3, v3, far, *state))
    k4, v4 = (after(block, state[1])[:SPLIT] for block in (k3, v3))
    first_far = next_block(jnp.concatenate([k4, v4], axis=1))
    bounds = after(bounds, late, weights[2], first_far)

    def sides(block):
        return chip_shift(block, 1), chip_shift(block, -1)

    def forwarded(before, behind):
        middle = before.shape[0] // 2
        return chip_shift(before[:middle], 1), chip_shift(behind[middle:], -1)

    near_weights = (weights[0], weights[1], weights[3])
    late_sides = sides(late)
    early = attend_last(False, bounds, start_rows, stack, rows, (k3, v3, far, first_far, *state))
    early_sides = sides(early)
    late_far = forwarded(*late_sides)
    late_near = project_near(late, *late_sides, *near_weights)
    early_far = forwarded(*early_sides)
    early_near = project_near(early, *early_sides, *near_weights)
    late_kept, late_given = project_far(late_far, weights[2], late_near)
    late_taken = swap(late_given)
    early_kept, early_given = project_far(early_far, weights[2], early_near)
    early_taken = swap(early_given)
    return join(early_kept, early_taken, late_kept, late_taken)


def solution(mesh):
    return jax.shard_map(
        body,
        mesh=mesh,
        in_specs=(P("seq", "head"), P("seq", "head"), P("seq", "head"), P("head", None), P()),
        out_specs=P("seq", "head"),
        check_vma=False,
    )
```

```python
import functools

import jax
import jax.numpy as jnp
from jax import lax
from jax.experimental import pallas as pl
from jax.experimental.pallas import tpu as pltpu
from jax.sharding import PartitionSpec as P

HD = 128
ROW = 8
TFIRST = 256
TQ = 512
TK = 512
SPLIT = 512
LATE_TILES = (256, 256)
EARLY_TILES = (256, 256)
LOG2E = 1.4426950408889634
SCALE = LOG2E / HD**0.5
MASKED = -1e30
LOWEST = -1e29
VMEM = pl.BlockSpec(memory_space=pltpu.VMEM)
SMEM = pl.BlockSpec(memory_space=pltpu.SMEM)
HBM = pl.BlockSpec(memory_space=pltpu.HBM)
NT = (((1,), (1,)), ((), ()))


def put_scores(score_ref, row, query, key_ref, k0, count):
    for j in range(0, count, TK):
        n = min(TK, count - j)
        score_ref[row + j : row + j + n, :] = lax.dot_general(
            key_ref[k0 + j : k0 + j + n, :], query, NT, preferred_element_type=jnp.float32
        )


def add_keys(score_ref, row, count, turned_ref, v0, old_max, old_sum, old_acc, start_row=None, q0=None):
    size = score_ref.shape[1]

    def piece(j, n):
        scores = score_ref[row + j : row + j + n, :]
        if start_row is None:
            return scores
        key_pos = j + lax.broadcasted_iota(jnp.int32, (n, size), 0)
        visible = key_pos >= start_row
        if q0 is not None and j + n > q0 + 1:
            visible = visible & (key_pos <= q0 + lax.broadcasted_iota(jnp.int32, (n, size), 1))
        return jnp.where(visible, scores, MASKED)

    pieces = [(j, min(TK, count - j)) for j in range(0, count, TK)]
    new_max = old_max
    for j, n in pieces:
        new_max = jnp.maximum(new_max, jnp.max(piece(j, n), axis=0, keepdims=True))
    rescale = jnp.exp2((old_max - new_max) * SCALE)
    total = old_sum * rescale
    acc = old_acc * rescale
    for j, n in pieces:
        probs = jnp.exp2((piece(j, n) - new_max) * SCALE)
        total = total + jnp.sum(probs, axis=0, keepdims=True)
        acc = acc + jnp.dot(
            turned_ref[:, v0 + j : v0 + j + n], probs.astype(jnp.bfloat16), preferred_element_type=jnp.float32
        )
    return new_max, total, acc


def sweep(steps, first, key_ref, k0, count, turned_ref, v0, state, q_ref, score_refs, start_row):
    acc_ref, stat_ref = state

    def make(i):
        q_at, _ = first(i)
        put_scores(score_refs[i % 2], 0, q_ref[pl.ds(q_at, TQ), :], key_ref, k0, count)

    def use(i):
        columns = pl.ds(first(i)[1], TQ)
        start = None if start_row is None else start_row(i)
        stat_ref[0:1, columns], stat_ref[1:2, columns], acc_ref[:, columns] = add_keys(
            score_refs[i % 2], 0, count, turned_ref, v0, stat_ref[0:1, columns], stat_ref[1:2, columns],
            acc_ref[:, columns], start,
        )

    make(0)
    for i in range(steps):
        if i + 1 < steps:
            make(i + 1)
        use(i)


def first_kernel(
    rows, group, docs, length_ref, q_ref, k_ref, v_ref,
    acc_ref, stat_ref, stack_ref, start_ref, bound_ref,
    vt_ref, score_ref,
):
    first_row = lax.axis_index("seq") * rows
    tiles = range(0, rows, TFIRST)
    marks = [first_row, first_row + SPLIT, first_row + rows - 1]
    positions = first_row + lax.broadcasted_iota(jnp.int32, (1, rows), 1)

    def document(d, carried):
        begin, row_starts, found = carried
        row_starts = jnp.where(positions >= begin, begin, row_starts)
        found = [jnp.where(mark >= begin, begin, old) for mark, old in zip(marks, found)]
        return begin + length_ref[d], row_starts, found

    zero = jnp.int32(0)
    _, row_starts, found = lax.fori_loop(
        0, docs, document, (zero, jnp.zeros((1, rows), jnp.int32), [zero for _ in marks])
    )
    start_ref[0:1, :] = row_starts
    start_ref[1:8, :] = jnp.zeros((7, rows), jnp.int32)
    bound_ref[0] = first_row
    for i, value in enumerate(found):
        bound_ref[1 + i] = value
    for i in range(len(found) + 1, 8):
        bound_ref[i] = zero
    vt_ref[...] = v_ref[...].T
    for h in range(group):
        stack_ref[h * rows : (h + 1) * rows, :] = q_ref[:, h * HD : (h + 1) * HD]
    stat_ref[...] = jnp.zeros_like(stat_ref)
    offsets = {}
    used = 0
    for q0 in tiles:
        offsets[q0] = used
        used += q0 + TFIRST

    def head(h, carried):
        base = pl.multiple_of(h * rows, rows)

        def make(q0):
            put_scores(score_ref, offsets[q0], stack_ref[pl.ds(base + q0, TFIRST), :], k_ref, 0, q0 + TFIRST)

        def use(q0):
            columns = pl.ds(base + q0, TFIRST)
            start = start_ref[0:1, q0 : q0 + TFIRST] - first_row
            lowest = jnp.full((1, TFIRST), LOWEST, jnp.float32)
            none = jnp.zeros((1, TFIRST), jnp.float32)
            stat_ref[0:1, columns], stat_ref[1:2, columns], acc_ref[:, columns] = add_keys(
                score_ref, offsets[q0], q0 + TFIRST, vt_ref, 0, lowest, none, jnp.zeros((HD, TFIRST), jnp.float32), start, q0
            )

        order = list(reversed(tiles))
        make(order[0])
        for i, q0 in enumerate(order):
            if i + 1 < len(order):
                make(order[i + 1])
            use(q0)
        return carried

    lax.fori_loop(0, group, head, 0)


def middle_kernel(
    distance, rows, group, bound_ref, start_ref, q_ref, k_ref, v_ref, acc_in, stat_in, acc_ref, stat_ref, vt_ref, *score_refs
):
    acc_ref[...] = acc_in[...]
    stat_ref[...] = stat_in[...]
    first_key = bound_ref[0] - distance * rows
    needed = (bound_ref[1] < first_key + rows) & (first_key >= 0)
    inside = bound_ref[3] > first_key
    tiles = rows // TQ

    def work(masked):
        vt_ref[...] = v_ref[...].T

        def head(h, carried):
            def first(i):
                return (pl.multiple_of(h * rows + i * TQ, TQ),) * 2

            def start_row(i):
                return start_ref[0:1, i * TQ : (i + 1) * TQ] - first_key

            sweep(
                tiles, first, k_ref, 0, rows, vt_ref, 0, (acc_ref, stat_ref), q_ref, score_refs, start_row if masked else None
            )
            return carried

        lax.fori_loop(0, group, head, 0)

    pl.when(needed & jnp.logical_not(inside))(lambda: work(False))
    pl.when(needed & inside)(lambda: work(True))


def add_block(tiles, base, rows, group, q_ref, start_ref, acc_ref, stat_ref, vt_ref, score_refs, key_ref, v_block, key_count, first_key, masked, skipped):
    size = sum(tiles)
    offsets = [sum(tiles[:i]) for i in range(len(tiles))]
    vt_ref[:, :key_count] = v_block().T

    def head(h, carried):
        for i, (at, width) in enumerate(zip(offsets, tiles)):
            skip = skipped(at)
            query = q_ref[pl.ds(pl.multiple_of(h * rows + base + at, 128), width), :]
            put_scores(score_refs[i], 0, query, key_ref, skip, key_count - skip)
        for i, (at, width) in enumerate(zip(offsets, tiles)):
            skip = skipped(at)
            columns = pl.ds(pl.multiple_of(h * size + at, 128), width)
            start = start_ref[0:1, base + at : base + at + width] - (first_key + skip) if masked else None
            stat_ref[0:1, columns], stat_ref[1:2, columns], acc_ref[:, columns] = add_keys(
                score_refs[i], 0, key_count - skip, vt_ref, skip, stat_ref[0:1, columns], stat_ref[1:2, columns],
                acc_ref[:, columns], start,
            )
        return carried

    lax.fori_loop(0, group, head, 0)


def near_part(late, rows, group, bound_ref, start_ref, q_ref, k_ref, v_ref, far_ref, acc_in, stat_in, acc_ref, stat_ref, vt_ref, score_refs):
    base, tiles = (SPLIT, LATE_TILES) if late else (0, EARLY_TILES)
    size = sum(tiles)
    for h in range(group):
        acc_ref[:, h * size : (h + 1) * size] = acc_in[:, h * rows + base : h * rows + base + size]
        stat_ref[:, h * size : (h + 1) * size] = stat_in[:, h * rows + base : h * rows + base + size]
    block = functools.partial(add_block, tiles, base, rows, group, q_ref, start_ref, acc_ref, stat_ref, vt_ref, score_refs)
    near_key = bound_ref[0] - 3 * rows
    lowest = bound_ref[2] if late else bound_ref[1]
    needed = (lowest < near_key + rows) & (near_key >= 0)
    inside = bound_ref[3] > near_key
    pl.when(needed & jnp.logical_not(inside))(lambda: block(k_ref, lambda: v_ref[...], rows, near_key, False, lambda at: 0))
    pl.when(needed & inside)(lambda: block(k_ref, lambda: v_ref[...], rows, near_key, True, lambda at: 0))
    far_key = near_key - rows
    pl.when((lowest < far_key + rows) & (far_key >= 0))(
        lambda: block(
            far_ref.at[:, :HD], lambda: far_ref[:, HD:], rows - SPLIT, far_key + SPLIT, True, lambda at: at if late else 0
        )
    )


def give_rows(group, acc_ref, stat_ref, out_ref):
    size = out_ref.shape[0]
    for h in range(group):
        columns = slice(h * size, (h + 1) * size)
        scaled = acc_ref[:, columns] / stat_ref[1:2, columns]
        out_ref[:, h * HD : (h + 1) * HD] = scaled.T.astype(jnp.bfloat16)


def late_kernel(rows, group, bound_ref, start_ref, q_ref, k_ref, v_ref, far_ref, acc_in, stat_in, out_ref, acc_ref, stat_ref, vt_ref, *score_refs):
    near_part(
        True, rows, group, bound_ref, start_ref, q_ref, k_ref, v_ref, far_ref, acc_in, stat_in, acc_ref, stat_ref, vt_ref, score_refs
    )
    give_rows(group, acc_ref, stat_ref, out_ref)


def early_kernel(
    rows, group, bound_ref, start_ref, q_ref, k_ref, v_ref, far_ref, first_ref, acc_in, stat_in, out_ref, acc_ref, stat_ref, vt_ref, *score_refs
):
    near_part(
        False, rows, group, bound_ref, start_ref, q_ref, k_ref, v_ref, far_ref, acc_in, stat_in, acc_ref, stat_ref, vt_ref, score_refs
    )
    far_key = bound_ref[0] - 4 * rows
    pl.when((bound_ref[1] < far_key + SPLIT) & (far_key >= 0))(
        lambda: add_block(
            EARLY_TILES, 0, rows, group, q_ref, start_ref, acc_ref, stat_ref, vt_ref, score_refs,
            first_ref.at[:, :HD], lambda: first_ref[:, HD:], SPLIT, far_key, True, lambda at: at,
        )
    )
    give_rows(group, acc_ref, stat_ref, out_ref)


def cost(rows, keys, columns, weight=0):
    return pl.CostEstimate(flops=4 * weight * rows * keys * columns, bytes_accessed=6 * weight * rows * columns, transcendentals=weight * rows * keys * 3)


def params(mebibytes=32):
    return pltpu.CompilerParams(vmem_limit_bytes=mebibytes * 2**20)


def attend_first(doc_lengths, queries, keys, values):
    rows, columns = queries.shape
    group = columns // HD
    tiles = rows // TFIRST
    return pl.pallas_call(
        functools.partial(first_kernel, rows, group, doc_lengths.shape[0]),
        out_shape=[
            jax.ShapeDtypeStruct((HD, group * rows), jnp.float32),
            jax.ShapeDtypeStruct((8, group * rows), jnp.float32),
            jax.ShapeDtypeStruct((group * rows, HD), jnp.bfloat16),
            jax.ShapeDtypeStruct((8, rows), jnp.int32),
            jax.ShapeDtypeStruct((8,), jnp.int32),
        ],
        in_specs=[SMEM, VMEM, VMEM, VMEM],
        out_specs=[VMEM, VMEM, VMEM, VMEM, SMEM],
        scratch_shapes=[
            pltpu.VMEM((HD, rows), jnp.bfloat16),
            pltpu.VMEM((TFIRST * tiles * (tiles + 1) // 2, TFIRST), jnp.float32),
        ],
        compiler_params=params(32),
        cost_estimate=cost(rows, rows, columns, 1),
        name="attend_first",
    )(doc_lengths, queries, keys, values)


def attend_middle(distance, bounds, start_rows, stack, keys, values, state):
    rows = keys.shape[0]
    group = stack.shape[0] // rows
    return pl.pallas_call(
        functools.partial(middle_kernel, distance, rows, group),
        out_shape=[jax.ShapeDtypeStruct(s.shape, s.dtype) for s in state],
        in_specs=[SMEM] + [VMEM] * 6,
        out_specs=[VMEM, VMEM],
        scratch_shapes=[pltpu.VMEM((HD, rows), jnp.bfloat16)] + [pltpu.VMEM((rows, TQ), jnp.float32)] * 2,
        input_output_aliases={5: 0, 6: 1},
        compiler_params=params(),
        cost_estimate=cost(rows, rows, group * HD),
        name=f"attend_{distance}",
    )(bounds, start_rows, stack, keys, values, *state)


def attend_last(late, bounds, start_rows, stack, rows, arrays):
    tiles = LATE_TILES if late else EARLY_TILES
    size = sum(tiles)
    group = stack.shape[0] // rows
    return pl.pallas_call(
        functools.partial(late_kernel if late else early_kernel, rows, group),
        out_shape=jax.ShapeDtypeStruct((size, group * HD), jnp.bfloat16),
        in_specs=[SMEM] + [VMEM] * (2 + len(arrays)),
        out_specs=VMEM,
        scratch_shapes=[
            pltpu.VMEM((HD, group * size), jnp.float32),
            pltpu.VMEM((8, group * size), jnp.float32),
            pltpu.VMEM((HD, rows), jnp.bfloat16),
        ]
        + [pltpu.VMEM((rows, tile), jnp.float32) for tile in tiles],
        compiler_params=params(),
        cost_estimate=cost(size, rows, group * HD),
        name="attend_late" if late else "attend_early",
    )(bounds, start_rows, stack, *arrays)


def pack_kernel(k_hbm, v_hbm, far_ref, sem):
    late = far_ref.shape[0]
    copies = [
        pltpu.make_async_copy(source.at[pl.ds(SPLIT, late), :], far_ref.at[:, part], sem.at[i])
        for i, (source, part) in enumerate(((k_hbm, slice(0, HD)), (v_hbm, slice(HD, 2 * HD))))
    ]
    for copy in copies:
        copy.start()
    for copy in copies:
        copy.wait()


def pack(keys, values):
    return pl.pallas_call(
        pack_kernel,
        out_shape=jax.ShapeDtypeStruct((keys.shape[0] - SPLIT, 2 * HD), keys.dtype),
        in_specs=[HBM, HBM],
        out_specs=VMEM,
        scratch_shapes=[pltpu.SemaphoreType.DMA((2,))],
        compiler_params=params(),
        name="pack",
    )(keys, values)


def cut_kernel(chips, weight_hbm, *refs):
    weight_refs, sem = refs[:chips], refs[-1]
    wide = weight_refs[0].shape[1]
    chip = lax.axis_index("head") // 2
    copies = []
    for d in (1, 3, 2, 0):
        column = pl.multiple_of(lax.rem(chip + d, chips) * wide, wide)
        copies.append(pltpu.make_async_copy(weight_hbm.at[:, pl.ds(column, wide)], weight_refs[d], sem.at[d]))
    for copy in copies:
        copy.start()
    for copy in copies:
        copy.wait()


def cut(out_weight, chips):
    rows, columns = out_weight.shape
    block = jax.ShapeDtypeStruct((rows, columns // chips), out_weight.dtype)
    return pl.pallas_call(
        functools.partial(cut_kernel, chips),
        out_shape=[block] * chips,
        in_specs=[HBM],
        out_specs=[VMEM] * chips,
        scratch_shapes=[pltpu.SemaphoreType.DMA((chips,))],
        compiler_params=params(),
        name="cut",
    )(out_weight)


def near_kernel(own_ref, before_ref, after_ref, w0_ref, w1_ref, w3_ref, out_ref):
    block = jnp.concatenate([own_ref[...], before_ref[...], after_ref[...]], axis=1)
    weight = jnp.concatenate([w0_ref[...], w1_ref[...], w3_ref[...]], axis=0)
    out_ref[...] = jnp.dot(block, weight, preferred_element_type=jnp.float32)


def project_near(*operands):
    size, wide = operands[0].shape[0], operands[3].shape[1]
    return pl.pallas_call(
        near_kernel,
        out_shape=jax.ShapeDtypeStruct((size, wide), jnp.float32),
        in_specs=[VMEM] * 6,
        out_specs=VMEM,
        compiler_params=params(),
        name="project_near",
    )(*operands)


def far_kernel(first_ref, second_ref, weight_ref, near_ref, kept_ref, given_ref):
    size, columns = first_ref.shape
    core = lax.axis_index("head") % 2
    low, high = slice(0, columns), slice(columns, None)
    for i, block_ref in enumerate((first_ref, second_ref)):
        part = slice(i * size, (i + 1) * size)
        total = near_ref[part, :] + jnp.dot(block_ref[...], weight_ref[...], preferred_element_type=jnp.float32)

        def give(kept, given):
            kept_ref[part, :] = total[:, kept]
            given_ref[part, :] = total[:, given].astype(jnp.bfloat16)

        pl.when(core == 0)(lambda: give(low, high))
        pl.when(core == 1)(lambda: give(high, low))


def project_far(blocks, weight, near):
    rows, wide = near.shape
    return pl.pallas_call(
        far_kernel,
        out_shape=[jax.ShapeDtypeStruct((rows, wide // 2), t) for t in (jnp.float32, jnp.bfloat16)],
        in_specs=[VMEM] * 4,
        out_specs=[VMEM, VMEM],
        compiler_params=params(),
        name="project_far",
    )(*blocks, weight, near)


def join_kernel(*refs):
    out_ref = refs[-1]
    done = 0
    for kept, taken in zip(refs[0:-1:2], refs[1:-1:2]):
        size = kept.shape[0]
        out_ref[done : done + size, :] = (kept[...] + taken[...].astype(jnp.float32)).astype(jnp.bfloat16)
        done += size


def join(*parts):
    rows, columns = sum(part.shape[0] for part in parts[::2]), parts[0].shape[1]
    return pl.pallas_call(
        join_kernel,
        out_shape=jax.ShapeDtypeStruct((rows, columns), jnp.bfloat16),
        in_specs=[VMEM] * len(parts),
        out_specs=VMEM,
        compiler_params=params(),
        name="join",
    )(*parts)


def after(value, *others):
    return lax.optimization_barrier((value, others))[0]


def body(queries, keys, values, out_weight, doc_lengths):
    rows = queries.shape[0]
    seq_size = lax.axis_size("seq")
    head_size = lax.axis_size("head")
    chips = head_size // 2
    def next_block(block):
        return lax.ppermute(block, "seq", [(i, (i + 1) % seq_size) for i in range(seq_size)])

    def back(block, distance):
        return lax.ppermute(block, "seq", [(i, i - i % ROW + (i - distance) % ROW) for i in range(seq_size)])

    def four_on(block):
        owners = [i - i % ROW + (i + 3) % ROW for i in range(seq_size)]
        return lax.ppermute(block, "seq", [(i, (owner + 4) % seq_size) for i, owner in enumerate(owners)])

    def chip_shift(block, distance):
        route = [(i, (i + 2 * distance) % head_size) for i in range(head_size)]
        return lax.ppermute(block, "head", route)

    def swap(block):
        return lax.ppermute(block, "head", [(i, i ^ 1) for i in range(head_size)])

    k1, v1 = next_block(keys), next_block(values)
    far = back(pack(keys, values), 1)
    *state, stack, start_rows, bounds = attend_first(doc_lengths, queries, keys, values)
    k2, v2 = next_block(after(k1, state[1], v1)), next_block(after(v1, state[1]))
    blocks = cut(after(out_weight, k1, state[1], far), chips)
    far = back(after(far, v1), 2)
    weights = {0: blocks[0], 1: chip_shift(after(blocks[1], v1), 1), 3: chip_shift(after(blocks[3], v1), 3)}
    state = attend_middle(1, bounds, start_rows, stack, k1, v1, state)
    k3, v3 = next_block(after(k2, state[1])), next_block(after(v2, state[1]))
    weights[2] = chip_shift(after(blocks[2], state[1], weights[1]), 2)
    bounds = after(bounds, weights[1], weights[3], far)
    far = four_on(far)
    state = attend_middle(2, bounds, start_rows, stack, k2, v2, state)
    late = attend_last(True, bounds, start_rows, stack, rows, (k3, v3, far, *state))
    k4, v4 = (after(block, state[1])[:SPLIT] for block in (k3, v3))
    first_far = next_block(jnp.concatenate([k4, v4], axis=1))
    bounds = after(bounds, late, weights[2], first_far)

    def sides(block):
        return chip_shift(block, 1), chip_shift(block, -1)

    def forwarded(before, behind):
        middle = before.shape[0] // 2
        return chip_shift(before[:middle], 1), chip_shift(behind[middle:], -1)

    near_weights = (weights[0], weights[1], weights[3])
    late_sides = sides(late)
    early = attend_last(False, bounds, start_rows, stack, rows, (k3, v3, far, first_far, *state))
    early_sides = sides(early)
    late_far = forwarded(*late_sides)
    late_near = project_near(late, *late_sides, *near_weights)
    early_far = forwarded(*early_sides)
    early_near = project_near(early, *early_sides, *near_weights)
    late_kept, late_given = project_far(late_far, weights[2], late_near)
    late_taken = swap(late_given)
    early_kept, early_given = project_far(early_far, weights[2], early_near)
    early_taken = swap(early_given)
    return join(early_kept, early_taken, late_kept, late_taken)


def solution(mesh):
    return jax.shard_map(
        body,
        mesh=mesh,
        in_specs=(P("seq", "head"), P("seq", "head"), P("seq", "head"), P("head", None), P()),
        out_specs=P("seq", "head"),
        check_vma=False,
    )
```

```python
import functools

import jax
import jax.numpy as jnp
from jax import lax
from jax.experimental import pallas as pl
from jax.experimental.pallas import tpu as pltpu
from jax.sharding import PartitionSpec as P

HD = 128
ROW = 8
TFIRST = 256
TQ = 512
TK = 512
SPLIT = 512
LATE_TILES = (256, 256)
EARLY_TILES = (256, 256)
LOG2E = 1.4426950408889634
SCALE = LOG2E / HD**0.5
MASKED = -1e30
LOWEST = -1e29
VMEM = pl.BlockSpec(memory_space=pltpu.VMEM)
SMEM = pl.BlockSpec(memory_space=pltpu.SMEM)
HBM = pl.BlockSpec(memory_space=pltpu.HBM)
NT = (((1,), (1,)), ((), ()))


def put_scores(score_ref, row, query, key_ref, k0, count):
    for j in range(0, count, TK):
        n = min(TK, count - j)
        score_ref[row + j : row + j + n, :] = lax.dot_general(
            key_ref[k0 + j : k0 + j + n, :], query, NT, preferred_element_type=jnp.float32
        )


def add_keys(score_ref, row, count, turned_ref, v0, old_max, old_sum, old_acc, start_row=None, q0=None):
    size = score_ref.shape[1]

    def piece(j, n):
        scores = score_ref[row + j : row + j + n, :]
        if start_row is None:
            return scores
        key_pos = j + lax.broadcasted_iota(jnp.int32, (n, size), 0)
        visible = key_pos >= start_row
        if q0 is not None and j + n > q0 + 1:
            visible = visible & (key_pos <= q0 + lax.broadcasted_iota(jnp.int32, (n, size), 1))
        return jnp.where(visible, scores, MASKED)

    pieces = [(j, min(TK, count - j)) for j in range(0, count, TK)]
    new_max = old_max
    for j, n in pieces:
        new_max = jnp.maximum(new_max, jnp.max(piece(j, n), axis=0, keepdims=True))
    rescale = jnp.exp2((old_max - new_max) * SCALE)
    total = old_sum * rescale
    acc = old_acc * rescale
    for j, n in pieces:
        probs = jnp.exp2((piece(j, n) - new_max) * SCALE)
        total = total + jnp.sum(probs, axis=0, keepdims=True)
        acc = acc + jnp.dot(
            turned_ref[:, v0 + j : v0 + j + n], probs.astype(jnp.bfloat16), preferred_element_type=jnp.float32
        )
    return new_max, total, acc


def sweep(steps, first, key_ref, k0, count, turned_ref, v0, state, q_ref, score_refs, start_row):
    acc_ref, stat_ref = state

    def make(i):
        q_at, _ = first(i)
        put_scores(score_refs[i % 2], 0, q_ref[pl.ds(q_at, TQ), :], key_ref, k0, count)

    def use(i):
        columns = pl.ds(first(i)[1], TQ)
        start = None if start_row is None else start_row(i)
        stat_ref[0:1, columns], stat_ref[1:2, columns], acc_ref[:, columns] = add_keys(
            score_refs[i % 2], 0, count, turned_ref, v0, stat_ref[0:1, columns], stat_ref[1:2, columns],
            acc_ref[:, columns], start,
        )

    make(0)
    for i in range(steps):
        if i + 1 < steps:
            make(i + 1)
        use(i)


def first_kernel(
    rows, group, docs, length_ref, q_hbm, k_hbm, v_hbm,
    acc_ref, stat_ref, stack_ref, start_ref, bound_ref,
    q_ref, k_ref, v_ref, vt_ref, score_ref, sem,
):
    copies = [
        pltpu.make_async_copy(source, target, sem.at[i])
        for i, (source, target) in enumerate(((q_hbm, q_ref), (k_hbm, k_ref), (v_hbm, v_ref)))
    ]
    for copy in copies:
        copy.start()
    first_row = lax.axis_index("seq") * rows
    tiles = range(0, rows, TFIRST)
    marks = [first_row, first_row + SPLIT, first_row + rows - 1]
    positions = first_row + lax.broadcasted_iota(jnp.int32, (1, rows), 1)

    def document(d, carried):
        begin, row_starts, found = carried
        row_starts = jnp.where(positions >= begin, begin, row_starts)
        found = [jnp.where(mark >= begin, begin, old) for mark, old in zip(marks, found)]
        return begin + length_ref[d], row_starts, found

    zero = jnp.int32(0)
    _, row_starts, found = lax.fori_loop(
        0, docs, document, (zero, jnp.zeros((1, rows), jnp.int32), [zero for _ in marks])
    )
    start_ref[0:1, :] = row_starts
    start_ref[1:8, :] = jnp.zeros((7, rows), jnp.int32)
    bound_ref[0] = first_row
    for i, value in enumerate(found):
        bound_ref[1 + i] = value
    for i in range(len(found) + 1, 8):
        bound_ref[i] = zero
    for copy in copies:
        copy.wait()
    vt_ref[...] = v_ref[...].T
    for h in range(group):
        stack_ref[h * rows : (h + 1) * rows, :] = q_ref[:, h * HD : (h + 1) * HD]
    stat_ref[...] = jnp.zeros_like(stat_ref)
    offsets = {}
    used = 0
    for q0 in tiles:
        offsets[q0] = used
        used += q0 + TFIRST

    def head(h, carried):
        base = pl.multiple_of(h * rows, rows)

        def make(q0):
            put_scores(score_ref, offsets[q0], stack_ref[pl.ds(base + q0, TFIRST), :], k_ref, 0, q0 + TFIRST)

        def use(q0):
            columns = pl.ds(base + q0, TFIRST)
            start = start_ref[0:1, q0 : q0 + TFIRST] - first_row
            lowest = jnp.full((1, TFIRST), LOWEST, jnp.float32)
            none = jnp.zeros((1, TFIRST), jnp.float32)
            stat_ref[0:1, columns], stat_ref[1:2, columns], acc_ref[:, columns] = add_keys(
                score_ref, offsets[q0], q0 + TFIRST, vt_ref, 0, lowest, none, jnp.zeros((HD, TFIRST), jnp.float32), start, q0
            )

        order = list(reversed(tiles))
        make(order[0])
        for i, q0 in enumerate(order):
            if i + 1 < len(order):
                make(order[i + 1])
            use(q0)
        return carried

    lax.fori_loop(0, group, head, 0)


def middle_kernel(
    distance, rows, group, bound_ref, start_ref, q_ref, k_ref, v_ref, acc_in, stat_in, acc_ref, stat_ref, vt_ref, *score_refs
):
    acc_ref[...] = acc_in[...]
    stat_ref[...] = stat_in[...]
    first_key = bound_ref[0] - distance * rows
    needed = (bound_ref[1] < first_key + rows) & (first_key >= 0)
    inside = bound_ref[3] > first_key
    tiles = rows // TQ

    def work(masked):
        vt_ref[...] = v_ref[...].T

        def head(h, carried):
            def first(i):
                return (pl.multiple_of(h * rows + i * TQ, TQ),) * 2

            def start_row(i):
                return start_ref[0:1, i * TQ : (i + 1) * TQ] - first_key

            sweep(
                tiles, first, k_ref, 0, rows, vt_ref, 0, (acc_ref, stat_ref), q_ref, score_refs, start_row if masked else None
            )
            return carried

        lax.fori_loop(0, group, head, 0)

    pl.when(needed & jnp.logical_not(inside))(lambda: work(False))
    pl.when(needed & inside)(lambda: work(True))


def add_block(tiles, base, rows, group, q_ref, start_ref, acc_ref, stat_ref, vt_ref, score_refs, key_ref, v_block, key_count, first_key, masked, skipped):
    size = sum(tiles)
    offsets = [sum(tiles[:i]) for i in range(len(tiles))]
    vt_ref[:, :key_count] = v_block().T

    def head(h, carried):
        for i, (at, width) in enumerate(zip(offsets, tiles)):
            skip = skipped(at)
            query = q_ref[pl.ds(pl.multiple_of(h * rows + base + at, 128), width), :]
            put_scores(score_refs[i], 0, query, key_ref, skip, key_count - skip)
        for i, (at, width) in enumerate(zip(offsets, tiles)):
            skip = skipped(at)
            columns = pl.ds(pl.multiple_of(h * size + at, 128), width)
            start = start_ref[0:1, base + at : base + at + width] - (first_key + skip) if masked else None
            stat_ref[0:1, columns], stat_ref[1:2, columns], acc_ref[:, columns] = add_keys(
                score_refs[i], 0, key_count - skip, vt_ref, skip, stat_ref[0:1, columns], stat_ref[1:2, columns],
                acc_ref[:, columns], start,
            )
        return carried

    lax.fori_loop(0, group, head, 0)


def near_part(late, rows, group, bound_ref, start_ref, q_ref, k_ref, v_ref, far_ref, acc_in, stat_in, acc_ref, stat_ref, vt_ref, score_refs):
    base, tiles = (SPLIT, LATE_TILES) if late else (0, EARLY_TILES)
    size = sum(tiles)
    for h in range(group):
        acc_ref[:, h * size : (h + 1) * size] = acc_in[:, h * rows + base : h * rows + base + size]
        stat_ref[:, h * size : (h + 1) * size] = stat_in[:, h * rows + base : h * rows + base + size]
    block = functools.partial(add_block, tiles, base, rows, group, q_ref, start_ref, acc_ref, stat_ref, vt_ref, score_refs)
    near_key = bound_ref[0] - 3 * rows
    lowest = bound_ref[2] if late else bound_ref[1]
    needed = (lowest < near_key + rows) & (near_key >= 0)
    inside = bound_ref[3] > near_key
    pl.when(needed & jnp.logical_not(inside))(lambda: block(k_ref, lambda: v_ref[...], rows, near_key, False, lambda at: 0))
    pl.when(needed & inside)(lambda: block(k_ref, lambda: v_ref[...], rows, near_key, True, lambda at: 0))
    far_key = near_key - rows
    pl.when((lowest < far_key + rows) & (far_key >= 0))(
        lambda: block(
            far_ref.at[:, :HD], lambda: far_ref[:, HD:], rows - SPLIT, far_key + SPLIT, True, lambda at: at if late else 0
        )
    )


def give_rows(group, acc_ref, stat_ref, out_ref):
    size = out_ref.shape[0]
    for h in range(group):
        columns = slice(h * size, (h + 1) * size)
        scaled = acc_ref[:, columns] / stat_ref[1:2, columns]
        out_ref[:, h * HD : (h + 1) * HD] = scaled.T.astype(jnp.bfloat16)


def late_kernel(rows, group, bound_ref, start_ref, q_ref, k_ref, v_ref, far_ref, acc_in, stat_in, out_ref, acc_ref, stat_ref, vt_ref, *score_refs):
    near_part(
        True, rows, group, bound_ref, start_ref, q_ref, k_ref, v_ref, far_ref, acc_in, stat_in, acc_ref, stat_ref, vt_ref, score_refs
    )
    give_rows(group, acc_ref, stat_ref, out_ref)


def early_kernel(
    rows, group, bound_ref, start_ref, q_ref, k_ref, v_ref, far_ref, first_ref, acc_in, stat_in, out_ref, acc_ref, stat_ref, vt_ref, *score_refs
):
    near_part(
        False, rows, group, bound_ref, start_ref, q_ref, k_ref, v_ref, far_ref, acc_in, stat_in, acc_ref, stat_ref, vt_ref, score_refs
    )
    far_key = bound_ref[0] - 4 * rows
    pl.when((bound_ref[1] < far_key + SPLIT) & (far_key >= 0))(
        lambda: add_block(
            EARLY_TILES, 0, rows, group, q_ref, start_ref, acc_ref, stat_ref, vt_ref, score_refs,
            first_ref.at[:, :HD], lambda: first_ref[:, HD:], SPLIT, far_key, True, lambda at: at,
        )
    )
    give_rows(group, acc_ref, stat_ref, out_ref)


def cost(rows, keys, columns, weight=0):
    return pl.CostEstimate(flops=4 * weight * rows * keys * columns, bytes_accessed=6 * weight * rows * columns, transcendentals=weight * rows * keys * 3)


def params(mebibytes=32):
    return pltpu.CompilerParams(vmem_limit_bytes=mebibytes * 2**20)


def attend_first(doc_lengths, queries, keys, values):
    rows, columns = queries.shape
    group = columns // HD
    tiles = rows // TFIRST
    return pl.pallas_call(
        functools.partial(first_kernel, rows, group, doc_lengths.shape[0]),
        out_shape=[
            jax.ShapeDtypeStruct((HD, group * rows), jnp.float32),
            jax.ShapeDtypeStruct((8, group * rows), jnp.float32),
            jax.ShapeDtypeStruct((group * rows, HD), jnp.bfloat16),
            jax.ShapeDtypeStruct((8, rows), jnp.int32),
            jax.ShapeDtypeStruct((8,), jnp.int32),
        ],
        in_specs=[SMEM, HBM, HBM, HBM],
        out_specs=[VMEM, VMEM, VMEM, VMEM, SMEM],
        scratch_shapes=[
            pltpu.VMEM(queries.shape, jnp.bfloat16),
            pltpu.VMEM(keys.shape, jnp.bfloat16),
            pltpu.VMEM(values.shape, jnp.bfloat16),
            pltpu.VMEM((HD, rows), jnp.bfloat16),
            pltpu.VMEM((TFIRST * tiles * (tiles + 1) // 2, TFIRST), jnp.float32),
            pltpu.SemaphoreType.DMA((3,)),
        ],
        compiler_params=params(32),
        cost_estimate=cost(rows, rows, columns, 1),
        name="attend_first",
    )(doc_lengths, queries, keys, values)


def attend_middle(distance, bounds, start_rows, stack, keys, values, state):
    rows = keys.shape[0]
    group = stack.shape[0] // rows
    return pl.pallas_call(
        functools.partial(middle_kernel, distance, rows, group),
        out_shape=[jax.ShapeDtypeStruct(s.shape, s.dtype) for s in state],
        in_specs=[SMEM] + [VMEM] * 6,
        out_specs=[VMEM, VMEM],
        scratch_shapes=[pltpu.VMEM((HD, rows), jnp.bfloat16)] + [pltpu.VMEM((rows, TQ), jnp.float32)] * 2,
        input_output_aliases={5: 0, 6: 1},
        compiler_params=params(),
        cost_estimate=cost(rows, rows, group * HD),
        name=f"attend_{distance}",
    )(bounds, start_rows, stack, keys, values, *state)


def attend_last(late, bounds, start_rows, stack, rows, arrays):
    tiles = LATE_TILES if late else EARLY_TILES
    size = sum(tiles)
    group = stack.shape[0] // rows
    return pl.pallas_call(
        functools.partial(late_kernel if late else early_kernel, rows, group),
        out_shape=jax.ShapeDtypeStruct((size, group * HD), jnp.bfloat16),
        in_specs=[SMEM] + [VMEM] * (2 + len(arrays)),
        out_specs=VMEM,
        scratch_shapes=[
            pltpu.VMEM((HD, group * size), jnp.float32),
            pltpu.VMEM((8, group * size), jnp.float32),
            pltpu.VMEM((HD, rows), jnp.bfloat16),
        ]
        + [pltpu.VMEM((rows, tile), jnp.float32) for tile in tiles],
        compiler_params=params(),
        cost_estimate=cost(size, rows, group * HD),
        name="attend_late" if late else "attend_early",
    )(bounds, start_rows, stack, *arrays)


def pack_kernel(k_hbm, v_hbm, far_ref, sem):
    late = far_ref.shape[0]
    copies = [
        pltpu.make_async_copy(source.at[pl.ds(SPLIT, late), :], far_ref.at[:, part], sem.at[i])
        for i, (source, part) in enumerate(((k_hbm, slice(0, HD)), (v_hbm, slice(HD, 2 * HD))))
    ]
    for copy in copies:
        copy.start()
    for copy in copies:
        copy.wait()


def pack(keys, values):
    return pl.pallas_call(
        pack_kernel,
        out_shape=jax.ShapeDtypeStruct((keys.shape[0] - SPLIT, 2 * HD), keys.dtype),
        in_specs=[HBM, HBM],
        out_specs=VMEM,
        scratch_shapes=[pltpu.SemaphoreType.DMA((2,))],
        compiler_params=params(60),
        name="pack",
    )(keys, values)


def cut_kernel(chips, weight_hbm, *refs):
    weight_refs, sem = refs[:chips], refs[-1]
    wide = weight_refs[0].shape[1]
    chip = lax.axis_index("head") // 2
    copies = []
    for d in (1, 3, 2, 0):
        column = pl.multiple_of(lax.rem(chip + d, chips) * wide, wide)
        copies.append(pltpu.make_async_copy(weight_hbm.at[:, pl.ds(column, wide)], weight_refs[d], sem.at[d]))
    for copy in copies:
        copy.start()
    for copy in copies:
        copy.wait()


def cut(out_weight, chips):
    rows, columns = out_weight.shape
    block = jax.ShapeDtypeStruct((rows, columns // chips), out_weight.dtype)
    return pl.pallas_call(
        functools.partial(cut_kernel, chips),
        out_shape=[block] * chips,
        in_specs=[HBM],
        out_specs=[VMEM] * chips,
        scratch_shapes=[pltpu.SemaphoreType.DMA((chips,))],
        compiler_params=params(),
        name="cut",
    )(out_weight)


def near_kernel(own_ref, before_ref, after_ref, w0_ref, w1_ref, w3_ref, out_ref):
    block = jnp.concatenate([own_ref[...], before_ref[...], after_ref[...]], axis=1)
    weight = jnp.concatenate([w0_ref[...], w1_ref[...], w3_ref[...]], axis=0)
    out_ref[...] = jnp.dot(block, weight, preferred_element_type=jnp.float32)


def project_near(*operands):
    size, wide = operands[0].shape[0], operands[3].shape[1]
    return pl.pallas_call(
        near_kernel,
        out_shape=jax.ShapeDtypeStruct((size, wide), jnp.float32),
        in_specs=[VMEM] * 6,
        out_specs=VMEM,
        compiler_params=params(),
        name="project_near",
    )(*operands)


def far_kernel(first_ref, second_ref, weight_ref, near_ref, kept_ref, given_ref):
    size, columns = first_ref.shape
    core = lax.axis_index("head") % 2
    low, high = slice(0, columns), slice(columns, None)
    for i, block_ref in enumerate((first_ref, second_ref)):
        part = slice(i * size, (i + 1) * size)
        total = near_ref[part, :] + jnp.dot(block_ref[...], weight_ref[...], preferred_element_type=jnp.float32)

        def give(kept, given):
            kept_ref[part, :] = total[:, kept]
            given_ref[part, :] = total[:, given].astype(jnp.bfloat16)

        pl.when(core == 0)(lambda: give(low, high))
        pl.when(core == 1)(lambda: give(high, low))


def project_far(blocks, weight, near):
    rows, wide = near.shape
    return pl.pallas_call(
        far_kernel,
        out_shape=[jax.ShapeDtypeStruct((rows, wide // 2), t) for t in (jnp.float32, jnp.bfloat16)],
        in_specs=[VMEM] * 4,
        out_specs=[VMEM, VMEM],
        compiler_params=params(),
        name="project_far",
    )(*blocks, weight, near)


def join_kernel(*refs):
    out_ref = refs[-1]
    done = 0
    for kept, taken in zip(refs[0:-1:2], refs[1:-1:2]):
        size = kept.shape[0]
        out_ref[done : done + size, :] = (kept[...] + taken[...].astype(jnp.float32)).astype(jnp.bfloat16)
        done += size


def join(*parts):
    rows, columns = sum(part.shape[0] for part in parts[::2]), parts[0].shape[1]
    return pl.pallas_call(
        join_kernel,
        out_shape=jax.ShapeDtypeStruct((rows, columns), jnp.bfloat16),
        in_specs=[VMEM] * len(parts),
        out_specs=VMEM,
        compiler_params=params(),
        name="join",
    )(*parts)


def after(value, *others):
    return lax.optimization_barrier((value, others))[0]


def body(queries, keys, values, out_weight, doc_lengths):
    rows = queries.shape[0]
    seq_size = lax.axis_size("seq")
    head_size = lax.axis_size("head")
    chips = head_size // 2
    def next_block(block):
        return lax.ppermute(block, "seq", [(i, (i + 1) % seq_size) for i in range(seq_size)])

    def back(block, distance):
        return lax.ppermute(block, "seq", [(i, i - i % ROW + (i - distance) % ROW) for i in range(seq_size)])

    def four_on(block):
        owners = [i - i % ROW + (i + 3) % ROW for i in range(seq_size)]
        return lax.ppermute(block, "seq", [(i, (owner + 4) % seq_size) for i, owner in enumerate(owners)])

    def chip_shift(block, distance):
        route = [(i, (i + 2 * distance) % head_size) for i in range(head_size)]
        return lax.ppermute(block, "head", route)

    def swap(block):
        return lax.ppermute(block, "head", [(i, i ^ 1) for i in range(head_size)])

    k1, v1 = next_block(keys), next_block(values)
    far = back(pack(keys, values), 1)
    *state, stack, start_rows, bounds = attend_first(doc_lengths, queries, keys, values)
    k2, v2 = next_block(after(k1, state[1], v1)), next_block(after(v1, state[1]))
    blocks = cut(after(out_weight, k1, state[1], far), chips)
    far = back(after(far, v1), 2)
    weights = {0: blocks[0], 1: chip_shift(after(blocks[1], v1), 1), 3: chip_shift(after(blocks[3], v1), 3)}
    state = attend_middle(1, bounds, start_rows, stack, k1, v1, state)
    k3, v3 = next_block(after(k2, state[1])), next_block(after(v2, state[1]))
    weights[2] = chip_shift(after(blocks[2], state[1], weights[1]), 2)
    bounds = after(bounds, weights[1], weights[3], far)
    far = four_on(far)
    state = attend_middle(2, bounds, start_rows, stack, k2, v2, state)
    late = attend_last(True, bounds, start_rows, stack, rows, (k3, v3, far, *state))
    k4, v4 = (after(block, state[1])[:SPLIT] for block in (k3, v3))
    first_far = next_block(jnp.concatenate([k4, v4], axis=1))
    bounds = after(bounds, late, weights[2], first_far)

    def sides(block):
        return chip_shift(block, 1), chip_shift(block, -1)

    def forwarded(before, behind):
        middle = before.shape[0] // 2
        return chip_shift(before[:middle], 1), chip_shift(behind[middle:], -1)

    near_weights = (weights[0], weights[1], weights[3])
    late_sides = sides(late)
    early = attend_last(False, bounds, start_rows, stack, rows, (k3, v3, far, first_far, *state))
    early_sides = sides(early)
    late_far = forwarded(*late_sides)
    late_near = project_near(late, *late_sides, *near_weights)
    early_far = forwarded(*early_sides)
    early_near = project_near(early, *early_sides, *near_weights)
    late_kept, late_given = project_far(late_far, weights[2], late_near)
    late_taken = swap(late_given)
    early_kept, early_given = project_far(early_far, weights[2], early_near)
    early_taken = swap(early_given)
    return join(early_kept, early_taken, late_kept, late_taken)


def solution(mesh):
    return jax.shard_map(
        body,
        mesh=mesh,
        in_specs=(P("seq", "head"), P("seq", "head"), P("seq", "head"), P("head", None), P()),
        out_specs=P("seq", "head"),
        check_vma=False,
    )
```
